32 devices in a mesh: view: 16 (over z, x, core), dp: 2 (over y).
Axes of the slice: x: 2, y: 2, z: 4, core: 2. Of those that a mesh axis runs over, the one named last changes fastest.
Arguments:
- tokens: bfloat16 [2, 16, 1, 512, 512], P('dp', 'view'), may hold values from -6 to 6
- counts: int32 [2, 16], P('dp', 'view'), may hold values from 1 to 1, as said below
- slot_item: int32 [2, 16, 1], P('dp', 'view'), may hold values from -1 to 2, as said below
- slot_view: int32 [2, 16, 1], P('dp', 'view'), may hold values from 0 to 4, as said below
- keyframe: int32 [2, 16, 1], P('dp', 'view'), may hold values 0 or 1
- w_query: bfloat16 [512, 512], replicated, may hold values from -0.25 to 0.25
- w_keyval: bfloat16 [512, 1024], replicated, may hold values from -0.25 to 0.25
- w_output: bfloat16 [512, 512], replicated, may hold values from -2 to 2
- w_up: bfloat16 [512, 2048], replicated, may hold values from -0.25 to 0.25
- bias_up: bfloat16 [2048], replicated, may hold values from -1.5 to 1.5
- w_down: bfloat16 [2048, 512], replicated, may hold values from -0.125 to 0.125
- bias_down: bfloat16 [512], replicated, may hold values from -1.5 to 1.5
- gain_attn: bfloat16 [512], replicated, may hold values from 0.5 to 1.5
- shift_attn: bfloat16 [512], replicated, may hold values from -1.5 to 1.5
- gain_mlp: bfloat16 [512], replicated, may hold values from 0.5 to 1.5
- shift_mlp: bfloat16 [512], replicated, may hold values from -1.5 to 1.5
- cotangent: bfloat16 [2, 16, 1, 512, 512], P('dp', 'view'), may hold values from -6 to 6
Outputs:
- block_output: bfloat16 [2, 16, 1, 512, 512], P('dp', 'view')
- grad_tokens: float32 [2, 16, 1, 512, 512], P('dp', 'view')
- grad_query: float32 [512, 512], replicated
- grad_keyval: float32 [512, 1024], replicated
- grad_output: float32 [512, 512], replicated
- grad_up: float32 [512, 2048], replicated
- grad_bias_up: float32 [2048], replicated
- grad_down: float32 [2048, 512], replicated
- grad_bias_down: float32 [512], replicated
- grad_gain_attn: float32 [512], replicated
- grad_shift_attn: float32 [512], replicated
- grad_gain_mlp: float32 [512], replicated
- grad_shift_mlp: float32 [512], replicated
The draws below stay inside these ranges and needn't reach their ends.
Inputs may be any that keep to these rules, and one draw needn't show every extreme that they name: `counts`: A device's filled slots are its first ones; in every group some device of the cycle has all 1 filled. `slot_item`: for each group and slot index, items hold that slot on runs of 5 neighbouring devices of the cycle, wrapping past its last device; one such run crosses from the last device to the first; -1 marks a slot without an item. `slot_view`: along an item's run of devices its view numbers rise from 0 to 4.
All inputs are finite; a program needn't handle non-finite values. No bound on the sum of `keyframe` on one device may be relied on, other than what follows from the above.
Results may differ from the reference program's by a relative error of at most 0.01.
Values may be sent and summed in bfloat16 or wider, within the bound.
A program may use at most 256 MiB of HBM per device.

```python
from functools import partial
import jax
import jax.numpy as jnp
from jax import lax

D = 512
HEADS = 8
HEAD_DIM = 64
FF = 2048
VIEWS = 5
PATCHES = 400
LANG = 77
ROWS = 512
SLOTS = 1
GROUPS = 2
CYCLE = 16


def cycle_layout(key):
    per_cycle = CYCLE // VIEWS
    key_pick, key_wrap = jax.random.split(key)
    crossing = jax.random.randint(key_pick, (GROUPS, SLOTS), 0, per_cycle)
    extra = jax.random.randint(key_wrap, (GROUPS, SLOTS), 0, VIEWS - 1)
    anchor = (CYCLE - VIEWS + 1 + extra - VIEWS * crossing) % CYCLE
    device = jnp.arange(CYCLE, dtype=jnp.int32)[None, :, None]
    position = (device - anchor[:, None, :]) % CYCLE
    item_index = jnp.where(position < per_cycle * VIEWS, position // VIEWS, -1)
    view_index = position % VIEWS
    return (item_index.astype(jnp.int32), view_index.astype(jnp.int32))


def draw_slot_item(key, part):
    item_index, view_index = cycle_layout(key)
    return item_index


def draw_slot_view(key, part):
    item_index, view_index = cycle_layout(key)
    return view_index


def draw_counts(key, part):
    key = jax.random.fold_in(key, 11)
    key_halve, key_full = jax.random.split(key)
    halvings = jax.random.randint(key_halve, (GROUPS, CYCLE), 0, 2)
    capacity = jnp.full((GROUPS, CYCLE), SLOTS, jnp.int32)
    filled = jnp.maximum(jnp.right_shift(capacity, halvings), 1)
    fullest = jax.random.randint(key_full, (GROUPS, 1), 0, CYCLE)
    device = jnp.arange(CYCLE, dtype=jnp.int32)[None, :]
    return jnp.where(device == fullest, capacity, filled).astype(jnp.int32)


def plant(entries, stream_key, low, largest):
    longest = entries.shape.index(max(entries.shape))
    spots = []
    for shift in (0, 1):
        where = [jax.random.randint(jax.random.fold_in(stream_key, axis), (), 0, length) for axis, length in enumerate(entries.shape)]
        where[longest] = (where[longest] + shift) % entries.shape[longest]
        spots.append(tuple(where))
    return entries.at[spots[0]].set(low).at[spots[1]].set(largest)


def level_of(rng, shape, cuts, least, high):
    def one(axis_at, blocks):
        draws = jax.random.uniform(jax.random.fold_in(jax.random.fold_in(rng, 6), axis_at), (blocks,), jnp.float32, least / len(cuts), high / len(cuts))
        return jnp.repeat(jnp.exp(draws), shape[axis_at] // blocks).reshape((-1,) + (1,) * (len(shape) - axis_at - 1))

    level = one(*cuts[0])
    for cut in cuts[1:]:
        level = level * one(*cut)
    return level


def bell_draw(own_key, dims, scale, bound, pieces=(), kind=jnp.bfloat16):
    level = level_of(own_key, dims, pieces, -0.22, 0.18) if pieces else 1.0
    drawn = jax.random.normal(own_key, dims, jnp.float32) * scale * level
    return jnp.minimum(jnp.maximum(drawn, -bound), bound).astype(kind)


def setup_inputs(seed: int = 0) -> dict:
    arg_keys = jax.random.split(jax.random.key(seed), 18)
    return {
        "tokens": bell_draw(arg_keys[0], (GROUPS, CYCLE, SLOTS, ROWS, D), 1.0, 6.0, ((0, 2), (1, 16))),
        "counts": draw_counts(jax.random.fold_in(arg_keys[17], 71), 0),
        "slot_item": draw_slot_item(jax.random.fold_in(arg_keys[17], 71), 0),
        "slot_view": draw_slot_view(jax.random.fold_in(arg_keys[17], 71), 0),
        "keyframe": plant((jax.random.randint(arg_keys[4], (GROUPS, CYCLE, SLOTS), 0, 8) < 7).astype(jnp.int32), jax.random.fold_in(arg_keys[4], 1), 0, 1),
        "w_query": bell_draw(arg_keys[5], (D, D), D ** -0.5, 0.25),
        "w_keyval": bell_draw(arg_keys[6], (D, 2 * D), D ** -0.5, 0.25),
        "w_output": bell_draw(arg_keys[7], (D, D), (D // 64) ** -0.5, 2.0),
        "w_up": bell_draw(arg_keys[8], (D, FF), D ** -0.5, 0.25),
        "bias_up": bell_draw(arg_keys[9], (FF,), 0.3, 1.5),
        "w_down": bell_draw(arg_keys[10], (FF, D), FF ** -0.5, 0.125),
        "bias_down": bell_draw(arg_keys[11], (D,), 0.3, 1.5),
        "gain_attn": jnp.clip(1.0 + 0.1 * jax.random.normal(arg_keys[12], (D,), jnp.float32), 0.5, 1.5).astype(jnp.bfloat16),
        "shift_attn": bell_draw(arg_keys[13], (D,), 0.3, 1.5),
        "gain_mlp": jnp.clip(1.0 + 0.1 * jax.random.normal(arg_keys[14], (D,), jnp.float32), 0.5, 1.5).astype(jnp.bfloat16),
        "shift_mlp": bell_draw(arg_keys[15], (D,), 0.3, 1.5),
        "cotangent": bell_draw(arg_keys[16], (GROUPS, CYCLE, SLOTS, ROWS, D), 1.0, 6.0, ((0, 2), (1, 16))),
    }


HIGHEST = lax.Precision.HIGHEST
NEGATIVE = -1e+30
EPSILON = 1e-05

@jax.custom_vjp
def low(v):
    return lax.optimization_barrier(v.astype(jnp.bfloat16)).astype(jnp.float32)

@jax.custom_vjp
def low_back(v):
    return v

def low_keep(v):
    return (low(v), None)

def low_pass(kept, grad):
    return (grad,)

def back_keep(v):
    return (v, None)

def back_low(kept, grad):
    return (low(grad),)
low.defvjp(low_keep, low_pass)
low_back.defvjp(back_keep, back_low)

def label_rows(counts, slot_item, slot_view, keyframe):
    slot_index = jnp.arange(slot_item.shape[-1], dtype=jnp.int32)
    slot_filled = (slot_index < counts[..., None]) & (keyframe == 1) & (slot_item >= 0)
    row_index = jnp.arange(ROWS, dtype=jnp.int32)
    language = row_index - PATCHES
    row_live = (row_index < PATCHES) | (slot_view[..., None] == 0) & (language < LANG)
    return jnp.where(slot_filled[..., None] & row_live, slot_item[..., None], -1).astype(jnp.int32)

def layer_norm(values, gain, shift):
    average = lax.optimization_barrier(jnp.mean(values, -1, keepdims=True))
    centered = values - average
    variance = lax.optimization_barrier(jnp.mean(centered * centered, -1, keepdims=True))
    return centered * lax.rsqrt(variance + EPSILON) * gain + shift

def project(values, weight):
    return jnp.einsum('...d,de->...e', values, weight, precision=HIGHEST)

def by_slot(array):
    shifted = jnp.moveaxis(array, 2, 1)
    return shifted.reshape((GROUPS * SLOTS,) + shifted.shape[2:])

def heads_first(array):
    return jnp.moveaxis(array.reshape(array.shape[0], array.shape[1], HEADS, HEAD_DIM), 2, 0)

def head_attention(blocks, cycle_labels, window_labels):
    query_head, key_head, value_head = blocks
    scores = low_back(jnp.einsum('nre,nke->nrk', query_head, key_head, precision=HIGHEST) * HEAD_DIM ** (-0.5))
    matching = (cycle_labels[:, :, None] == window_labels[:, None, :]) & (window_labels[:, None, :] >= 0)
    masked = jnp.where(matching, scores, NEGATIVE)
    top_score = lax.optimization_barrier(jnp.max(masked, -1, keepdims=True))
    log_total = top_score + jnp.log(lax.optimization_barrier(jnp.sum(jnp.exp(masked - top_score), -1, keepdims=True)))
    attention = low(jnp.exp(masked - log_total))
    return jnp.einsum('nrk,nke->nre', attention, value_head, precision=HIGHEST)

def attend_cycle(blocks):
    query_cycle, keyval_cycle, label_cycle = blocks
    window = jnp.concatenate([jnp.roll(keyval_cycle, offset, 0) for offset in range(1 - VIEWS, VIEWS)], 1)
    window_labels = jnp.concatenate([jnp.roll(label_cycle, offset, 0) for offset in range(1 - VIEWS, VIEWS)], 1)
    per_head = jax.checkpoint(partial(head_attention, cycle_labels=label_cycle, window_labels=window_labels))
    mixed_heads = lax.map(per_head, (heads_first(query_cycle), heads_first(window[..., :D]), heads_first(window[..., D:])))
    return jnp.moveaxis(mixed_heads, 0, 2).reshape(CYCLE, ROWS, D)

def forward(tokens, w_query, w_keyval, w_output, w_up, bias_up, w_down, bias_down, gain_attn, shift_attn, gain_mlp, shift_mlp, labels=None):
    live = (labels >= 0).astype(tokens.dtype)[..., None]
    normed = low(layer_norm(tokens, gain_attn, shift_attn))
    queries = low(low_back(project(normed, w_query)))
    key_values = low(low_back(project(normed, w_keyval)))
    mixed_cycles = lax.map(jax.checkpoint(attend_cycle), (by_slot(queries), by_slot(key_values), by_slot(labels)))
    mixed = jnp.moveaxis(mixed_cycles.reshape(GROUPS, SLOTS, CYCLE, ROWS, D), 1, 2)
    mixed = low(low_back(mixed))
    attended = low_back(project(mixed, w_output))
    residual = tokens + live * attended
    normed_mlp = low(layer_norm(residual, gain_mlp, shift_mlp))
    before = low_back(project(normed_mlp, w_up) + bias_up)
    activated = low(jax.nn.gelu(before, approximate=False))
    branch = low_back(project(activated, w_down) + bias_down)
    return residual + live * branch

def reference(tokens, counts, slot_item, slot_view, keyframe, w_query, w_keyval, w_output, w_up, bias_up, w_down, bias_down, gain_attn, shift_attn, gain_mlp, shift_mlp, cotangent):
    labels = label_rows(counts, slot_item, slot_view, keyframe)
    arrays = tuple((array.astype(jnp.float32) for array in (tokens, w_query, w_keyval, w_output, w_up, bias_up, w_down, bias_down, gain_attn, shift_attn, gain_mlp, shift_mlp)))
    output, pullback = jax.vjp(partial(forward, labels=labels), *arrays)
    gradients = pullback(cotangent.astype(jnp.float32))
    return (output.astype(jnp.bfloat16), gradients[0], gradients[1], gradients[2], gradients[3], gradients[4], gradients[5], gradients[6], gradients[7], gradients[8], gradients[9], gradients[10], gradients[11])
```

```python
import functools

import jax
import jax.numpy as jnp
from jax import lax
from jax.experimental import pallas as pl
from jax.experimental.pallas import tpu as pltpu
from jax.sharding import PartitionSpec as P

D = 512
HEADS = 8
HEAD_DIM = 64
PAIRS = HEADS // 2
PAIR = 2 * HEAD_DIM
VIEWS = 5
PATCHES = 400
LANG = 77
ROWS = 512
USED = 480
TAIL = USED - PATCHES
SENT = 496
KEYS = VIEWS * PATCHES + TAIL
KEYS_PADDED = 2176
FF = 2048
FF_BLOCK = 512
NEGATIVE = -1e30
EPSILON = 1e-5
CHUNKS = 6
CHUNK_ROWS = 1024

BF16 = jnp.bfloat16
F32 = jnp.float32
MESH = pl.DeviceIdType.MESH
NN = (((1,), (0,)), ((), ()))
NT = (((1,), (1,)), ((), ()))
TN = (((0,), (0,)), ((), ()))
TT = (((0,), (1,)), ((), ()))
MIB = 2**20

VMEM = pltpu.VMEM
IN_VMEM = pl.BlockSpec(memory_space=pltpu.VMEM)
IN_SMEM = pl.BlockSpec(memory_space=pltpu.SMEM)
ANYWHERE = pl.BlockSpec(memory_space=pl.ANY)


def dot(left, right, dims):
    return lax.dot_general(left, right, dims, preferred_element_type=F32)


def normalise(values):
    average = jnp.mean(values, -1, keepdims=True)
    centered = values - average
    variance = jnp.mean(centered * centered, -1, keepdims=True)
    scale = lax.rsqrt(variance + EPSILON)
    return centered * scale, scale


def norm_backward(grad, unit, scale, gain):
    grad = grad * gain
    first = jnp.mean(grad, -1, keepdims=True)
    second = jnp.mean(grad * unit, -1, keepdims=True)
    return scale * (grad - first - unit * second)


def greet(others):
    barrier = pltpu.get_barrier_semaphore()
    for other in others:
        pl.semaphore_signal(barrier, inc=1, device_id=other, device_id_type=MESH)
    pl.semaphore_wait(barrier, len(others))


def gather_kernel(count, block, window, own_sem, send_sem, recv_sem, pass_sem, given_sem):
    me = lax.axis_index("view")
    step = 1 - 2 * lax.rem(me, 2)

    def at(offset):
        return {"view": lax.rem(me + offset + count, count)}

    far = (4, -4, 2, -2)
    greet([at(offset) for offset in far] + [at(step)])
    own = pltpu.make_async_copy(block, window.at[4], own_sem)
    own.start()

    def to(k, offset):
        return pltpu.make_async_remote_copy(
            block, window.at[4 - offset], send_sem.at[k], recv_sem.at[k], at(offset), MESH
        )

    def across(k, offset, source):
        return pltpu.make_async_remote_copy(
            source,
            window.at[4 + offset - step],
            pass_sem.at[k],
            given_sem.at[k],
            at(step),
            MESH,
        )

    sends = [to(k, offset) for k, offset in enumerate(far)]
    for copy in sends:
        copy.start()
    passes = [across(0, 0, block)]
    passes[0].start()
    for k, offset in ((2, -2), (3, 2)):
        sends[k].wait_recv()
        copy = across(k - 1, offset, window.at[4 + offset])
        copy.start()
        passes.append(copy)
    even = lax.rem(me, 2) == 0
    for k in (0, 1):
        sends[k].wait_recv()
    copy = across(3, 4 * step, window.at[4 + 4 * step])
    copy.start()
    passes.append(copy)
    for copy in passes:
        copy.wait()
    for copy in sends:
        copy.wait_send()
    own.wait()


def gather_window(block, count):
    return pl.pallas_call(
        functools.partial(gather_kernel, count),
        out_shape=jax.ShapeDtypeStruct((2 * VIEWS - 1, SENT, D), BF16),
        in_specs=[ANYWHERE],
        out_specs=ANYWHERE,
        scratch_shapes=[pltpu.SemaphoreType.DMA] + [pltpu.SemaphoreType.DMA((4,))] * 4,
        compiler_params=pltpu.CompilerParams(collective_id=0, has_side_effects=True),
        name="gather_window",
    )(block)


def compute_kernel(
    view,
    filled,
    window,
    cotangent,
    w_query,
    w_keyval,
    w_output,
    w_up,
    bias_up,
    w_down,
    bias_down,
    gain_attn,
    shift_attn,
    gain_mlp,
    shift_mlp,
    block_output,
    residual_grad,
    grads,
    sums_up,
    sums,
    parts,
    own_part,
    normed_all,
    query_norm,
    key_bias,
    keyval,
    query,
    weights,
    mixed,
    inverse,
    keyval_grad,
    query_grad,
    mixed_grad,
    normed_mlp,
    branch_grad,
    branch,
    mlp_back,
    blocks,
    block_sem,
):
    my_view = view[0]
    my_filled = filled[0]
    gain_a = gain_attn[...].astype(F32)
    shift_a = shift_attn[...].astype(F32)
    gain_m = gain_mlp[...].astype(F32)
    shift_m = shift_mlp[...].astype(F32)

    copies = []
    for j in range(VIEWS):
        slot = jnp.where(my_view + j < VIEWS, 4 + j, j - 1)
        copies.append(pltpu.make_async_copy(window.at[slot], blocks.at[j], block_sem.at[j]))
        copies[-1].start()
    copies[0].wait()
    own_rows = blocks[0, :USED, :]
    own_unit, _ = normalise(own_rows.astype(F32))
    own_normed = (own_unit * gain_a + shift_a).astype(BF16)
    query_norm[...] = own_normed
    normed_all[:PATCHES, :] = own_normed[:PATCHES, :]
    my_label = blocks[0, USED:SENT, :PAIR].astype(F32)

    def bias_of(label):
        match = jnp.logical_and(label == my_label, label >= 0)
        return jnp.where(match, 0.0, NEGATIVE)[:1, :]

    key_bias[:PATCHES, :] = jnp.broadcast_to(bias_of(my_label), (PATCHES, PAIR)).astype(BF16)
    language = own_rows[PATCHES:, :]
    language_bias = bias_of(my_label)
    for j in range(1, VIEWS):
        copies[j].wait()
        block = blocks[j, :USED, :]
        label = blocks[j, USED:SENT, :PAIR].astype(F32)
        unit, _ = normalise(block[:PATCHES, :].astype(F32))
        rows = slice(j * PATCHES, (j + 1) * PATCHES)
        normed_all[rows, :] = (unit * gain_a + shift_a).astype(BF16)
        bias = bias_of(label)
        key_bias[rows, :] = jnp.broadcast_to(bias, (PATCHES, PAIR)).astype(BF16)
        holds = lax.rem(my_view + j, VIEWS) == 0
        language = jnp.where(holds, block[PATCHES:, :], language)
        language_bias = jnp.where(holds, bias, language_bias)
    unit, _ = normalise(language.astype(F32))
    normed_all[VIEWS * PATCHES : KEYS, :] = (unit * gain_a + shift_a).astype(BF16)
    index = lax.broadcasted_iota(jnp.int32, (TAIL, PAIR), 0)
    key_bias[VIEWS * PATCHES : KEYS, :] = jnp.where(
        index < LANG, jnp.broadcast_to(language_bias, (TAIL, PAIR)), NEGATIVE
    ).astype(BF16)
    normed_all[KEYS:, :] = jnp.zeros((KEYS_PADDED - KEYS, D), BF16)
    key_bias[KEYS:, :] = jnp.full((KEYS_PADDED - KEYS, PAIR), NEGATIVE, BF16)

    query[...] = (dot(own_normed, w_query[...], NN).astype(BF16) * HEAD_DIM**-0.5).astype(BF16)
    for c in range(2):
        columns = slice(c * D, (c + 1) * D)
        keyval[:, columns] = dot(normed_all[...], w_keyval[:, columns], NN).astype(BF16)

    lane = lax.broadcasted_iota(jnp.int32, (1, PAIR), 1)
    low_half = lane < HEAD_DIM

    def half_of(half, first, second):
        return jnp.where(low_half, first, second) if half == 0 else jnp.where(low_half, second, first)

    def head_keys(p, half):
        pair = keyval[:, pl.ds(pl.multiple_of(p * PAIR, PAIR), PAIR)]
        return half_of(half, pair, key_bias[...])

    def head_values(p, half):
        pair = keyval[:, pl.ds(pl.multiple_of(D + p * PAIR, PAIR), PAIR)]
        return half_of(half, pair, jnp.ones((), BF16))

    def forward_pair(p, _):
        columns = pl.ds(pl.multiple_of(p * PAIR, PAIR), PAIR)
        pair = query[:, columns]
        outs = []
        totals = []
        for half in range(2):
            one = (lane == HEAD_DIM * (1 - half)).astype(BF16)
            scores = dot(half_of(half, pair, one), head_keys(p, half), NT)
            top = jnp.max(scores, -1, keepdims=True)
            weight = jnp.exp(scores - top).astype(BF16)
            weights[2 * p + half] = weight
            out = dot(weight, head_values(p, half), NN)
            outs.append(out)
            totals.append(pltpu.roll(out, HEAD_DIM, 1))
        inv = 1.0 / jnp.where(low_half, totals[0], totals[1])
        full = jnp.where(low_half, outs[0], outs[1]) * inv
        inverse[:, columns] = inv
        own_part[:, columns] = full
        mixed[:, columns] = full.astype(BF16)
        return 0

    lax.fori_loop(0, PAIRS, forward_pair, 0)

    row = lax.broadcasted_iota(jnp.int32, (USED, PAIR), 0)
    has_language = (my_view == 0).astype(jnp.int32)
    live_rows = my_filled * (PATCHES + LANG * has_language)
    live = (row < live_rows).astype(F32)[:, :1]
    own = own_rows.astype(F32)
    res = own + live * dot(mixed[...], w_output[...], NN)
    residual_grad[...] = res
    unit_m, scale_m = normalise(res)
    normed_mlp[...] = (unit_m * gain_m + shift_m).astype(BF16)
    upstream = cotangent[:USED, :].astype(F32)
    branch_grad[...] = (live * upstream).astype(BF16)
    branch[...] = jnp.zeros((USED, D), F32)
    mlp_back[...] = jnp.zeros((USED, D), F32)

    def feed_forward(c, _):
        columns = pl.ds(pl.multiple_of(c * FF_BLOCK, FF_BLOCK), FF_BLOCK)
        before = dot(normed_mlp[...], w_up[:, columns], NN) + bias_up[:, columns].astype(F32)
        chance = 0.5 + 0.5 * lax.erf(before * 0.5**0.5)
        density = jnp.exp(-0.5 * before * before) * 0.3989422804014327
        activated = (before * chance).astype(BF16)
        slope = chance + before * density
        grads[pl.ds(pl.multiple_of(FF + c * FF_BLOCK, FF_BLOCK), FF_BLOCK), :] = dot(
            activated, branch_grad[...], TN
        ).astype(BF16)
        branch[...] += dot(activated, w_down[columns, :], NN)
        before_full = dot(branch_grad[...], w_down[columns, :], NT) * slope
        before_grad = before_full.astype(BF16)
        sums_up[:, columns] = jnp.sum(before_grad.astype(F32), 0, keepdims=True)
        grads[columns, :] = dot(normed_mlp[...], before_grad, TN).astype(BF16)
        mlp_back[...] += dot(before_grad, w_up[:, columns], NT)
        return 0

    lax.fori_loop(0, FF // FF_BLOCK, feed_forward, 0)
    block_output[:USED, :] = (
        residual_grad[...] + live * (branch[...] + bias_down[...].astype(F32))
    ).astype(BF16)
    block_output[USED:, :] = jnp.zeros((ROWS - USED, D), BF16)
    unit_m, scale_m = normalise(residual_grad[...])
    back = mlp_back[...]
    sums[0:1, :] = jnp.sum(branch_grad[...].astype(F32), 0, keepdims=True)
    sums[1:2, :] = jnp.sum(back * unit_m, 0, keepdims=True)
    sums[2:3, :] = jnp.sum(back, 0, keepdims=True)
    res_grad = upstream + norm_backward(back, unit_m, scale_m, gain_m)
    residual_grad[...] = res_grad
    attended_grad = (live * res_grad).astype(BF16)
    grads[2 * FF : 2 * FF + D, :] = dot(mixed[...], attended_grad, TN).astype(BF16)
    mixed_grad[...] = dot(attended_grad, w_output[...], NT).astype(BF16)

    def backward_pair(p, _):
        columns = pl.ds(pl.multiple_of(p * PAIR, PAIR), PAIR)
        grad = mixed_grad[:, columns].astype(F32)
        inv = inverse[:, columns]
        scaled = grad * inv
        product = scaled * own_part[:, columns]
        scaled_low = scaled.astype(BF16)
        scaled_t = scaled.T.astype(BF16)
        query_t = query[:, columns].astype(F32).T.astype(BF16)
        query_parts = []
        for half in range(2):
            here = low_half if half == 0 else jnp.logical_not(low_half)
            dots = -jnp.sum(jnp.where(here, product, 0.0), -1, keepdims=True)
            dots_high = dots.astype(BF16)
            dots_low = (dots - dots_high.astype(F32)).astype(BF16)
            other = HEAD_DIM * (1 - half)
            rest = jnp.where(
                lane == other, dots_high, jnp.where(lane == other + 1, dots_low, jnp.zeros((), BF16))
            )
            weight = weights[2 * p + half]
            slope = dot(half_of(half, scaled_low, rest), head_values(p, half), NT)
            score_grad = weight * slope.astype(BF16)
            query_parts.append(dot(score_grad, head_keys(p, half), NN))
            rows = slice(half * HEAD_DIM, (half + 1) * HEAD_DIM)
            start = pl.multiple_of(p * PAIR, PAIR) + half * HEAD_DIM
            keyval_grad[pl.ds(start, HEAD_DIM), :] = dot(query_t[rows, :], score_grad, NN).astype(
                BF16
            )
            keyval_grad[pl.ds(D + start, HEAD_DIM), :] = dot(
                scaled_t[rows, :], weight, NN
            ).astype(BF16)
        part = jnp.where(low_half, query_parts[0], query_parts[1]) * HEAD_DIM**-0.5
        query_grad[:, columns] = part.astype(BF16)
        return 0

    lax.fori_loop(0, PAIRS, backward_pair, 0)

    base = 2 * FF + D
    grads[base : base + D, :] = dot(query_norm[...], query_grad[...], TN).astype(BF16)
    for c in range(2):
        rows = slice(c * D, (c + 1) * D)
        grads[base + D + c * D : base + 2 * D + c * D, :] = dot(
            keyval_grad[rows, :], normed_all[...], NN
        ).astype(BF16)
    from_query = dot(query_grad[...], w_query[...], NT)
    normed = query_norm[...].astype(F32)
    shift_sum = jnp.sum(from_query, 0, keepdims=True)
    gain_sum = jnp.sum(from_query * normed, 0, keepdims=True)
    parts_at = []
    for j in range(VIEWS + 1):
        rows = slice(j * PATCHES, min((j + 1) * PATCHES, KEYS))
        piece = dot(keyval_grad[:, rows], w_keyval[...], TT)
        normed = normed_all[rows, :].astype(F32)
        shift_sum += jnp.sum(piece, 0, keepdims=True)
        gain_sum += jnp.sum(piece * normed, 0, keepdims=True)
        if j == 0:
            own_part[:PATCHES, :] = from_query[:PATCHES, :] + piece
        elif j < VIEWS:
            parts[j - 1, :PATCHES, :] = piece.astype(BF16)
        else:
            own_part[PATCHES:, :] = from_query[PATCHES:, :] + jnp.where(my_view == 0, piece, 0.0)
            for i in range(1, VIEWS):
                holds = lax.rem(my_view + i, VIEWS) == 0
                parts[i - 1, PATCHES:, :] = jnp.where(holds, piece, 0.0).astype(BF16)
    sums[3:4, :] = (gain_sum - shift_a * shift_sum) / gain_a
    sums[4:5, :] = shift_sum
    sums[5:8, :] = jnp.zeros((3, D), F32)


def compute(*args):
    shape = jax.ShapeDtypeStruct
    outs = (
        shape((ROWS, D), BF16),
        shape((USED, D), F32),
        shape((CHUNKS * CHUNK_ROWS, D), BF16),
        shape((1, FF), F32),
        shape((8, D), F32),
        shape((VIEWS - 1, USED, D), BF16),
        shape((USED, D), F32),
    )
    scratch = [
        VMEM((KEYS_PADDED, D), BF16),
        VMEM((USED, D), BF16),
        VMEM((KEYS_PADDED, PAIR), BF16),
        VMEM((KEYS_PADDED, 2 * D), BF16),
        VMEM((USED, D), BF16),
        VMEM((HEADS, USED, KEYS_PADDED), BF16),
        VMEM((USED, D), BF16),
        VMEM((USED, D), F32),
        VMEM((2 * D, KEYS_PADDED), BF16),
        VMEM((USED, D), BF16),
        VMEM((USED, D), BF16),
        VMEM((USED, D), BF16),
        VMEM((USED, D), BF16),
        VMEM((USED, D), F32),
        VMEM((USED, D), F32),
        VMEM((VIEWS, SENT, D), BF16),
        pltpu.SemaphoreType.DMA((VIEWS,)),
    ]
    return pl.pallas_call(
        compute_kernel,
        out_shape=outs,
        in_specs=[IN_SMEM] * 2 + [ANYWHERE] + [IN_VMEM] * (len(args) - 3),
        out_specs=[IN_VMEM] * len(outs),
        scratch_shapes=scratch,
        compiler_params=pltpu.CompilerParams(vmem_limit_bytes=63 * MIB),
        name="compute",
    )(*args)


def on_device(count, tokens, counts, slot_item, slot_view, keyframe, *rest):
    weights, cotangent = rest[:-1], rest[-1]
    rows = tokens.reshape(ROWS, D)
    item = slot_item.reshape(())
    filled = (counts.reshape(()) > 0) & (keyframe.reshape(()) == 1) & (item >= 0)
    label = jnp.where(filled, item, -1).astype(BF16)
    block = jnp.concatenate([rows[:USED], jnp.broadcast_to(label, (SENT - USED, D))])
    window = gather_window(block, count)
    weights = tuple(w.reshape(1, -1) if w.ndim == 1 else w for w in weights)
    cot = cotangent.reshape(ROWS, D)
    block_output, residual_grad, grads, sums_up, sums, parts, own_part = compute(
        slot_view.reshape(1), filled.astype(jnp.int32).reshape(1), window, cot, *weights
    )
    block_output = jnp.concatenate([block_output[:USED], rows[USED:]])
    view = slot_view.reshape(())
    total = own_part
    for offset in range(1 - VIEWS, VIEWS):
        if offset != 0:
            valid = (view + offset >= 0) & (view + offset < VIEWS)
            sent = jnp.where(valid, parts[(offset + VIEWS) % VIEWS - 1], 0)
            pairs = [(source, (source + offset) % count) for source in range(count)]
            total = total + lax.ppermute(sent, "view", pairs).astype(F32)
    gain = rest[7].astype(F32)
    unit, scale = normalise(rows[:USED].astype(F32))
    used = residual_grad + norm_backward(total, unit, scale, gain)
    grad_tokens = jnp.concatenate([used, cot[USED:].astype(F32)])
    grads, sums_up, sums = lax.psum((grads.astype(F32), sums_up, sums), ("view", "dp"))
    return (
        block_output.reshape(tokens.shape),
        grad_tokens.reshape(tokens.shape),
        grads[2 * FF + D : 2 * FF + 2 * D],
        grads[2 * FF + 2 * D :].T,
        grads[2 * FF : 2 * FF + D],
        jnp.concatenate([grads[c * D : (c + 1) * D] for c in range(FF // D)], 1),
        sums_up.reshape(-1),
        grads[FF : 2 * FF],
        sums[0],
        sums[3],
        sums[4],
        sums[1],
        sums[2],
    )


def solution(mesh):
    count = mesh.shape["view"]
    slots = P("dp", "view", None)
    rows = P("dp", "view", None, None, None)
    in_specs = (rows, P("dp", "view"), slots, slots, slots) + (P(),) * 11 + (rows,)
    out_specs = (rows, rows) + (P(),) * 11
    return jax.shard_map(
        functools.partial(on_device, count),
        mesh=mesh,
        in_specs=in_specs,
        out_specs=out_specs,
        check_vma=False,
    )
```

```python
import functools

import jax
import jax.numpy as jnp
from jax import lax
from jax.experimental import pallas as pl
from jax.experimental.pallas import tpu as pltpu
from jax.sharding import PartitionSpec as P

D = 512
HEADS = 8
HEAD_DIM = 64
PAIRS = HEADS // 2
PAIR = 2 * HEAD_DIM
VIEWS = 5
PATCHES = 400
LANG = 77
ROWS = 512
USED = 480
TAIL = USED - PATCHES
SENT = 496
KEYS = VIEWS * PATCHES + TAIL
KEYS_PADDED = 2176
FF = 2048
FF_BLOCK = 512
NEGATIVE = -1e30
EPSILON = 1e-5
GRAD_ROWS = 2 * FF + 4 * D
SUMS = 16
SHARD = 16
STAGES = 8

BF16 = jnp.bfloat16
F32 = jnp.float32
MESH = pl.DeviceIdType.MESH
NN = (((1,), (0,)), ((), ()))
NT = (((1,), (1,)), ((), ()))
TN = (((0,), (0,)), ((), ()))
TT = (((0,), (1,)), ((), ()))
MIB = 2**20

VMEM = pltpu.VMEM
IN_VMEM = pl.BlockSpec(memory_space=pltpu.VMEM)
IN_SMEM = pl.BlockSpec(memory_space=pltpu.SMEM)
ANYWHERE = pl.BlockSpec(memory_space=pl.ANY)


def dot(left, right, dims):
    return lax.dot_general(left, right, dims, preferred_element_type=F32)


def normalise(values):
    average = jnp.mean(values, -1, keepdims=True)
    centered = values - average
    variance = jnp.mean(centered * centered, -1, keepdims=True)
    scale = lax.rsqrt(variance + EPSILON)
    return centered * scale, scale


def norm_backward(grad, unit, scale, gain):
    grad = grad * gain
    first = jnp.mean(grad, -1, keepdims=True)
    second = jnp.mean(grad * unit, -1, keepdims=True)
    return scale * (grad - first - unit * second)


def greet(others):
    barrier = pltpu.get_barrier_semaphore()
    for other in others:
        pl.semaphore_signal(barrier, inc=1, device_id=other, device_id_type=MESH)
    pl.semaphore_wait(barrier, len(others))


def gather_kernel(count, block, window, own_sem, send_sem, recv_sem, pass_sem, given_sem):
    me = lax.axis_index("view")
    step = 1 - 2 * lax.rem(me, 2)

    def at(offset):
        return {"view": lax.rem(me + offset + count, count)}

    far = (4, -4, 2, -2)
    greet([at(offset) for offset in far] + [at(step)])
    own = pltpu.make_async_copy(block, window.at[4], own_sem)
    own.start()

    def to(k, offset):
        return pltpu.make_async_remote_copy(
            block, window.at[4 - offset], send_sem.at[k], recv_sem.at[k], at(offset), MESH
        )

    def across(k, offset, source):
        return pltpu.make_async_remote_copy(
            source,
            window.at[4 + offset - step],
            pass_sem.at[k],
            given_sem.at[k],
            at(step),
            MESH,
        )

    sends = [to(k, offset) for k, offset in enumerate(far)]
    for copy in sends:
        copy.start()
    passes = [across(0, 0, block)]
    passes[0].start()
    for k, offset in ((2, -2), (3, 2)):
        sends[k].wait_recv()
        copy = across(k - 1, offset, window.at[4 + offset])
        copy.start()
        passes.append(copy)
    even = lax.rem(me, 2) == 0
    for k in (0, 1):
        sends[k].wait_recv()
    copy = across(3, 4 * step, window.at[4 + 4 * step])
    copy.start()
    passes.append(copy)
    for copy in passes:
        copy.wait()
    for copy in sends:
        copy.wait_send()
    own.wait()


def gather_window(block, count):
    return pl.pallas_call(
        functools.partial(gather_kernel, count),
        out_shape=jax.ShapeDtypeStruct((2 * VIEWS - 1, SENT, D), BF16),
        in_specs=[ANYWHERE],
        out_specs=ANYWHERE,
        scratch_shapes=[pltpu.SemaphoreType.DMA] + [pltpu.SemaphoreType.DMA((4,))] * 4,
        compiler_params=pltpu.CompilerParams(collective_id=0, has_side_effects=True),
        name="gather_window",
    )(block)


def compute_kernel(
    view,
    filled,
    window,
    cotangent,
    w_query,
    w_keyval,
    w_output,
    w_up,
    bias_up,
    w_down,
    bias_down,
    gain_attn,
    shift_attn,
    gain_mlp,
    shift_mlp,
    block_output,
    residual_grad,
    grads,
    sums,
    parts,
    own_part,
    normed_all,
    query_norm,
    key_bias,
    keyval,
    query,
    weights,
    mixed,
    inverse,
    keyval_grad,
    query_grad,
    mixed_grad,
    normed_mlp,
    branch_grad,
    branch,
    mlp_back,
    blocks,
    block_sem,
):
    my_view = view[0]
    my_filled = filled[0]
    gain_a = gain_attn[...].astype(F32)
    shift_a = shift_attn[...].astype(F32)
    gain_m = gain_mlp[...].astype(F32)
    shift_m = shift_mlp[...].astype(F32)

    copies = []
    for j in range(VIEWS):
        slot = jnp.where(my_view + j < VIEWS, 4 + j, j - 1)
        copies.append(pltpu.make_async_copy(window.at[slot], blocks.at[j], block_sem.at[j]))
        copies[-1].start()
    copies[0].wait()
    own_rows = blocks[0, :USED, :]
    own_unit, _ = normalise(own_rows.astype(F32))
    own_normed = (own_unit * gain_a + shift_a).astype(BF16)
    query_norm[...] = own_normed
    normed_all[:PATCHES, :] = own_normed[:PATCHES, :]
    my_label = blocks[0, USED:SENT, :PAIR].astype(F32)

    def bias_of(label):
        match = jnp.logical_and(label == my_label, label >= 0)
        return jnp.where(match, 0.0, NEGATIVE)[:1, :]

    key_bias[:PATCHES, :] = jnp.broadcast_to(bias_of(my_label), (PATCHES, PAIR)).astype(BF16)
    language = own_rows[PATCHES:, :]
    language_bias = bias_of(my_label)
    for j in range(1, VIEWS):
        copies[j].wait()
        block = blocks[j, :USED, :]
        label = blocks[j, USED:SENT, :PAIR].astype(F32)
        unit, _ = normalise(block[:PATCHES, :].astype(F32))
        rows = slice(j * PATCHES, (j + 1) * PATCHES)
        normed_all[rows, :] = (unit * gain_a + shift_a).astype(BF16)
        bias = bias_of(label)
        key_bias[rows, :] = jnp.broadcast_to(bias, (PATCHES, PAIR)).astype(BF16)
        holds = lax.rem(my_view + j, VIEWS) == 0
        language = jnp.where(holds, block[PATCHES:, :], language)
        language_bias = jnp.where(holds, bias, language_bias)
    unit, _ = normalise(language.astype(F32))
    normed_all[VIEWS * PATCHES : KEYS, :] = (unit * gain_a + shift_a).astype(BF16)
    index = lax.broadcasted_iota(jnp.int32, (TAIL, PAIR), 0)
    key_bias[VIEWS * PATCHES : KEYS, :] = jnp.where(
        index < LANG, jnp.broadcast_to(language_bias, (TAIL, PAIR)), NEGATIVE
    ).astype(BF16)
    normed_all[KEYS:, :] = jnp.zeros((KEYS_PADDED - KEYS, D), BF16)
    key_bias[KEYS:, :] = jnp.full((KEYS_PADDED - KEYS, PAIR), NEGATIVE, BF16)

    query[...] = (dot(own_normed, w_query[...], NN).astype(BF16) * HEAD_DIM**-0.5).astype(BF16)
    for c in range(2):
        columns = slice(c * D, (c + 1) * D)
        keyval[:, columns] = dot(normed_all[...], w_keyval[:, columns], NN).astype(BF16)

    lane = lax.broadcasted_iota(jnp.int32, (1, PAIR), 1)
    low_half = lane < HEAD_DIM

    def half_of(half, first, second):
        return jnp.where(low_half, first, second) if half == 0 else jnp.where(low_half, second, first)

    def head_keys(p, half):
        pair = keyval[:, pl.ds(pl.multiple_of(p * PAIR, PAIR), PAIR)]
        return half_of(half, pair, key_bias[...])

    def head_values(p, half):
        pair = keyval[:, pl.ds(pl.multiple_of(D + p * PAIR, PAIR), PAIR)]
        return half_of(half, pair, jnp.ones((), BF16))

    def forward_pair(p, _):
        columns = pl.ds(pl.multiple_of(p * PAIR, PAIR), PAIR)
        pair = query[:, columns]
        outs = []
        totals = []
        for half in range(2):
            one = (lane == HEAD_DIM * (1 - half)).astype(BF16)
            scores = dot(half_of(half, pair, one), head_keys(p, half), NT)
            top = jnp.max(scores, -1, keepdims=True)
            weight = jnp.exp(scores - top).astype(BF16)
            weights[2 * p + half] = weight
            out = dot(weight, head_values(p, half), NN)
            outs.append(out)
            totals.append(pltpu.roll(out, HEAD_DIM, 1))
        inv = 1.0 / jnp.where(low_half, totals[0], totals[1])
        full = jnp.where(low_half, outs[0], outs[1]) * inv
        inverse[:, columns] = inv
        own_part[:, columns] = full
        mixed[:, columns] = full.astype(BF16)
        return 0

    lax.fori_loop(0, PAIRS, forward_pair, 0)

    row = lax.broadcasted_iota(jnp.int32, (USED, PAIR), 0)
    has_language = (my_view == 0).astype(jnp.int32)
    live_rows = my_filled * (PATCHES + LANG * has_language)
    live = (row < live_rows).astype(F32)[:, :1]
    own = own_rows.astype(F32)
    res = own + live * dot(mixed[...], w_output[...], NN)
    residual_grad[...] = res
    unit_m, scale_m = normalise(res)
    normed_mlp[...] = (unit_m * gain_m + shift_m).astype(BF16)
    upstream = cotangent[:USED, :].astype(F32)
    branch_grad[...] = (live * upstream).astype(BF16)
    branch[...] = jnp.zeros((USED, D), F32)
    mlp_back[...] = jnp.zeros((USED, D), F32)

    def feed_forward(c, _):
        columns = pl.ds(pl.multiple_of(c * FF_BLOCK, FF_BLOCK), FF_BLOCK)
        before = dot(normed_mlp[...], w_up[:, columns], NN) + bias_up[:, columns].astype(F32)
        chance = 0.5 + 0.5 * lax.erf(before * 0.5**0.5)
        density = jnp.exp(-0.5 * before * before) * 0.3989422804014327
        activated = (before * chance).astype(BF16)
        slope = chance + before * density
        grads[columns, :] = dot(
            activated, branch_grad[...], TN
        ).astype(BF16)
        branch[...] += dot(activated, w_down[columns, :], NN)
        before_full = dot(branch_grad[...], w_down[columns, :], NT) * slope
        before_grad = before_full.astype(BF16)
        sums[pl.ds(c, 1), :] = jnp.sum(before_grad.astype(F32), 0, keepdims=True)
        up_rows = pl.ds(pl.multiple_of(FF + c * FF_BLOCK, FF_BLOCK), FF_BLOCK)
        grads[up_rows, :] = dot(normed_mlp[...], before_grad, TN).astype(BF16)
        mlp_back[...] += dot(before_grad, w_up[:, columns], NT)
        return 0

    lax.fori_loop(0, FF // FF_BLOCK, feed_forward, 0)
    block_output[:USED, :] = (
        residual_grad[...] + live * (branch[...] + bias_down[...].astype(F32))
    ).astype(BF16)
    block_output[USED:, :] = jnp.zeros((ROWS - USED, D), BF16)
    unit_m, scale_m = normalise(residual_grad[...])
    back = mlp_back[...]
    sums[4:5, :] = jnp.sum(branch_grad[...].astype(F32), 0, keepdims=True)
    sums[5:6, :] = jnp.sum(back * unit_m, 0, keepdims=True)
    sums[6:7, :] = jnp.sum(back, 0, keepdims=True)
    res_grad = upstream + norm_backward(back, unit_m, scale_m, gain_m)
    residual_grad[...] = res_grad
    attended_grad = (live * res_grad).astype(BF16)
    grads[2 * FF : 2 * FF + D, :] = dot(mixed[...], attended_grad, TN).astype(BF16)
    mixed_grad[...] = dot(attended_grad, w_output[...], NT).astype(BF16)

    def backward_pair(p, _):
        columns = pl.ds(pl.multiple_of(p * PAIR, PAIR), PAIR)
        grad = mixed_grad[:, columns].astype(F32)
        inv = inverse[:, columns]
        scaled = grad * inv
        product = scaled * own_part[:, columns]
        scaled_low = scaled.astype(BF16)
        scaled_t = scaled.T.astype(BF16)
        query_t = query[:, columns].astype(F32).T.astype(BF16)
        query_parts = []
        for half in range(2):
            here = low_half if half == 0 else jnp.logical_not(low_half)
            dots = -jnp.sum(jnp.where(here, product, 0.0), -1, keepdims=True)
            dots_high = dots.astype(BF16)
            dots_low = (dots - dots_high.astype(F32)).astype(BF16)
            other = HEAD_DIM * (1 - half)
            rest = jnp.where(
                lane == other, dots_high, jnp.where(lane == other + 1, dots_low, jnp.zeros((), BF16))
            )
            weight = weights[2 * p + half]
            slope = dot(half_of(half, scaled_low, rest), head_values(p, half), NT)
            score_grad = weight * slope.astype(BF16)
            query_parts.append(dot(score_grad, head_keys(p, half), NN))
            rows = slice(half * HEAD_DIM, (half + 1) * HEAD_DIM)
            start = pl.multiple_of(p * PAIR, PAIR) + half * HEAD_DIM
            keyval_grad[pl.ds(start, HEAD_DIM), :] = dot(query_t[rows, :], score_grad, NN).astype(
                BF16
            )
            keyval_grad[pl.ds(D + start, HEAD_DIM), :] = dot(
                scaled_t[rows, :], weight, NN
            ).astype(BF16)
        part = jnp.where(low_half, query_parts[0], query_parts[1]) * HEAD_DIM**-0.5
        query_grad[:, columns] = part.astype(BF16)
        return 0

    lax.fori_loop(0, PAIRS, backward_pair, 0)

    base = 2 * FF + D
    grads[base : base + D, :] = dot(query_norm[...], query_grad[...], TN).astype(BF16)
    for c in range(2):
        rows = slice(c * D, (c + 1) * D)
        grads[base + D + c * D : base + 2 * D + c * D, :] = dot(
            keyval_grad[rows, :], normed_all[...], NN
        ).T.astype(BF16)
    from_query = dot(query_grad[...], w_query[...], NT)
    normed = query_norm[...].astype(F32)
    shift_sum = jnp.sum(from_query, 0, keepdims=True)
    gain_sum = jnp.sum(from_query * normed, 0, keepdims=True)
    parts_at = []
    for j in range(VIEWS + 1):
        rows = slice(j * PATCHES, min((j + 1) * PATCHES, KEYS))
        piece = dot(keyval_grad[:, rows], w_keyval[...], TT)
        normed = normed_all[rows, :].astype(F32)
        shift_sum += jnp.sum(piece, 0, keepdims=True)
        gain_sum += jnp.sum(piece * normed, 0, keepdims=True)
        if j == 0:
            own_part[:PATCHES, :] = from_query[:PATCHES, :] + piece
        elif j < VIEWS:
            parts[j - 1, :PATCHES, :] = piece.astype(BF16)
        else:
            own_part[PATCHES:, :] = from_query[PATCHES:, :] + jnp.where(my_view == 0, piece, 0.0)
            for i in range(1, VIEWS):
                holds = lax.rem(my_view + i, VIEWS) == 0
                parts[i - 1, PATCHES:, :] = jnp.where(holds, piece, 0.0).astype(BF16)
    sums[7:8, :] = (gain_sum - shift_a * shift_sum) / gain_a
    sums[8:9, :] = shift_sum
    sums[9:, :] = jnp.zeros((SUMS - 9, D), F32)


def compute(grad_rows, *args):
    shape = jax.ShapeDtypeStruct
    outs = (
        shape((ROWS, D), BF16),
        shape((USED, D), F32),
        shape((grad_rows, D), BF16),
        shape((SUMS, D), F32),
        shape((VIEWS - 1, USED, D), BF16),
        shape((USED, D), F32),
    )
    scratch = [
        VMEM((KEYS_PADDED, D), BF16),
        VMEM((USED, D), BF16),
        VMEM((KEYS_PADDED, PAIR), BF16),
        VMEM((KEYS_PADDED, 2 * D), BF16),
        VMEM((USED, D), BF16),
        VMEM((HEADS, USED, KEYS_PADDED), BF16),
        VMEM((USED, D), BF16),
        VMEM((USED, D), F32),
        VMEM((2 * D, KEYS_PADDED), BF16),
        VMEM((USED, D), BF16),
        VMEM((USED, D), BF16),
        VMEM((USED, D), BF16),
        VMEM((USED, D), BF16),
        VMEM((USED, D), F32),
        VMEM((USED, D), F32),
        VMEM((VIEWS, SENT, D), BF16),
        pltpu.SemaphoreType.DMA((VIEWS,)),
    ]
    return pl.pallas_call(
        compute_kernel,
        out_shape=outs,
        in_specs=[IN_SMEM] * 2 + [ANYWHERE] + [IN_VMEM] * (len(args) - 3),
        out_specs=[IN_VMEM] * len(outs),
        scratch_shapes=scratch,
        compiler_params=pltpu.CompilerParams(vmem_limit_bytes=63 * MIB),
        name="compute",
    )(*args)


def reduce_kernel(
    count,
    groups,
    chunks,
    view,
    parts,
    own_part,
    residual_grad,
    tokens,
    cotangent,
    gain_attn,
    grads,
    sums,
    grad_tokens,
    summed,
    sums_out,
    acc,
    arrived_core,
    arrived_first,
    arrived_second,
    arrived_last,
    send_sem,
    recv_sem,
    local_sem,
    sums_at,
    sums_send,
    sums_recv,
    swap_out,
    swap_in,
    far_out,
    far_in,
    swap_sem,
    far_sem,
):
    me = lax.axis_index("view")
    group = lax.axis_index("dp")
    depth = count // 4
    core = lax.rem(me, 2)
    place = {"x": lax.rem(me // 2, 2), "y": group, "z": me // 4}
    size = {"x": 2, "y": groups, "z": depth}
    half = 2 * 2 * groups * depth * SHARD
    orders = (("x", "y", "z"), ("y", "x", "z"))
    arrived = (arrived_first, arrived_second, arrived_last)
    step = 1 - 2 * core

    def peer(dim, j):
        at = lax.rem(place[dim] + j, size[dim])
        if dim == "x":
            return {"view": me + 2 * (at - place["x"])}
        if dim == "y":
            return {"dp": at}
        return {"view": me + 4 * (at - place["z"])}

    def along(offset):
        return {"view": lax.rem(me + offset + count, count)}

    sibling = {"view": me + step}
    peers = [peer(dim, j) for dim in "xyz" for j in range(1, size[dim])]
    greet([sibling] + peers + [along(offset) for offset in (4, -4, 2, -2)])

    levels = []
    for order in orders:
        rows = half // 2
        offset = 0
        level = [(0, rows)]
        for dim in order:
            rows = rows // size[dim]
            offset = offset + place[dim] * rows
            level.append((offset, rows))
        levels.append(level)

    def copies(stage, k):
        out = []

        def add(source, target, device):
            n = len(out)
            out.append(
                pltpu.make_async_remote_copy(
                    source, target, send_sem.at[k, stage, n], recv_sem.at[k, stage, n], device, MESH
                )
            )

        for p, order in enumerate(orders):
            base = k * 2 * half + p * half

            def whole(offset, rows):
                return summed.at[pl.ds(pl.multiple_of(base + core * (half // 2) + offset, SHARD), rows)]

            if stage == 0:
                start = pl.multiple_of(base + (1 - core) * (half // 2), SHARD)
                add(grads.at[pl.ds(start, half // 2)], arrived_core.at[k, p], sibling)
            elif stage < 4:
                dim = order[stage - 1]
                offset, _ = levels[p][stage - 1]
                _, rows = levels[p][stage]
                for j in range(1, size[dim]):
                    at = lax.rem(place[dim] + j, size[dim])
                    start = pl.multiple_of(offset + at * rows, SHARD)
                    if p == 0 or stage == 3:
                        slot = p * (size[dim] - 1) + j - 1 if stage == 3 else j - 1
                    else:
                        slot = size["x" if stage == 1 else "y"] - 1 + j - 1
                    add(
                        acc.at[k, p, pl.ds(start, rows)],
                        arrived[stage - 1].at[k, slot, pl.ds(0, rows)],
                        peer(dim, j),
                    )
            elif stage < 7:
                dim = order[6 - stage]
                offset, rows = levels[p][7 - stage]
                target = whole(offset, rows)
                if stage == 4:
                    source = acc.at[k, p, pl.ds(pl.multiple_of(offset, SHARD), rows)]
                else:
                    source = target
                for j in range(1, size[dim]):
                    add(source, target, peer(dim, j))
            else:
                target = whole(0, half // 2)
                add(target, target, sibling)
        return out

    def own_shard(k, p):
        offset, rows = levels[p][3]
        start = k * 2 * half + p * half + core * (half // 2) + offset
        return pltpu.make_async_copy(
            acc.at[k, p, pl.ds(pl.multiple_of(offset, SHARD), rows)],
            summed.at[pl.ds(pl.multiple_of(start, SHARD), rows)],
            local_sem.at[k, p],
        )

    def start_stage(stage, k):
        for copy in copies(stage, k):
            copy.start()
        if stage == 4:
            for p in range(2):
                own_shard(k, p).start()

    def finish_stage(stage, k):
        for copy in copies(stage, k):
            copy.wait()
        if stage == 4:
            for p in range(2):
                own_shard(k, p).wait()
        for p, order in enumerate(orders):
            if stage == 0:
                start = pl.multiple_of(k * 2 * half + p * half + core * (half // 2), SHARD)
                mine = grads[pl.ds(start, half // 2), :].astype(F32)
                acc[k, p] = (mine + arrived_core[k, p].astype(F32)).astype(BF16)
            elif stage < 4:
                dim = order[stage - 1]
                offset, rows = levels[p][stage]
                at = pl.ds(pl.multiple_of(offset, SHARD), rows)
                total = acc[k, p, at, :].astype(F32)
                for j in range(1, size[dim]):
                    if p == 0 or stage == 3:
                        slot = p * (size[dim] - 1) + j - 1 if stage == 3 else j - 1
                    else:
                        slot = size["x" if stage == 1 else "y"] - 1 + j - 1
                    total += arrived[stage - 1][k, slot, :rows, :].astype(F32)
                acc[k, p, at, :] = total.astype(BF16)

    def tick(t, _):
        for stage in range(STAGES, -1, -1):
            k = t - stage

            def go():
                if stage > 0:
                    finish_stage(stage - 1, k)
                if stage < STAGES:
                    start_stage(stage, k)

            pl.when(jnp.logical_and(k >= 0, k < chunks))(go)
        return 0

    sums_dims = ("core", "x", "y", "z")

    def sums_copies(level):
        dim = sums_dims[level]
        if dim == "core":
            targets = [(sibling, 2, core)]
        else:
            targets = [(peer(dim, j), size[dim], place[dim]) for j in range(1, size[dim])]
        return [
            pltpu.make_async_remote_copy(
                sums_at.at[level, mine],
                sums_at.at[level, mine],
                sums_send.at[level, n],
                sums_recv.at[level, n],
                device,
                MESH,
            )
            for n, (device, _, mine) in enumerate(targets)
        ]

    def sums_start(level, value):
        dim = sums_dims[level]
        sums_at[level, core if dim == "core" else place[dim]] = value
        for copy in sums_copies(level):
            copy.start()

    def sums_finish(level):
        for copy in sums_copies(level):
            copy.wait()
        dim = sums_dims[level]
        total = sums_at[level, 0]
        for i in range(1, 2 if dim == "core" else size[dim]):
            total += sums_at[level, i]
        return total

    my_view = view[0]

    def part_for(offset):
        slot = lax.rem(offset + VIEWS, VIEWS) - 1
        at = my_view + offset
        valid = jnp.logical_and(at >= 0, at < VIEWS)
        return jnp.where(valid, parts[slot], jnp.zeros((), BF16))

    def swap(n):
        return pltpu.make_async_remote_copy(
            swap_out.at[n], swap_in.at[n], swap_sem.at[0, n], swap_sem.at[1, n], sibling, MESH
        )

    far = (2 + 0 * step, -2 + 0 * step, 4 * step, -4 * step)

    def far_copy(n):
        return pltpu.make_async_remote_copy(
            far_out.at[n], far_in.at[n], far_sem.at[0, n], far_sem.at[1, n], along(far[n]), MESH
        )

    sums_start(0, sums[...])
    for n, offset in enumerate((step, 2 + step, -2 + step, -3 * step)):
        swap_out[n] = part_for(offset)
        swap(n).start()
    lax.fori_loop(0, 1, tick, 0)
    far_out[3] = part_for(far[3])
    far_copy(3).start()
    sums_start(1, sums_finish(0))
    for n in range(3):
        swap(n + 1).wait()
        far_out[n] = (part_for(far[n]).astype(F32) + swap_in[n + 1].astype(F32)).astype(BF16)
        far_copy(n).start()
    lax.fori_loop(1, 2, tick, 0)
    sums_start(2, sums_finish(1))
    lax.fori_loop(2, 3, tick, 0)
    sums_start(3, sums_finish(2))
    lax.fori_loop(3, chunks + STAGES, tick, 0)
    sums_out[...] = sums_finish(3)
    swap(0).wait()
    for n in range(4):
        far_copy(n).wait()
    total = own_part[...] + swap_in[0].astype(F32)
    for n in range(4):
        total += far_in[n].astype(F32)
    unit, scale = normalise(tokens[:USED, :].astype(F32))
    gain = gain_attn[...].astype(F32)
    grad_tokens[:USED, :] = residual_grad[...] + norm_backward(total, unit, scale, gain)
    grad_tokens[USED:, :] = cotangent[USED:, :].astype(F32)


def reduce(count, groups, *args):
    depth = count // 4
    half = 2 * 2 * groups * depth * SHARD
    chunks = -(-GRAD_ROWS // (2 * half))
    shape = jax.ShapeDtypeStruct
    dma = pltpu.SemaphoreType.DMA
    most = 2 * max(groups, depth)
    levels = max(groups, depth)
    first = max(half // 4, half // 2 // groups)
    scratch = [
        VMEM((chunks, 2, half // 2, D), BF16),
        VMEM((chunks, 2, half // 2, D), BF16),
        VMEM((chunks, groups, first, D), BF16),
        VMEM((chunks, groups, half // 4 // groups, D), BF16),
        VMEM((chunks, 2 * (depth - 1), SHARD, D), BF16),
        dma((chunks, STAGES, most)),
        dma((chunks, STAGES, most)),
        dma((chunks, 2)),
        VMEM((4, levels, SUMS, D), F32),
        dma((4, levels)),
        dma((4, levels)),
        VMEM((4, USED, D), BF16),
        VMEM((4, USED, D), BF16),
        VMEM((4, USED, D), BF16),
        VMEM((4, USED, D), BF16),
        dma((2, 4)),
        dma((2, 4)),
    ]
    return pl.pallas_call(
        functools.partial(reduce_kernel, count, groups, chunks),
        out_shape=(
            shape((ROWS, D), F32),
            shape((chunks * 2 * half, D), BF16),
            shape((SUMS, D), F32),
        ),
        in_specs=[IN_SMEM] + [IN_VMEM] * (len(args) - 1),
        out_specs=[IN_VMEM, ANYWHERE, IN_VMEM],
        scratch_shapes=scratch,
        compiler_params=pltpu.CompilerParams(
            collective_id=1, has_side_effects=True, vmem_limit_bytes=60 * MIB
        ),
        name="reduce",
    )(*args)


def widen_kernel(block, down, up, out, query, keyval):
    b = pl.program_id(0)
    value = block[...].astype(F32)
    blocks = FF // D
    for target, first, last in (
        (down, 0, blocks),
        (up, blocks, 2 * blocks),
        (out, 2 * blocks, 2 * blocks + 1),
        (query, 2 * blocks + 1, 2 * blocks + 2),
        (keyval, 2 * blocks + 2, 2 * blocks + 4),
    ):

        def store(target=target):
            target[...] = value

        pl.when(jnp.logical_and(b >= first, b < last))(store)


def widen(summed):
    blocks = FF // D
    shape = jax.ShapeDtypeStruct

    def at(first, number, by_rows):
        def index(b):
            i = jnp.clip(b - first, 0, number - 1)
            return (i, 0) if by_rows else (0, i)

        return pl.BlockSpec((D, D), index)

    return pl.pallas_call(
        widen_kernel,
        grid=(GRAD_ROWS // D,),
        out_shape=(
            shape((FF, D), F32),
            shape((D, FF), F32),
            shape((D, D), F32),
            shape((D, D), F32),
            shape((D, 2 * D), F32),
        ),
        in_specs=[pl.BlockSpec((D, D), lambda b: (b, 0))],
        out_specs=[
            at(0, blocks, True),
            at(blocks, blocks, False),
            at(2 * blocks, 1, True),
            at(2 * blocks + 1, 1, True),
            at(2 * blocks + 2, 2, False),
        ],
        name="widen",
    )(summed)


def on_device(count, groups, tokens, counts, slot_item, slot_view, keyframe, *rest):
    weights, cotangent = rest[:-1], rest[-1]
    rows = tokens.reshape(ROWS, D)
    item = slot_item.reshape(())
    filled = (counts.reshape(()) > 0) & (keyframe.reshape(()) == 1) & (item >= 0)
    label = jnp.where(filled, item, -1).astype(BF16)
    block = jnp.concatenate([rows[:USED], jnp.broadcast_to(label, (SENT - USED, D))])
    window = gather_window(block, count)
    weights = tuple(w.reshape(1, -1) if w.ndim == 1 else w for w in weights)
    cot = cotangent.reshape(ROWS, D)
    view = slot_view.reshape(1)
    chunk = 2 * count * groups * SHARD
    grad_rows = -(-GRAD_ROWS // chunk) * chunk
    block_output, residual_grad, grads, sums, parts, own_part = compute(
        grad_rows, view, filled.astype(jnp.int32).reshape(1), window, cot, *weights
    )
    block_output = jnp.concatenate([block_output[:USED], rows[USED:]])
    grad_tokens, summed, sums = reduce(
        count, groups, view, parts, own_part, residual_grad, rows, cot, weights[7], grads, sums
    )
    down, up, out, query, keyval = widen(summed)
    return (
        block_output.reshape(tokens.shape),
        grad_tokens.reshape(tokens.shape),
        query,
        keyval,
        out,
        up,
        sums[:4].reshape(-1),
        down,
        sums[4],
        sums[7],
        sums[8],
        sums[5],
        sums[6],
    )


def solution(mesh):
    count = mesh.shape["view"]
    groups = mesh.shape["dp"]
    slots = P("dp", "view", None)
    rows = P("dp", "view", None, None, None)
    in_specs = (rows, P("dp", "view"), slots, slots, slots) + (P(),) * 11 + (rows,)
    out_specs = (rows, rows) + (P(),) * 11
    return jax.shard_map(
        functools.partial(on_device, count, groups),
        mesh=mesh,
        in_specs=in_specs,
        out_specs=out_specs,
        check_vma=False,
    )
```

```python
import functools

import jax
import jax.numpy as jnp
from jax import lax
from jax.experimental import pallas as pl
from jax.experimental.pallas import tpu as pltpu
from jax.sharding import PartitionSpec as P

D = 512
HEADS = 8
HEAD_DIM = 64
PAIRS = HEADS // 2
PAIR = 2 * HEAD_DIM
VIEWS = 5
PATCHES = 400
LANG = 77
ROWS = 512
USED = 480
TAIL = USED - PATCHES
SENT = 496
KEYS = VIEWS * PATCHES + TAIL
KEYS_PADDED = 2176
FF = 2048
FF_BLOCK = 512
NEGATIVE = -1e30
EPSILON = 1e-5
GRAD_ROWS = 2 * FF + 4 * D
SUMS = 16
SHARD = 16
STAGES = 8
SKEW = 2

BF16 = jnp.bfloat16
F32 = jnp.float32
MESH = pl.DeviceIdType.MESH
NN = (((1,), (0,)), ((), ()))
NT = (((1,), (1,)), ((), ()))
TN = (((0,), (0,)), ((), ()))
TT = (((0,), (1,)), ((), ()))
MIB = 2**20

VMEM = pltpu.VMEM
IN_VMEM = pl.BlockSpec(memory_space=pltpu.VMEM)
IN_SMEM = pl.BlockSpec(memory_space=pltpu.SMEM)
ANYWHERE = pl.BlockSpec(memory_space=pl.ANY)


def dot(left, right, dims):
    return lax.dot_general(left, right, dims, preferred_element_type=F32)


def normalise(values):
    average = jnp.mean(values, -1, keepdims=True)
    centered = values - average
    variance = jnp.mean(centered * centered, -1, keepdims=True)
    scale = lax.rsqrt(variance + EPSILON)
    return centered * scale, scale


def norm_backward(grad, unit, scale, gain):
    grad = grad * gain
    first = jnp.mean(grad, -1, keepdims=True)
    second = jnp.mean(grad * unit, -1, keepdims=True)
    return scale * (grad - first - unit * second)


def greet(others):
    barrier = pltpu.get_barrier_semaphore()
    for other in others:
        pl.semaphore_signal(barrier, inc=1, device_id=other, device_id_type=MESH)
    pl.semaphore_wait(barrier, len(others))


def gather_kernel(count, block, window, own_sem, send_sem, recv_sem, pass_sem, given_sem):
    me = lax.axis_index("view")
    step = 1 - 2 * lax.rem(me, 2)

    def at(offset):
        return {"view": lax.rem(me + offset + count, count)}

    far = (4, -4, 2, -2)
    greet([at(offset) for offset in far] + [at(step)])
    own = pltpu.make_async_copy(block, window.at[4], own_sem)
    own.start()

    def to(k, offset):
        return pltpu.make_async_remote_copy(
            block, window.at[4 - offset], send_sem.at[k], recv_sem.at[k], at(offset), MESH
        )

    def across(k, offset, source):
        return pltpu.make_async_remote_copy(
            source,
            window.at[4 + offset - step],
            pass_sem.at[k],
            given_sem.at[k],
            at(step),
            MESH,
        )

    sends = [to(k, offset) for k, offset in enumerate(far)]
    for copy in sends:
        copy.start()
    passes = [across(0, 0, block)]
    passes[0].start()
    for k, offset in ((2, -2), (3, 2)):
        sends[k].wait_recv()
        copy = across(k - 1, offset, window.at[4 + offset])
        copy.start()
        passes.append(copy)
    even = lax.rem(me, 2) == 0
    for k in (0, 1):
        sends[k].wait_recv()
    copy = across(3, 4 * step, window.at[4 + 4 * step])
    copy.start()
    passes.append(copy)
    for copy in passes:
        copy.wait()
    for copy in sends:
        copy.wait_send()
    own.wait()


def gather_window(block, count):
    return pl.pallas_call(
        functools.partial(gather_kernel, count),
        out_shape=jax.ShapeDtypeStruct((2 * VIEWS - 1, SENT, D), BF16),
        in_specs=[ANYWHERE],
        out_specs=ANYWHERE,
        scratch_shapes=[pltpu.SemaphoreType.DMA] + [pltpu.SemaphoreType.DMA((4,))] * 4,
        compiler_params=pltpu.CompilerParams(collective_id=0, has_side_effects=True),
        name="gather_window",
    )(block)


def main_kernel(
    count,
    groups,
    chunks,
    part_rows,
    view,
    filled,
    window,
    tokens,
    cotangent,
    w_query,
    w_keyval,
    w_output,
    w_up,
    w_down,
    vectors,
    block_output,
    grad_tokens,
    summed,
    sums_out,
    spilled,
    normed_all,
    query_norm,
    key_bias,
    keyval,
    query,
    weights,
    mixed,
    mixed_full,
    inverse,
    keyval_grad,
    mixed_grad,
    normed_mlp,
    branch_grad,
    residual,
    branch,
    mlp_back,
    labels,
    arena,
    grads,
    arrived_core,
    arrived_first,
    arrived_second,
    arrived_last,
    far_in,
    sums_at,
    window_sem,
    weight_sem,
    spill_sem,
    send_sem,
    recv_sem,
    local_sem,
    sums_send,
    sums_recv,
    swap_sem,
    far_sem,
):
    me = lax.axis_index("view")
    group = lax.axis_index("dp")
    depth = count // 4
    core = lax.rem(me, 2)
    step = 1 - 2 * core
    place = {"x": lax.rem(me // 2, 2), "y": group, "z": me // 4}
    size = {"x": 2, "y": groups, "z": depth}
    orders = (("x", "y", "z"), ("y", "x", "z"))[-(2 if part_rows < D else 1) :]
    chunk_rows = len(orders) * part_rows
    fine = chunk_rows == D
    arrived = (arrived_first, arrived_second, arrived_last)

    def peer(dim, j):
        at = lax.rem(place[dim] + j, size[dim])
        if dim == "x":
            return {"view": me + 2 * (at - place["x"])}
        if dim == "y":
            return {"dp": at}
        return {"view": me + 4 * (at - place["z"])}

    def along(offset):
        return {"view": lax.rem(me + offset + count, count)}

    sibling = {"view": me + step}

    def window_at(n):
        return weights.at[n // 4, :, pl.ds(n % 4 * D, D)]

    def window_copies(n):
        return (
            pltpu.make_async_copy(
                window.at[n, pl.ds(0, USED), :], window_at(n), window_sem.at[0, n]
            ),
            pltpu.make_async_copy(
                window.at[n, pl.ds(USED, SENT - USED), :], labels.at[n], window_sem.at[1, n]
            ),
        )

    def weight_copies():
        blocks = FF // D
        return [
            pltpu.make_async_copy(
                w_up.at[:, pl.ds(c * D, D)], arena.at[c], weight_sem.at[c]
            )
            for c in range(blocks)
        ] + [
            pltpu.make_async_copy(
                w_down.at[pl.ds(c * D, D), :], arena.at[blocks + c], weight_sem.at[blocks + c]
            )
            for c in range(blocks)
        ]

    for n in range(2 * VIEWS - 1):
        for copy in window_copies(n):
            copy.start()
    for copy in weight_copies():
        copy.start()
    peers = [peer(dim, j) for dim in "xyz" for j in range(1, size[dim])]
    greet([sibling] + peers + [along(offset) for offset in (4, -4, 2, -2)])

    levels = []
    for order in orders:
        rows = part_rows
        offset = 0
        level = [(0, rows)]
        for dim in order:
            rows = rows // size[dim]
            offset = offset + place[dim] * rows
            level.append((offset, rows))
        levels.append(level)
    own_columns = pl.ds(pl.multiple_of(core * (D // 2), D // 2), D // 2)
    other_columns = pl.ds(pl.multiple_of((1 - core) * (D // 2), D // 2), D // 2)

    def slot_of(stage, p, j):
        slot = j - 1
        for order in orders[:p]:
            slot += size[order[stage - 1]] - 1
        return slot

    def rows_of(k, p, offset, rows):
        return pl.ds(pl.multiple_of(k * chunk_rows + p * part_rows + offset, SHARD), rows)

    def copies(stage, k):
        out = []

        def add(source, target, device):
            n = len(out)
            out.append(
                pltpu.make_async_remote_copy(
                    source, target, send_sem.at[k, stage, n], recv_sem.at[k, stage, n], device, MESH
                )
            )

        if stage == 0:
            add(grads.at[rows_of(k, 0, 0, chunk_rows), other_columns], arrived_core.at[k], sibling)
        elif stage == 7:
            whole = summed.at[rows_of(k, 0, 0, chunk_rows), own_columns]
            add(whole, whole, sibling)
        for p, order in enumerate(orders):
            if 0 < stage < 4:
                dim = order[stage - 1]
                offset, _ = levels[p][stage - 1]
                _, rows = levels[p][stage]
                for j in range(1, size[dim]):
                    at = offset + lax.rem(place[dim] + j, size[dim]) * rows
                    add(
                        grads.at[rows_of(k, p, at, rows), own_columns],
                        arrived[stage - 1].at[k, slot_of(stage, p, j), pl.ds(0, rows), :],
                        peer(dim, j),
                    )
            elif 4 <= stage < 7:
                dim = order[6 - stage]
                offset, rows = levels[p][7 - stage]
                at = rows_of(k, p, offset, rows)
                source = grads if stage == 4 else summed
                for j in range(1, size[dim]):
                    add(source.at[at, own_columns], summed.at[at, own_columns], peer(dim, j))
        return out

    def own_shard(k, p):
        at = rows_of(k, p, *levels[p][3])
        return pltpu.make_async_copy(
            grads.at[at, own_columns], summed.at[at, own_columns], local_sem.at[k, p]
        )

    def start_stage(stage, k):
        for copy in copies(stage, k):
            copy.start()
        if stage == 4:
            for p in range(len(orders)):
                own_shard(k, p).start()

    def finish_stage(stage, k):
        for copy in copies(stage, k):
            copy.wait()
        if stage == 4:
            for p in range(len(orders)):
                own_shard(k, p).wait()
        if stage == 0:
            at = rows_of(k, 0, 0, chunk_rows)
            total = grads[at, own_columns].astype(F32) + arrived_core[k].astype(F32)
            grads[at, own_columns] = total.astype(BF16)
        elif stage < 4:
            for p, order in enumerate(orders):
                offset, rows = levels[p][stage]
                at = rows_of(k, p, offset, rows)
                total = grads[at, own_columns].astype(F32)
                for j in range(1, size[order[stage - 1]]):
                    total += arrived[stage - 1][k, slot_of(stage, p, j), :rows, :].astype(F32)
                grads[at, own_columns] = total.astype(BF16)

    blocks = FF // D

    def tick(t):
        for stage in range(STAGES, -1, -1):
            at = t - SKEW * stage
            if fine:
                late = at - (2 * blocks + 1)
                early = jnp.logical_and(at >= 0, at < 2 * blocks)
                valid = jnp.logical_and(late >= 0, late < 2 * PAIRS)
                valid = jnp.logical_or(early, jnp.logical_and(valid, lax.rem(late, 2) == 0))
                k = jnp.where(early, at, 2 * blocks + late // 2)
            else:
                k = at
                valid = jnp.logical_and(at >= 0, at < chunks)

            def go(stage=stage, k=k):
                if stage > 0:
                    finish_stage(stage - 1, k)
                if stage < STAGES:
                    start_stage(stage, k)

            pl.when(valid)(go)

    sums_dims = ("core", "x", "y", "z")

    def sums_copies(level):
        dim = sums_dims[level]
        if dim == "core":
            targets, mine = [sibling], core
        else:
            targets, mine = [peer(dim, j) for j in range(1, size[dim])], place[dim]
        return [
            pltpu.make_async_remote_copy(
                sums_at.at[level, mine],
                sums_at.at[level, mine],
                sums_send.at[level, n],
                sums_recv.at[level, n],
                device,
                MESH,
            )
            for n, device in enumerate(targets)
        ]

    def sums_start(level, value):
        dim = sums_dims[level]
        sums_at[level, core if dim == "core" else place[dim]] = value
        for copy in sums_copies(level):
            copy.start()

    def sums_finish(level):
        for copy in sums_copies(level):
            copy.wait()
        dim = sums_dims[level]
        total = sums_at[level, 0]
        for i in range(1, 2 if dim == "core" else size[dim]):
            total += sums_at[level, i]
        return total

    my_view = view[0]
    my_filled = filled[0]
    gain_a = vectors[5:6, :]
    shift_a = vectors[6:7, :]
    gain_m = vectors[7:8, :]
    shift_m = vectors[8:9, :]

    own_rows = tokens[:USED, :]
    own_unit, _ = normalise(own_rows.astype(F32))
    own_normed = (own_unit * gain_a + shift_a).astype(BF16)
    query_norm[...] = own_normed
    normed_all[:PATCHES, :] = own_normed[:PATCHES, :]
    query[...] = (dot(own_normed, w_query[...], NN).astype(BF16) * HEAD_DIM**-0.5).astype(BF16)
    for n in range(2 * VIEWS - 1):
        for copy in window_copies(n):
            copy.wait()
    my_label = labels[VIEWS - 1, :, :PAIR].astype(F32)

    def bias_of(label):
        match = jnp.logical_and(label == my_label, label >= 0)
        return jnp.where(match, 0.0, NEGATIVE)[:1, :]

    def window_block(n, rows):
        return weights[n // 4, rows, n % 4 * D : (n % 4 + 1) * D]

    key_bias[:PATCHES, :] = jnp.broadcast_to(bias_of(my_label), (PATCHES, PAIR)).astype(BF16)
    language = own_rows[PATCHES:, :]
    language_bias = bias_of(my_label)
    for j in range(1, VIEWS):
        ahead = my_view + j < VIEWS
        block = jnp.where(
            ahead, window_block(4 + j, slice(0, USED)), window_block(j - 1, slice(0, USED))
        )
        label = jnp.where(ahead, labels[4 + j, :, :PAIR], labels[j - 1, :, :PAIR]).astype(F32)
        unit, _ = normalise(block[:PATCHES, :].astype(F32))
        rows = slice(j * PATCHES, (j + 1) * PATCHES)
        normed_all[rows, :] = (unit * gain_a + shift_a).astype(BF16)
        bias = bias_of(label)
        key_bias[rows, :] = jnp.broadcast_to(bias, (PATCHES, PAIR)).astype(BF16)
        holds = lax.rem(my_view + j, VIEWS) == 0
        language = jnp.where(holds, block[PATCHES:, :], language)
        language_bias = jnp.where(holds, bias, language_bias)
    unit, _ = normalise(language.astype(F32))
    normed_all[VIEWS * PATCHES : KEYS, :] = (unit * gain_a + shift_a).astype(BF16)
    index = lax.broadcasted_iota(jnp.int32, (TAIL, PAIR), 0)
    key_bias[VIEWS * PATCHES : KEYS, :] = jnp.where(
        index < LANG, jnp.broadcast_to(language_bias, (TAIL, PAIR)), NEGATIVE
    ).astype(BF16)
    normed_all[KEYS:, :] = jnp.zeros((KEYS_PADDED - KEYS, D), BF16)
    key_bias[KEYS:, :] = jnp.full((KEYS_PADDED - KEYS, PAIR), NEGATIVE, BF16)
    for c in range(2):
        columns = slice(c * D, (c + 1) * D)
        keyval[:, columns] = dot(normed_all[...], w_keyval[:, columns], NN).astype(BF16)

    lane = lax.broadcasted_iota(jnp.int32, (1, PAIR), 1)
    low_half = lane < HEAD_DIM

    def half_of(half, first, second):
        return jnp.where(low_half, first, second) if half == 0 else jnp.where(low_half, second, first)

    def head_keys(p, half):
        pair = keyval[:, pl.ds(pl.multiple_of(p * PAIR, PAIR), PAIR)]
        return half_of(half, pair, key_bias[...])

    def head_values(p, half):
        pair = keyval[:, pl.ds(pl.multiple_of(D + p * PAIR, PAIR), PAIR)]
        return half_of(half, pair, jnp.ones((), BF16))

    def spill(p, half):
        return pltpu.make_async_copy(
            weights.at[2 * lax.rem(p, 2) + half], spilled.at[2 * p + half], spill_sem.at[lax.rem(p, 2), half]
        )

    def unspill(p, half):
        return pltpu.make_async_copy(
            spilled.at[2 * p + half], weights.at[2 * lax.rem(p, 2) + half], spill_sem.at[lax.rem(p, 2), half]
        )

    def forward_pair(p, _):
        columns = pl.ds(pl.multiple_of(p * PAIR, PAIR), PAIR)
        pair = query[:, columns]
        outs = []
        totals = []

        def settle():
            for half in range(2):
                spill(p - 1, half).wait()

        pl.when(jnp.logical_and(p >= 1, p < 3))(settle)
        for half in range(2):
            one = (lane == HEAD_DIM * (1 - half)).astype(BF16)
            scores = dot(half_of(half, pair, one), head_keys(p, half), NT)
            top = jnp.max(scores, -1, keepdims=True)
            weight = jnp.exp(scores - top).astype(BF16)
            weights[2 * lax.rem(p, 2) + half] = weight
            out = dot(weight, head_values(p, half), NN)
            outs.append(out)
            totals.append(pltpu.roll(out, HEAD_DIM, 1))
        inv = 1.0 / jnp.where(low_half, totals[0], totals[1])
        full = jnp.where(low_half, outs[0], outs[1]) * inv
        inverse[:, columns] = inv
        mixed_full[:, columns] = full
        mixed[:, columns] = full.astype(BF16)

        def save():
            for half in range(2):
                spill(p, half).start()

        pl.when(p < 2)(save)
        return 0

    lax.fori_loop(0, PAIRS, forward_pair, 0)

    row = lax.broadcasted_iota(jnp.int32, (USED, PAIR), 0)
    has_language = (my_view == 0).astype(jnp.int32)
    live_rows = my_filled * (PATCHES + LANG * has_language)
    live = (row < live_rows).astype(F32)[:, :1]
    res = tokens[:USED, :].astype(F32) + live * dot(mixed[...], w_output[...], NN)
    residual[...] = res
    unit_m, scale_m = normalise(res)
    normed_mlp[...] = (unit_m * gain_m + shift_m).astype(BF16)
    upstream = cotangent[:USED, :].astype(F32)
    branch_grad[...] = (live * upstream).astype(BF16)
    branch[...] = jnp.zeros((USED, D), F32)
    mlp_back[...] = jnp.zeros((USED, D), F32)
    for copy in weight_copies():
        copy.wait()

    def feed_forward(c, _):
        up = arena[c]
        down = arena[blocks + c]
        before = dot(normed_mlp[...], up, NN) + vectors[pl.ds(c, 1), :]
        chance = 0.5 + 0.5 * lax.erf(before * 0.5**0.5)
        density = jnp.exp(-0.5 * before * before) * 0.3989422804014327
        activated = (before * chance).astype(BF16)
        slope = chance + before * density
        start = pl.multiple_of(2 * c * D, D)
        grads[pl.ds(start, D), :] = dot(activated, branch_grad[...], TN).astype(BF16)
        branch[...] += dot(activated, down, NN)
        before_full = dot(branch_grad[...], down, NT) * slope
        before_grad = before_full.astype(BF16)
        sums_out[pl.ds(c, 1), :] = jnp.sum(before_grad.astype(F32), 0, keepdims=True)
        grads[pl.ds(start + D, D), :] = dot(normed_mlp[...], before_grad, TN).astype(BF16)
        mlp_back[...] += dot(before_grad, up, NT)
        if fine:
            tick(2 * c)
            tick(2 * c + 1)
        return 0

    lax.fori_loop(0, blocks, feed_forward, 0)
    block_output[:USED, :] = (residual[...] + live * (branch[...] + vectors[4:5, :])).astype(BF16)
    block_output[USED:, :] = tokens[USED:, :]
    unit_m, scale_m = normalise(residual[...])
    back = mlp_back[...]
    sums_out[4:5, :] = jnp.sum(branch_grad[...].astype(F32), 0, keepdims=True)
    sums_out[5:6, :] = jnp.sum(back * unit_m, 0, keepdims=True)
    sums_out[6:7, :] = jnp.sum(back, 0, keepdims=True)
    res_grad = upstream + norm_backward(back, unit_m, scale_m, gain_m)
    grad_tokens[:USED, :] = res_grad
    grad_tokens[USED:, :] = cotangent[USED:, :].astype(F32)
    attended_grad = (live * res_grad).astype(BF16)
    base = 2 * FF
    out_grad = dot(mixed[...], attended_grad, TN).astype(BF16)
    for i in range(PAIRS):
        grads[base + i * D : base + i * D + PAIR, :] = out_grad[i * PAIR : (i + 1) * PAIR, :]
    mixed_grad[...] = dot(attended_grad, w_output[...], NT).astype(BF16)

    branch[...] = jnp.zeros((USED, D), F32)

    def backward_pair(i, _):
        p = PAIRS - 1 - i
        columns = pl.ds(pl.multiple_of(p * PAIR, PAIR), PAIR)
        grad = mixed_grad[:, columns].astype(F32)
        inv = inverse[:, columns]
        scaled = grad * inv
        product = scaled * mixed_full[:, columns]
        scaled_low = scaled.astype(BF16)
        scaled_t = scaled.T.astype(BF16)
        query_t = query[:, columns].astype(F32).T.astype(BF16)
        query_parts = []
        start = pl.multiple_of(p * PAIR, PAIR)

        def settle():
            for half in range(2):
                unspill(p, half).wait()

        pl.when(p < 2)(settle)
        for half in range(2):
            here = low_half if half == 0 else jnp.logical_not(low_half)
            dots = -jnp.sum(jnp.where(here, product, 0.0), -1, keepdims=True)
            dots_high = dots.astype(BF16)
            dots_low = (dots - dots_high.astype(F32)).astype(BF16)
            other = HEAD_DIM * (1 - half)
            rest = jnp.where(
                lane == other, dots_high, jnp.where(lane == other + 1, dots_low, jnp.zeros((), BF16))
            )
            weight = weights[2 * lax.rem(p, 2) + half]
            slope = dot(half_of(half, scaled_low, rest), head_values(p, half), NT)
            score_grad = weight * slope.astype(BF16)
            query_parts.append(dot(score_grad, head_keys(p, half), NN))
            rows = slice(half * HEAD_DIM, (half + 1) * HEAD_DIM)
            at = start + half * HEAD_DIM
            keyval_grad[pl.ds(at, HEAD_DIM), :] = dot(query_t[rows, :], score_grad, NN).astype(BF16)
            keyval_grad[pl.ds(D + at, HEAD_DIM), :] = dot(scaled_t[rows, :], weight, NN).astype(BF16)
            if fine and half == 0:
                tick(2 * blocks + 2 * i)

        def load():
            for half in range(2):
                unspill(p - 2, half).start()

        pl.when(p >= 2)(load)
        part = jnp.where(low_half, query_parts[0], query_parts[1]) * HEAD_DIM**-0.5
        query_grad = part.astype(BF16)
        at = pl.multiple_of(base + i * D, D)
        grads[pl.ds(at + PAIR, PAIR), :] = dot(query_grad, query_norm[...], TN).astype(BF16)
        for c in range(2):
            of_pair = keyval_grad[pl.ds(c * D + start, PAIR), :]
            grads[pl.ds(at + (2 + c) * PAIR, PAIR), :] = dot(of_pair, normed_all[...], NN).astype(
                BF16
            )
        branch[...] += dot(query_grad, w_query[:, columns], NT)
        if fine:
            tick(2 * blocks + 2 * i + 1)
        return 0

    lax.fori_loop(0, PAIRS, backward_pair, 0)

    from_query = branch[...]
    normed = query_norm[...].astype(F32)
    shift_sum = jnp.sum(from_query, 0, keepdims=True)
    gain_sum = jnp.sum(from_query * normed, 0, keepdims=True)

    def parts_at(j):
        return weights.at[0, :, (j - 1) * D : j * D]

    for j in range(VIEWS + 1):
        rows = slice(j * PATCHES, min((j + 1) * PATCHES, KEYS))
        piece = dot(keyval_grad[:, rows], w_keyval[...], TT)
        normed = normed_all[rows, :].astype(F32)
        shift_sum += jnp.sum(piece, 0, keepdims=True)
        gain_sum += jnp.sum(piece * normed, 0, keepdims=True)
        if j == 0:
            branch[:PATCHES, :] += piece
        elif j < VIEWS:
            parts_at(j)[:PATCHES, :] = piece.astype(BF16)
        else:
            branch[PATCHES:, :] += jnp.where(my_view == 0, piece, 0.0)
            for i in range(1, VIEWS):
                holds = lax.rem(my_view + i, VIEWS) == 0
                parts_at(i)[PATCHES:, :] = jnp.where(holds, piece, 0.0).astype(BF16)
    sums_out[7:8, :] = (gain_sum - shift_a * shift_sum) / gain_a
    sums_out[8:9, :] = shift_sum
    sums_out[9:, :] = jnp.zeros((SUMS - 9, D), F32)

    def part_for(offset):
        slot = lax.rem(offset + VIEWS, VIEWS) - 1
        at = my_view + offset
        valid = jnp.logical_and(at >= 0, at < VIEWS)
        value = jnp.zeros((USED, D), BF16)
        for n in range(VIEWS - 1):
            value = jnp.where(jnp.logical_and(valid, slot == n), parts_at(n + 1)[...], value)
        return value

    def swap(n):
        return pltpu.make_async_remote_copy(
            arena.at[n, pl.ds(0, USED), :],
            arena.at[4 + n, pl.ds(0, USED), :],
            swap_sem.at[0, n],
            swap_sem.at[1, n],
            sibling,
            MESH,
        )

    far = (2 + 0 * step, -2 + 0 * step, 4 * step, -4 * step)

    def far_copy(n):
        return pltpu.make_async_remote_copy(
            arena.at[(n + 1) % 4, pl.ds(0, USED), :],
            far_in.at[n],
            far_sem.at[0, n],
            far_sem.at[1, n],
            along(far[n]),
            MESH,
        )

    ticks = 2 * blocks + 2 * PAIRS if fine else 0
    last = ticks + STAGES * SKEW if fine else chunks + STAGES * SKEW

    def run_ticks(first, end):
        def body(t, _):
            tick(t)
            return 0

        lax.fori_loop(first, end, body, 0)

    if not fine:
        run_ticks(0, SKEW + 1)
        ticks = SKEW + 1
    sums_start(0, sums_out[...])
    for n, offset in enumerate((step, 2 + step, -2 + step, -3 * step)):
        arena[n, :USED, :] = part_for(offset)
        swap(n).start()
    run_ticks(ticks, ticks + 1)
    sums_start(1, sums_finish(0))
    swap(0).wait()
    arena[0, :USED, :] = part_for(far[3])
    far_copy(3).start()
    for n in range(3):
        swap(n + 1).wait()
        both = part_for(far[n]).astype(F32) + arena[5 + n, :USED, :].astype(F32)
        arena[n + 1, :USED, :] = both.astype(BF16)
        far_copy(n).start()
    run_ticks(ticks + 1, ticks + 2)
    sums_start(2, sums_finish(1))
    run_ticks(ticks + 2, ticks + 4)
    sums_start(3, sums_finish(2))
    run_ticks(ticks + 4, last)
    sums_out[...] = sums_finish(3)
    total = branch[...] + arena[4, :USED, :].astype(F32)
    for n in range(4):
        far_copy(n).wait()
        total += far_in[n].astype(F32)
    unit, scale = normalise(tokens[:USED, :].astype(F32))
    grad_tokens[:USED, :] += norm_backward(total, unit, scale, gain_a)


def main(count, groups, *args):
    depth = count // 4
    part_rows = 2 * groups * depth * SHARD
    parts = 2 if part_rows < D else 1
    chunk_rows = parts * part_rows
    chunks = -(-GRAD_ROWS // chunk_rows)
    shape = jax.ShapeDtypeStruct
    dma = pltpu.SemaphoreType.DMA
    wide = max(groups, depth)
    half = D // 2
    orders = ((2, groups, depth), (groups, 2, depth))[-parts:]
    slots = [sum(order[stage] - 1 for order in orders) for stage in range(3)]
    left = [part_rows // order[0] for order in orders]
    first = max(left)
    second = max(rows // order[1] for rows, order in zip(left, orders))
    scratch = [
        VMEM((KEYS_PADDED, D), BF16),
        VMEM((USED, D), BF16),
        VMEM((KEYS_PADDED, PAIR), BF16),
        VMEM((KEYS_PADDED, 2 * D), BF16),
        VMEM((USED, D), BF16),
        VMEM((4, USED, KEYS_PADDED), BF16),
        VMEM((USED, D), BF16),
        VMEM((USED, D), F32),
        VMEM((USED, D), F32),
        VMEM((2 * D, KEYS_PADDED), BF16),
        VMEM((USED, D), BF16),
        VMEM((USED, D), BF16),
        VMEM((USED, D), BF16),
        VMEM((USED, D), F32),
        VMEM((USED, D), F32),
        VMEM((USED, D), F32),
        VMEM((2 * VIEWS - 1, SENT - USED, D), BF16),
        VMEM((2 * FF // D, D, D), BF16),
        VMEM((chunks * chunk_rows, D), BF16),
        VMEM((chunks, chunk_rows, half), BF16),
        VMEM((chunks, slots[0], first, half), BF16),
        VMEM((chunks, slots[1], second, half), BF16),
        VMEM((chunks, slots[2], SHARD, half), BF16),
        VMEM((4, USED, D), BF16),
        VMEM((4, wide, SUMS, D), F32),
        dma((2, 2 * VIEWS - 1)),
        dma((2 * FF // D,)),
        dma((2, 2)),
        dma((chunks, STAGES, 2 * wide)),
        dma((chunks, STAGES, 2 * wide)),
        dma((chunks, 2)),
        dma((4, wide)),
        dma((4, wide)),
        dma((2, 4)),
        dma((2, 4)),
    ]
    return pl.pallas_call(
        functools.partial(main_kernel, count, groups, chunks, part_rows),
        out_shape=(
            shape((ROWS, D), BF16),
            shape((ROWS, D), F32),
            shape((chunks * chunk_rows, D), BF16),
            shape((SUMS, D), F32),
            shape((4, USED, KEYS_PADDED), BF16),
        ),
        in_specs=[IN_SMEM] * 2 + [ANYWHERE] + [IN_VMEM] * 5 + [ANYWHERE] * 2 + [IN_VMEM],
        out_specs=[IN_VMEM, IN_VMEM, ANYWHERE, IN_VMEM, ANYWHERE],
        scratch_shapes=scratch,
        compiler_params=pltpu.CompilerParams(
            collective_id=1, has_side_effects=True, vmem_limit_bytes=63 * MIB
        ),
        name="main",
    )(*args)


def widen_kernel(block, down, up, out, query, keyval):
    b = pl.program_id(0)
    blocks = FF // D

    def store_rows():
        down[...] = block[...].astype(F32)

    def store_columns():
        up[...] = block[...].astype(F32)

    def store_pair():
        out[...] = block[:PAIR, :].astype(F32)
        query[...] = block[PAIR : 2 * PAIR, :].astype(F32).T
        keyval[...] = block[2 * PAIR : 3 * PAIR, :].astype(F32).T

    def store_values():
        keyval[...] = block[3 * PAIR :, :].astype(F32).T

    early = b < 2 * blocks
    pl.when(jnp.logical_and(early, lax.rem(b, 2) == 0))(store_rows)
    pl.when(jnp.logical_and(early, lax.rem(b, 2) == 1))(store_columns)
    pl.when(jnp.logical_and(b >= 2 * blocks, b < 2 * blocks + PAIRS))(store_pair)
    pl.when(b >= 2 * blocks + PAIRS)(store_values)


def widen(summed):
    blocks = FF // D
    late = 2 * blocks + PAIRS
    shape = jax.ShapeDtypeStruct

    def pair(b):
        return PAIRS - 1 - jnp.clip(b - 2 * blocks, 0, PAIRS - 1)

    def keyval_column(b):
        return jnp.where(b < late, pair(b), 2 * PAIRS - 1 - (b - late))

    return pl.pallas_call(
        widen_kernel,
        grid=(late + PAIRS,),
        out_shape=(
            shape((FF, D), F32),
            shape((D, FF), F32),
            shape((D, D), F32),
            shape((D, D), F32),
            shape((D, 2 * D), F32),
        ),
        in_specs=[pl.BlockSpec((D, D), lambda b: (jnp.where(b < late, b, b - PAIRS), 0))],
        out_specs=[
            pl.BlockSpec((D, D), lambda b: (jnp.clip(b // 2, 0, blocks - 1), 0)),
            pl.BlockSpec((D, D), lambda b: (0, jnp.clip(b // 2, 0, blocks - 1))),
            pl.BlockSpec((PAIR, D), lambda b: (jnp.clip(b - 2 * blocks, 0, PAIRS - 1), 0)),
            pl.BlockSpec((D, PAIR), lambda b: (0, pair(b))),
            pl.BlockSpec((D, PAIR), lambda b: (0, keyval_column(b))),
        ],
        name="widen",
    )(summed)


def on_device(
    count,
    groups,
    tokens,
    counts,
    slot_item,
    slot_view,
    keyframe,
    w_query,
    w_keyval,
    w_output,
    w_up,
    bias_up,
    w_down,
    bias_down,
    gain_attn,
    shift_attn,
    gain_mlp,
    shift_mlp,
    cotangent,
):
    rows = tokens.reshape(ROWS, D)
    item = slot_item.reshape(())
    filled = (counts.reshape(()) > 0) & (keyframe.reshape(()) == 1) & (item >= 0)
    label = jnp.where(filled, item, -1).astype(BF16)
    block = jnp.concatenate([rows[:USED], jnp.broadcast_to(label, (SENT - USED, D))])
    window = gather_window(block, count)
    vectors = jnp.concatenate(
        [bias_up, bias_down, gain_attn, shift_attn, gain_mlp, shift_mlp, jnp.zeros((7 * D,), BF16)]
    )
    vectors = vectors.astype(F32).reshape(SUMS, D)
    block_output, grad_tokens, summed, sums, _ = main(
        count,
        groups,
        slot_view.reshape(1),
        filled.astype(jnp.int32).reshape(1),
        window,
        rows,
        cotangent.reshape(ROWS, D),
        w_query,
        w_keyval,
        w_output,
        w_up,
        w_down,
        vectors,
    )
    down, up, out, query, keyval = widen(summed)
    return (
        block_output.reshape(tokens.shape),
        grad_tokens.reshape(tokens.shape),
        query,
        keyval,
        out,
        up,
        sums[:4].reshape(-1),
        down,
        sums[4],
        sums[7],
        sums[8],
        sums[5],
        sums[6],
    )


def solution(mesh):
    count = mesh.shape["view"]
    groups = mesh.shape["dp"]
    slots = P("dp", "view", None)
    rows = P("dp", "view", None, None, None)
    in_specs = (rows, P("dp", "view"), slots, slots, slots) + (P(),) * 11 + (rows,)
    out_specs = (rows, rows) + (P(),) * 11
    return jax.shard_map(
        functools.partial(on_device, count, groups),
        mesh=mesh,
        in_specs=in_specs,
        out_specs=out_specs,
        check_vma=False,
    )
```

```python
import functools

import jax
import jax.numpy as jnp
from jax import lax
from jax.experimental import pallas as pl
from jax.experimental.pallas import tpu as pltpu
from jax.sharding import PartitionSpec as P

D = 512
HEADS = 8
HEAD_DIM = 64
PAIRS = HEADS // 2
PAIR = 2 * HEAD_DIM
VIEWS = 5
PATCHES = 400
LANG = 77
ROWS = 512
USED = 480
TAIL = USED - PATCHES
SENT = 496
KEYS = VIEWS * PATCHES + TAIL
KEYS_PADDED = 2176
FF = 2048
FF_BLOCK = 512
NEGATIVE = -1e30
EPSILON = 1e-5
GRAD_ROWS = 2 * FF + 4 * D
SUMS = 16
SHARD = 16
STAGES = 8
SKEW = 2
IN_FLIGHT = 4
PIECES = ((0, 128), (128, 128), (256, 128), (384, 112))

BF16 = jnp.bfloat16
F32 = jnp.float32
MESH = pl.DeviceIdType.MESH
NN = (((1,), (0,)), ((), ()))
NT = (((1,), (1,)), ((), ()))
TN = (((0,), (0,)), ((), ()))
TT = (((0,), (1,)), ((), ()))
MIB = 2**20

VMEM = pltpu.VMEM
IN_VMEM = pl.BlockSpec(memory_space=pltpu.VMEM)
IN_SMEM = pl.BlockSpec(memory_space=pltpu.SMEM)
ANYWHERE = pl.BlockSpec(memory_space=pl.ANY)


def dot(left, right, dims):
    return lax.dot_general(left, right, dims, preferred_element_type=F32)


def normalise(values):
    average = jnp.mean(values, -1, keepdims=True)
    centered = values - average
    variance = jnp.mean(centered * centered, -1, keepdims=True)
    scale = lax.rsqrt(variance + EPSILON)
    return centered * scale, scale


def norm_backward(grad, unit, scale, gain):
    grad = grad * gain
    first = jnp.mean(grad, -1, keepdims=True)
    second = jnp.mean(grad * unit, -1, keepdims=True)
    return scale * (grad - first - unit * second)


def greet(others):
    barrier = pltpu.get_barrier_semaphore()
    for other in others:
        pl.semaphore_signal(barrier, inc=1, device_id=other, device_id_type=MESH)
    pl.semaphore_wait(barrier, len(others))


def main_kernel(
    count,
    groups,
    chunks,
    part_rows,
    counts,
    slot_item,
    slot_view,
    keyframe,
    tokens,
    cotangent,
    w_query,
    w_keyval,
    w_output,
    bias_up,
    bias_down,
    gain_attn,
    shift_attn,
    gain_mlp,
    shift_mlp,
    w_up,
    w_down,
    block_output,
    grad_tokens,
    summed,
    sums_out,
    spilled,
    normed_all,
    query_norm,
    key_bias,
    keyval,
    query,
    weights,
    mixed,
    mixed_full,
    inverse,
    keyval_grad,
    mixed_grad,
    normed_mlp,
    branch_grad,
    residual,
    branch,
    mlp_back,
    sent,
    vectors,
    arena,
    grads,
    arrived_core,
    arrived_first,
    arrived_second,
    arrived_last,
    far_in,
    sums_at,
    there_sem,
    here_sem,
    weight_sem,
    spill_sem,
    send_sem,
    recv_sem,
    local_sem,
    sums_send,
    sums_recv,
    swap_sem,
    far_sem,
):
    me = lax.axis_index("view")
    group = lax.axis_index("dp")
    depth = count // 4
    core = lax.rem(me, 2)
    step = 1 - 2 * core
    place = {"x": lax.rem(me // 2, 2), "y": group, "z": me // 4}
    size = {"x": 2, "y": groups, "z": depth}
    orders = (("x", "y", "z"), ("y", "x", "z"))[-(2 if part_rows < D else 1) :]
    chunk_rows = len(orders) * part_rows
    fine = chunk_rows == D
    arrived = (arrived_first, arrived_second, arrived_last)

    def peer(dim, j):
        at = lax.rem(place[dim] + j, size[dim])
        if dim == "x":
            return {"view": me + 2 * (at - place["x"])}
        if dim == "y":
            return {"dp": at}
        return {"view": me + 4 * (at - place["z"])}

    def along(offset):
        return {"view": lax.rem(me + offset + count, count)}

    sibling = {"view": me + step}

    def window_at(offset, first, rows):
        n = VIEWS - 1 + offset
        columns = pl.ds(pl.multiple_of(lax.rem(n, 4) * D, D), D)
        return weights.at[n // 4, pl.ds(first, rows), columns]

    def weight_copies():
        blocks = FF // D
        return [
            pltpu.make_async_copy(
                w_up.at[:, pl.ds(c * D, D)], arena.at[c], weight_sem.at[c]
            )
            for c in range(blocks)
        ] + [
            pltpu.make_async_copy(
                w_down.at[pl.ds(c * D, D), :], arena.at[blocks + c], weight_sem.at[blocks + c]
            )
            for c in range(blocks)
        ]

    for copy in weight_copies():
        copy.start()
    my_view = slot_view[0]
    is_filled = jnp.logical_and(
        jnp.logical_and(counts[0] > 0, keyframe[0] == 1), slot_item[0] >= 0
    )
    my_filled = is_filled.astype(jnp.int32)
    label_here = jnp.where(is_filled, slot_item[0], -1).astype(F32)
    sent[: SENT - USED, :] = jnp.full((SENT - USED, D), label_here, F32).astype(BF16)
    sent[SENT - USED :, :] = tokens[:USED, :]
    peers = [peer(dim, j) for dim in "xyz" for j in range(1, size[dim])]
    greet([sibling] + peers)

    turn = 1 - 2 * place["x"]

    def hop(kind, source, offset, first, rows, device):
        return pltpu.make_async_remote_copy(
            source,
            window_at(offset, first, rows),
            there_sem.at[kind],
            here_sem.at[kind],
            device,
            MESH,
        )

    def piece_kind(line, q):
        return line * len(PIECES) + q

    def along_z(line, q):
        first, rows = PIECES[q]
        ahead = 4 - 8 * line
        source = sent.at[pl.ds(first, rows), :]
        return hop(piece_kind(line, q), source, -ahead, first, rows, along(ahead))

    def relay_x(q):
        first, rows = PIECES[q]
        source = window_at(4 * turn, first, rows)
        return hop(piece_kind(2, q), source, 2 * turn, first, rows, along(2 * turn))

    def across_relayed(q):
        first, rows = PIECES[q]
        source = window_at(-2 * turn, first, rows)
        return hop(piece_kind(3, q), source, -2 * turn - step, first, rows, sibling)

    last_kind = 4 * len(PIECES)
    direct_x = hop(last_kind, sent, -2 * turn, 0, SENT, along(2 * turn))
    across_own = hop(last_kind + 1, sent, -step, 0, SENT, sibling)
    across_x = hop(
        last_kind + 2, window_at(2 * turn, 0, SENT), 2 * turn - step, 0, SENT, sibling
    )
    across_z = hop(last_kind + 3, window_at(4 * step, 0, SENT), 3 * step, 0, SENT, sibling)
    for q in range(len(PIECES)):
        for line in range(2):
            along_z(line, q).start()
    direct_x.start()
    across_own.start()

    levels = []
    for order in orders:
        rows = part_rows
        offset = 0
        level = [(0, rows)]
        for dim in order:
            rows = rows // size[dim]
            offset = offset + place[dim] * rows
            level.append((offset, rows))
        levels.append(level)
    own_columns = pl.ds(pl.multiple_of(core * (D // 2), D // 2), D // 2)
    other_columns = pl.ds(pl.multiple_of((1 - core) * (D // 2), D // 2), D // 2)

    def slot_of(stage, p, j):
        slot = j - 1
        for order in orders[:p]:
            slot += size[order[stage - 1]] - 1
        return slot

    def rows_of(k, p, offset, rows):
        return pl.ds(pl.multiple_of(k * chunk_rows + p * part_rows + offset, SHARD), rows)

    def held(k):
        return lax.rem(k, IN_FLIGHT)

    first_sem = [0]
    for stage in range(STAGES):
        first_sem.append(first_sem[-1] + stage_copies(stage, size, orders))

    def copies(stage, k):
        out = []

        def add(source, target, device):
            n = first_sem[stage] + len(out)
            out.append(
                pltpu.make_async_remote_copy(
                    source, target, send_sem.at[held(k), n], recv_sem.at[held(k), n], device, MESH
                )
            )

        if stage == 0:
            add(grads.at[rows_of(k, 0, 0, chunk_rows), other_columns], arrived_core.at[held(k)], sibling)
        elif stage == 7:
            whole = summed.at[rows_of(k, 0, 0, chunk_rows), own_columns]
            add(whole, whole, sibling)
        for p, order in enumerate(orders):
            if 0 < stage < 4:
                dim = order[stage - 1]
                offset, _ = levels[p][stage - 1]
                _, rows = levels[p][stage]
                for j in range(1, size[dim]):
                    at = offset + lax.rem(place[dim] + j, size[dim]) * rows
                    add(
                        grads.at[rows_of(k, p, at, rows), own_columns],
                        arrived[stage - 1].at[held(k), slot_of(stage, p, j), pl.ds(0, rows), :],
                        peer(dim, j),
                    )
            elif 4 <= stage < 7:
                dim = order[6 - stage]
                offset, rows = levels[p][7 - stage]
                at = rows_of(k, p, offset, rows)
                source = grads if stage == 4 else summed
                for j in range(1, size[dim]):
                    add(source.at[at, own_columns], summed.at[at, own_columns], peer(dim, j))
        return out

    def own_shard(k, p):
        at = rows_of(k, p, *levels[p][3])
        return pltpu.make_async_copy(
            grads.at[at, own_columns], summed.at[at, own_columns], local_sem.at[held(k), p]
        )

    def start_stage(stage, k):
        for copy in copies(stage, k):
            copy.start()
        if stage == 4:
            for p in range(len(orders)):
                own_shard(k, p).start()

    def finish_stage(stage, k):
        for copy in copies(stage, k):
            copy.wait()
        if stage == 4:
            for p in range(len(orders)):
                own_shard(k, p).wait()
        if stage == 0:
            at = rows_of(k, 0, 0, chunk_rows)
            total = grads[at, own_columns].astype(F32) + arrived_core[held(k)].astype(F32)
            grads[at, own_columns] = total.astype(BF16)
        elif stage < 4:
            for p, order in enumerate(orders):
                offset, rows = levels[p][stage]
                at = rows_of(k, p, offset, rows)
                total = grads[at, own_columns].astype(F32)
                for j in range(1, size[order[stage - 1]]):
                    total += arrived[stage - 1][held(k), slot_of(stage, p, j), :rows, :].astype(F32)
                grads[at, own_columns] = total.astype(BF16)

    blocks = FF // D

    def tick(t):
        for stage in range(STAGES, -1, -1):
            at = t - SKEW * stage
            if fine:
                late = at - (2 * blocks + 1)
                early = jnp.logical_and(at >= 0, at < 2 * blocks)
                valid = jnp.logical_and(late >= 0, late < 2 * PAIRS)
                valid = jnp.logical_or(early, jnp.logical_and(valid, lax.rem(late, 2) == 0))
                k = jnp.where(early, at, 2 * blocks + late // 2)
            else:
                k = at
                valid = jnp.logical_and(at >= 0, at < chunks)

            def go(stage=stage, k=k):
                if stage > 0:
                    finish_stage(stage - 1, k)
                if stage < STAGES:
                    start_stage(stage, k)

            pl.when(valid)(go)

    sums_dims = ("core", "x", "y", "z")

    def sums_copies(level):
        dim = sums_dims[level]
        if dim == "core":
            targets, mine = [sibling], core
        else:
            targets, mine = [peer(dim, j) for j in range(1, size[dim])], place[dim]
        return [
            pltpu.make_async_remote_copy(
                sums_at.at[level, mine],
                sums_at.at[level, mine],
                sums_send.at[level, n],
                sums_recv.at[level, n],
                device,
                MESH,
            )
            for n, device in enumerate(targets)
        ]

    def sums_start(level, value):
        dim = sums_dims[level]
        sums_at[level, core if dim == "core" else place[dim]] = value
        for copy in sums_copies(level):
            copy.start()

    def sums_finish(level):
        for copy in sums_copies(level):
            copy.wait()
        dim = sums_dims[level]
        total = sums_at[level, 0]
        for i in range(1, 2 if dim == "core" else size[dim]):
            total += sums_at[level, i]
        return total

    for c in range(blocks):
        vectors[c : c + 1, :] = bias_up[c * D : (c + 1) * D].astype(F32).reshape(1, D)
    for n, vector in enumerate((bias_down, gain_attn, shift_attn, gain_mlp, shift_mlp)):
        vectors[4 + n : 5 + n, :] = vector[...].astype(F32).reshape(1, D)
    gain_a = vectors[5:6, :]
    shift_a = vectors[6:7, :]
    gain_m = vectors[7:8, :]
    shift_m = vectors[8:9, :]

    def project_keys(first, rows, values):
        unit, _ = normalise(values.astype(F32))
        normed = (unit * gain_a + shift_a).astype(BF16)
        normed_all[first : first + rows, :] = normed
        keyval[first : first + rows, :] = dot(normed, w_keyval[...], NN).astype(BF16)

    own_rows = tokens[:USED, :]
    own_unit, _ = normalise(own_rows.astype(F32))
    query_norm[...] = (own_unit * gain_a + shift_a).astype(BF16)
    query[...] = (dot(query_norm[...], w_query[...], NN).astype(BF16) * HEAD_DIM**-0.5).astype(BF16)
    project_keys(0, PATCHES, own_rows[:PATCHES, :])
    relayed = jnp.where(turn > 0, 1, 0)
    for q in range(len(PIECES)):
        along_z(relayed, q).wait_recv()
        relay_x(q).start()
    direct_x.wait_recv()
    across_x.start()
    for q in range(len(PIECES)):
        along_z(1 - relayed, q).wait_recv()
    across_z.start()
    for q in range(len(PIECES)):
        relay_x(q).wait_recv()
        across_relayed(q).start()
    for copy in (across_own, across_x, across_z):
        copy.wait()
    direct_x.wait_send()
    for q in range(len(PIECES)):
        for line in range(2):
            along_z(line, q).wait_send()
        relay_x(q).wait_send()
        across_relayed(q).wait()
    my_label = sent[: SENT - USED, :PAIR].astype(F32)

    def bias_of(label):
        match = jnp.logical_and(label == my_label, label >= 0)
        return jnp.where(match, 0.0, NEGATIVE)[:1, :]

    def block_at(n, first, rows, columns=D):
        return weights[n // 4, first : first + rows, n % 4 * D : n % 4 * D + columns]

    key_bias[:PATCHES, :] = jnp.broadcast_to(bias_of(my_label), (PATCHES, PAIR)).astype(BF16)
    language = own_rows[PATCHES:, :]
    language_bias = bias_of(my_label)
    top_rows = SENT - USED
    for j in range(1, VIEWS):
        ahead = my_view + j < VIEWS
        holds = lax.rem(my_view + j, VIEWS) == 0

        def either(first, rows, columns=D):
            return jnp.where(
                ahead, block_at(4 + j, first, rows, columns), block_at(j - 1, first, rows, columns)
            )

        project_keys(j * PATCHES, PATCHES, either(top_rows, PATCHES))
        bias = bias_of(either(0, top_rows, PAIR).astype(F32))
        rows = slice(j * PATCHES, (j + 1) * PATCHES)
        key_bias[rows, :] = jnp.broadcast_to(bias, (PATCHES, PAIR)).astype(BF16)
        language = jnp.where(holds, either(top_rows + PATCHES, TAIL), language)
        language_bias = jnp.where(holds, bias, language_bias)
    project_keys(VIEWS * PATCHES, TAIL, language)
    index = lax.broadcasted_iota(jnp.int32, (TAIL, PAIR), 0)
    key_bias[VIEWS * PATCHES : KEYS, :] = jnp.where(
        index < LANG, jnp.broadcast_to(language_bias, (TAIL, PAIR)), NEGATIVE
    ).astype(BF16)
    normed_all[KEYS:, :] = jnp.zeros((KEYS_PADDED - KEYS, D), BF16)
    keyval[KEYS:, :] = jnp.zeros((KEYS_PADDED - KEYS, 2 * D), BF16)
    key_bias[KEYS:, :] = jnp.full((KEYS_PADDED - KEYS, PAIR), NEGATIVE, BF16)

    lane = lax.broadcasted_iota(jnp.int32, (1, PAIR), 1)
    low_half = lane < HEAD_DIM

    def half_of(half, first, second):
        return jnp.where(low_half, first, second) if half == 0 else jnp.where(low_half, second, first)

    def head_keys(p, half):
        pair = keyval[:, pl.ds(pl.multiple_of(p * PAIR, PAIR), PAIR)]
        return half_of(half, pair, key_bias[...])

    def head_values(p, half):
        pair = keyval[:, pl.ds(pl.multiple_of(D + p * PAIR, PAIR), PAIR)]
        return half_of(half, pair, jnp.ones((), BF16))

    def spill(p, half):
        return pltpu.make_async_copy(
            weights.at[2 * lax.rem(p, 2) + half, pl.ds(0, USED), :], spilled.at[2 * p + half], spill_sem.at[lax.rem(p, 2), half]
        )

    def unspill(p, half):
        return pltpu.make_async_copy(
            spilled.at[2 * p + half], weights.at[2 * lax.rem(p, 2) + half, pl.ds(0, USED), :], spill_sem.at[lax.rem(p, 2), half]
        )

    def forward_pair(p, _):
        columns = pl.ds(pl.multiple_of(p * PAIR, PAIR), PAIR)
        pair = query[:, columns]
        outs = []
        totals = []

        def settle():
            for half in range(2):
                spill(p - 1, half).wait()

        pl.when(jnp.logical_and(p >= 1, p < 3))(settle)
        for half in range(2):
            one = (lane == HEAD_DIM * (1 - half)).astype(BF16)
            scores = dot(half_of(half, pair, one), head_keys(p, half), NT)
            top = jnp.max(scores, -1, keepdims=True)
            weight = jnp.exp(scores - top).astype(BF16)
            weights[2 * lax.rem(p, 2) + half, :USED, :] = weight
            out = dot(weight, head_values(p, half), NN)
            outs.append(out)
            totals.append(pltpu.roll(out, HEAD_DIM, 1))
        inv = 1.0 / jnp.where(low_half, totals[0], totals[1])
        full = jnp.where(low_half, outs[0], outs[1]) * inv
        inverse[:, columns] = inv
        mixed_full[:, columns] = full
        mixed[:, columns] = full.astype(BF16)

        def save():
            for half in range(2):
                spill(p, half).start()

        pl.when(p < 2)(save)
        return 0

    lax.fori_loop(0, PAIRS, forward_pair, 0)

    row = lax.broadcasted_iota(jnp.int32, (USED, PAIR), 0)
    has_language = (my_view == 0).astype(jnp.int32)
    live_rows = my_filled * (PATCHES + LANG * has_language)
    live = (row < live_rows).astype(F32)[:, :1]
    res = tokens[:USED, :].astype(F32) + live * dot(mixed[...], w_output[...], NN)
    residual[...] = res
    unit_m, scale_m = normalise(res)
    normed_mlp[...] = (unit_m * gain_m + shift_m).astype(BF16)
    upstream = cotangent[:USED, :].astype(F32)
    branch_grad[...] = (live * upstream).astype(BF16)
    branch[...] = jnp.zeros((USED, D), F32)
    mlp_back[...] = jnp.zeros((USED, D), F32)
    for copy in weight_copies():
        copy.wait()

    def feed_forward(c, _):
        up = arena[c]
        down = arena[blocks + c]
        before = dot(normed_mlp[...], up, NN) + vectors[pl.ds(c, 1), :]
        chance = 0.5 + 0.5 * lax.erf(before * 0.5**0.5)
        density = jnp.exp(-0.5 * before * before) * 0.3989422804014327
        activated = (before * chance).astype(BF16)
        slope = chance + before * density
        start = pl.multiple_of(2 * c * D, D)
        grads[pl.ds(start, D), :] = dot(activated, branch_grad[...], TN).astype(BF16)
        branch[...] += dot(activated, down, NN)
        before_full = dot(branch_grad[...], down, NT) * slope
        before_grad = before_full.astype(BF16)
        sums_out[pl.ds(c, 1), :] = jnp.sum(before_grad.astype(F32), 0, keepdims=True)
        grads[pl.ds(start + D, D), :] = dot(normed_mlp[...], before_grad, TN).astype(BF16)
        mlp_back[...] += dot(before_grad, up, NT)
        if fine:
            tick(2 * c)
            tick(2 * c + 1)
        return 0

    lax.fori_loop(0, blocks, feed_forward, 0)
    block_output[:USED, :] = (residual[...] + live * (branch[...] + vectors[4:5, :])).astype(BF16)
    block_output[USED:, :] = tokens[USED:, :]
    unit_m, scale_m = normalise(residual[...])
    back = mlp_back[...]
    sums_out[4:5, :] = jnp.sum(branch_grad[...].astype(F32), 0, keepdims=True)
    sums_out[5:6, :] = jnp.sum(back * unit_m, 0, keepdims=True)
    sums_out[6:7, :] = jnp.sum(back, 0, keepdims=True)
    res_grad = upstream + norm_backward(back, unit_m, scale_m, gain_m)
    grad_tokens[:USED, :] = res_grad
    grad_tokens[USED:, :] = cotangent[USED:, :].astype(F32)
    attended_grad = (live * res_grad).astype(BF16)
    base = 2 * FF
    out_grad = dot(mixed[...], attended_grad, TN).astype(BF16)
    for i in range(PAIRS):
        grads[base + i * D : base + i * D + PAIR, :] = out_grad[i * PAIR : (i + 1) * PAIR, :]
    mixed_grad[...] = dot(attended_grad, w_output[...], NT).astype(BF16)

    branch[...] = jnp.zeros((USED, D), F32)

    def backward_pair(i, _):
        p = PAIRS - 1 - i
        columns = pl.ds(pl.multiple_of(p * PAIR, PAIR), PAIR)
        grad = mixed_grad[:, columns].astype(F32)
        inv = inverse[:, columns]
        scaled = grad * inv
        product = scaled * mixed_full[:, columns]
        scaled_low = scaled.astype(BF16)
        scaled_t = scaled.T.astype(BF16)
        query_t = query[:, columns].astype(F32).T.astype(BF16)
        query_parts = []
        start = pl.multiple_of(p * PAIR, PAIR)

        def settle():
            for half in range(2):
                unspill(p, half).wait()

        pl.when(p < 2)(settle)
        for half in range(2):
            here = low_half if half == 0 else jnp.logical_not(low_half)
            dots = -jnp.sum(jnp.where(here, product, 0.0), -1, keepdims=True)
            dots_high = dots.astype(BF16)
            dots_low = (dots - dots_high.astype(F32)).astype(BF16)
            other = HEAD_DIM * (1 - half)
            rest = jnp.where(
                lane == other, dots_high, jnp.where(lane == other + 1, dots_low, jnp.zeros((), BF16))
            )
            weight = weights[2 * lax.rem(p, 2) + half, :USED, :]
            slope = dot(half_of(half, scaled_low, rest), head_values(p, half), NT)
            score_grad = weight * slope.astype(BF16)
            query_parts.append(dot(score_grad, head_keys(p, half), NN))
            rows = slice(half * HEAD_DIM, (half + 1) * HEAD_DIM)
            at = start + half * HEAD_DIM
            keyval_grad[pl.ds(at, HEAD_DIM), :] = dot(query_t[rows, :], score_grad, NN).astype(BF16)
            keyval_grad[pl.ds(D + at, HEAD_DIM), :] = dot(scaled_t[rows, :], weight, NN).astype(BF16)
            if fine and half == 0:
                tick(2 * blocks + 2 * i)

        def load():
            for half in range(2):
                unspill(p - 2, half).start()

        pl.when(p >= 2)(load)
        part = jnp.where(low_half, query_parts[0], query_parts[1]) * HEAD_DIM**-0.5
        query_grad = part.astype(BF16)
        at = pl.multiple_of(base + i * D, D)
        grads[pl.ds(at + PAIR, PAIR), :] = dot(query_grad, query_norm[...], TN).astype(BF16)
        for c in range(2):
            of_pair = keyval_grad[pl.ds(c * D + start, PAIR), :]
            grads[pl.ds(at + (2 + c) * PAIR, PAIR), :] = dot(of_pair, normed_all[...], NN).astype(
                BF16
            )
        branch[...] += dot(query_grad, w_query[:, columns], NT)
        if fine:
            tick(2 * blocks + 2 * i + 1)
        return 0

    lax.fori_loop(0, PAIRS, backward_pair, 0)

    from_query = branch[...]
    normed = query_norm[...].astype(F32)
    shift_sum = jnp.sum(from_query, 0, keepdims=True)
    gain_sum = jnp.sum(from_query * normed, 0, keepdims=True)

    def parts_at(j):
        return weights.at[0, :USED, (j - 1) * D : j * D]

    for j in range(VIEWS + 1):
        rows = slice(j * PATCHES, min((j + 1) * PATCHES, KEYS))
        piece = dot(keyval_grad[:, rows], w_keyval[...], TT)
        normed = normed_all[rows, :].astype(F32)
        shift_sum += jnp.sum(piece, 0, keepdims=True)
        gain_sum += jnp.sum(piece * normed, 0, keepdims=True)
        if j == 0:
            branch[:PATCHES, :] += piece
        elif j < VIEWS:
            parts_at(j)[:PATCHES, :] = piece.astype(BF16)
        else:
            branch[PATCHES:, :] += jnp.where(my_view == 0, piece, 0.0)
            for i in range(1, VIEWS):
                holds = lax.rem(my_view + i, VIEWS) == 0
                parts_at(i)[PATCHES:, :] = jnp.where(holds, piece, 0.0).astype(BF16)
    sums_out[7:8, :] = (gain_sum - shift_a * shift_sum) / gain_a
    sums_out[8:9, :] = shift_sum
    sums_out[9:, :] = jnp.zeros((SUMS - 9, D), F32)

    def part_for(offset):
        slot = lax.rem(offset + VIEWS, VIEWS) - 1
        at = my_view + offset
        valid = jnp.logical_and(at >= 0, at < VIEWS)
        value = jnp.zeros((USED, D), BF16)
        for n in range(VIEWS - 1):
            value = jnp.where(jnp.logical_and(valid, slot == n), parts_at(n + 1)[...], value)
        return value

    def swap(n):
        return pltpu.make_async_remote_copy(
            arena.at[n, pl.ds(0, USED), :],
            arena.at[4 + n, pl.ds(0, USED), :],
            swap_sem.at[0, n],
            swap_sem.at[1, n],
            sibling,
            MESH,
        )

    back_pieces = ((0, 160), (160, 160), (320, 160))

    def back(kind, slot, target, offset, q):
        first, rows = back_pieces[q]
        n = kind * len(back_pieces) + q
        return pltpu.make_async_remote_copy(
            arena.at[slot, pl.ds(first, rows), :],
            far_in.at[target, pl.ds(first, rows), :],
            far_sem.at[0, n],
            far_sem.at[1, n],
            along(offset),
            MESH,
        )

    def back_relay(q):
        return back(0, 1, 0, 2 * turn, q)

    def back_x(q):
        return back(1, 2, 1, 2 * turn, q)

    def back_up(q):
        return back(2, 3, 2, 4 * turn, q)

    def back_down(q):
        return back(3, 0, 3, -4 * turn, q)

    ticks = 2 * blocks + 2 * PAIRS if fine else 0
    last = ticks + STAGES * SKEW if fine else chunks + STAGES * SKEW

    def run_ticks(first, end):
        def body(t, _):
            tick(t)
            return 0

        lax.fori_loop(first, end, body, 0)

    if not fine:
        run_ticks(0, SKEW + 1)
        ticks = SKEW + 1
    sums_start(0, sums_out[...])
    for n, offset in enumerate((step, step - 2 * turn, step + 2 * turn, -3 * step)):
        arena[n, :USED, :] = part_for(offset)
        swap(n).start()
    run_ticks(ticks, ticks + 1)
    sums_start(1, sums_finish(0))
    pieces = range(len(back_pieces))
    for n, offset in ((1, -2 * turn), (2, 2 * turn)):
        swap(n).wait()
        both = part_for(offset).astype(F32) + arena[4 + n, :USED, :].astype(F32)
        arena[n, :USED, :] = both.astype(BF16)
        for q in pieces:
            (back_relay if n == 1 else back_x)(q).start()
    swap(0).wait()
    swap(3).wait()
    shared = arena[7, :USED, :].astype(F32)
    arena[0, :USED, :] = (
        part_for(-4 * turn).astype(F32) + jnp.where(step == turn, 0.0, shared)
    ).astype(BF16)
    for q in pieces:
        back_down(q).start()
    arena[3, :USED, :] = (
        part_for(4 * turn).astype(F32) + jnp.where(step == turn, shared, 0.0)
    ).astype(BF16)
    for q in pieces:
        first, rows = back_pieces[q]
        at = slice(first, first + rows)
        back_relay(q).wait_recv()
        both = arena[3, at, :].astype(F32) + far_in[0, at, :].astype(F32)
        arena[3, at, :] = both.astype(BF16)
        back_up(q).start()
    run_ticks(ticks + 1, ticks + 2)
    sums_start(2, sums_finish(1))
    run_ticks(ticks + 2, ticks + 4)
    sums_start(3, sums_finish(2))
    run_ticks(ticks + 4, last)
    sums_out[...] = sums_finish(3)
    total = branch[...] + arena[4, :USED, :].astype(F32)
    for q in pieces:
        back_relay(q).wait_send()
        for copy in (back_x(q), back_up(q), back_down(q)):
            copy.wait()
    for n in range(1, 4):
        total += far_in[n].astype(F32)
    unit, scale = normalise(tokens[:USED, :].astype(F32))
    grad_tokens[:USED, :] += norm_backward(total, unit, scale, gain_a)


def stage_copies(stage, size, orders):
    if stage in (0, 7):
        return 1
    return sum(size[order[stage - 1 if stage < 4 else 6 - stage]] - 1 for order in orders)


def main(count, groups, *args):
    depth = count // 4
    part_rows = 2 * groups * depth * SHARD
    parts = 2 if part_rows < D else 1
    chunk_rows = parts * part_rows
    chunks = -(-GRAD_ROWS // chunk_rows)
    shape = jax.ShapeDtypeStruct
    dma = pltpu.SemaphoreType.DMA
    wide = max(groups, depth)
    half = D // 2
    orders = ((2, groups, depth), (groups, 2, depth))[-parts:]
    slots = [sum(order[stage] - 1 for order in orders) for stage in range(3)]
    sems = 2 + 2 * sum(slots)
    held = min(chunks, IN_FLIGHT)
    left = [part_rows // order[0] for order in orders]
    first = max(left)
    second = max(rows // order[1] for rows, order in zip(left, orders))
    scratch = [
        VMEM((KEYS_PADDED, D), BF16),
        VMEM((USED, D), BF16),
        VMEM((KEYS_PADDED, PAIR), BF16),
        VMEM((KEYS_PADDED, 2 * D), BF16),
        VMEM((USED, D), BF16),
        VMEM((4, SENT, KEYS_PADDED), BF16),
        VMEM((USED, D), BF16),
        VMEM((USED, D), F32),
        VMEM((USED, D), F32),
        VMEM((2 * D, KEYS_PADDED), BF16),
        VMEM((USED, D), BF16),
        VMEM((USED, D), BF16),
        VMEM((USED, D), BF16),
        VMEM((USED, D), F32),
        VMEM((USED, D), F32),
        VMEM((USED, D), F32),
        VMEM((SENT, D), BF16),
        VMEM((SUMS, D), F32),
        VMEM((2 * FF // D, D, D), BF16),
        VMEM((chunks * chunk_rows, D), BF16),
        VMEM((held, chunk_rows, half), BF16),
        VMEM((held, slots[0], first, half), BF16),
        VMEM((held, slots[1], second, half), BF16),
        VMEM((held, slots[2], SHARD, half), BF16),
        VMEM((4, USED, D), BF16),
        VMEM((4, wide, SUMS, D), F32),
        dma((4 * len(PIECES) + 4,)),
        dma((4 * len(PIECES) + 4,)),
        dma((2 * FF // D,)),
        dma((2, 2)),
        dma((held, sems)),
        dma((held, sems)),
        dma((held, 2)),
        dma((4, wide)),
        dma((4, wide)),
        dma((2, 4)),
        dma((2, 12)),
    ]
    return pl.pallas_call(
        functools.partial(main_kernel, count, groups, chunks, part_rows),
        out_shape=(
            shape((ROWS, D), BF16),
            shape((ROWS, D), F32),
            shape((chunks * chunk_rows, D), BF16),
            shape((SUMS, D), F32),
            shape((4, USED, KEYS_PADDED), BF16),
        ),
        in_specs=[IN_SMEM] * 4 + [IN_VMEM] * 11 + [ANYWHERE] * 2,
        out_specs=[IN_VMEM, IN_VMEM, ANYWHERE, IN_VMEM, ANYWHERE],
        scratch_shapes=scratch,
        compiler_params=pltpu.CompilerParams(
            collective_id=1, has_side_effects=True, vmem_limit_bytes=63 * MIB
        ),
        name="main",
    )(*args)


def widen_kernel(
    summed,
    rows_in,
    grad_in,
    sums,
    down,
    up,
    out,
    query,
    keyval,
    rows_out,
    grad_out,
    grad_bias_up,
    grad_bias_down,
    grad_gain_mlp,
    grad_shift_mlp,
    grad_gain_attn,
    grad_shift_attn,
    narrow,
    wide,
    rows_held,
    grad_held,
    in_sem,
    out_sem,
    pass_sem,
):
    blocks = FF // D
    passes_in = [
        pltpu.make_async_copy(rows_in, rows_held, pass_sem.at[0]),
        pltpu.make_async_copy(grad_in, grad_held, pass_sem.at[1]),
    ]
    passes_out = [
        pltpu.make_async_copy(rows_held, rows_out, pass_sem.at[2]),
        pltpu.make_async_copy(grad_held, grad_out, pass_sem.at[3]),
    ]
    count = 2 * blocks + PAIRS
    loads = [
        pltpu.make_async_copy(summed.at[pl.ds(b * D, D), :], narrow.at[b], in_sem.at[b])
        for b in range(count)
    ]
    for copy in passes_in + loads:
        copy.start()
    for c in range(blocks):
        grad_bias_up[c * D : (c + 1) * D] = sums[c : c + 1, :].reshape(D)
    rest = (grad_bias_down, grad_gain_mlp, grad_shift_mlp, grad_gain_attn, grad_shift_attn)
    for n, target in enumerate(rest):
        target[...] = sums[blocks + n : blocks + n + 1, :].reshape(D)
    for copy in passes_in:
        copy.wait()
    for copy in passes_out:
        copy.start()
    stores = []

    def store(b, source, target):
        stores.append(pltpu.make_async_copy(source, target, out_sem.at[len(stores)]))
        stores[-1].start()

    for b in range(count):
        loads[b].wait()
        c = b // 2
        if b < 2 * blocks:
            wide[b] = narrow[b].astype(F32)
            at = pl.ds(c * D, D)
            store(b, wide.at[b], down.at[at, :] if b % 2 == 0 else up.at[:, at])
        else:
            i = b - 2 * blocks
            p = PAIRS - 1 - i
            wide[b, :PAIR, :] = narrow[b, :PAIR, :].astype(F32)
            store(b, wide.at[b, pl.ds(0, PAIR), :], out.at[pl.ds(i * PAIR, PAIR), :])
            base = 2 * blocks + PAIRS
            for n, (target, column) in enumerate(((query, p), (keyval, p), (keyval, PAIRS + p))):
                piece = narrow[b, (n + 1) * PAIR : (n + 2) * PAIR, :].astype(F32).T
                columns = slice(p * PAIR, (p + 1) * PAIR)
                wide[base + n, :, columns] = piece
                store(
                    b,
                    wide.at[base + n, :, pl.ds(p * PAIR, PAIR)],
                    target.at[:, pl.ds(column * PAIR, PAIR)],
                )
    for copy in stores + passes_out:
        copy.wait()


def widen(summed, rows, grad, sums):
    blocks = 2 * FF // D + PAIRS
    shape = jax.ShapeDtypeStruct
    dma = pltpu.SemaphoreType.DMA
    return pl.pallas_call(
        widen_kernel,
        out_shape=(
            shape((FF, D), F32),
            shape((D, FF), F32),
            shape((D, D), F32),
            shape((D, D), F32),
            shape((D, 2 * D), F32),
            shape(rows.shape, rows.dtype),
            shape(grad.shape, grad.dtype),
            shape((FF,), F32),
        )
        + (shape((D,), F32),) * 5,
        in_specs=[ANYWHERE] * 3 + [IN_VMEM],
        out_specs=[ANYWHERE] * 7 + [IN_VMEM] * 6,
        scratch_shapes=[
            VMEM((blocks, D, D), BF16),
            VMEM((blocks + 3, D, D), F32),
            VMEM(rows.shape, rows.dtype),
            VMEM(grad.shape, grad.dtype),
            dma((blocks,)),
            dma((blocks + 3 * PAIRS,)),
            dma((4,)),
        ],
        compiler_params=pltpu.CompilerParams(vmem_limit_bytes=60 * MIB),
        name="widen",
    )(summed, rows, grad, sums)


def on_device(
    count,
    groups,
    tokens,
    counts,
    slot_item,
    slot_view,
    keyframe,
    w_query,
    w_keyval,
    w_output,
    w_up,
    bias_up,
    w_down,
    bias_down,
    gain_attn,
    shift_attn,
    gain_mlp,
    shift_mlp,
    cotangent,
):
    block_output, grad_tokens, summed, sums, _ = main(
        count,
        groups,
        counts.reshape(1),
        slot_item.reshape(1),
        slot_view.reshape(1),
        keyframe.reshape(1),
        tokens.reshape(ROWS, D),
        cotangent.reshape(ROWS, D),
        w_query,
        w_keyval,
        w_output,
        bias_up,
        bias_down,
        gain_attn,
        shift_attn,
        gain_mlp,
        shift_mlp,
        w_up,
        w_down,
    )
    down, up, out, query, keyval, block_output, grad_tokens, *small = widen(
        summed, block_output, grad_tokens, sums
    )
    grad_bias_up, grad_bias_down, gain_mlp, shift_mlp, gain_attn, shift_attn = small
    return (
        block_output.reshape(tokens.shape),
        grad_tokens.reshape(tokens.shape),
        query,
        keyval,
        out,
        up,
        grad_bias_up,
        down,
        grad_bias_down,
        gain_attn,
        shift_attn,
        gain_mlp,
        shift_mlp,
    )


def solution(mesh):
    count = mesh.shape["view"]
    groups = mesh.shape["dp"]
    slots = P("dp", "view", None)
    rows = P("dp", "view", None, None, None)
    in_specs = (rows, P("dp", "view"), slots, slots, slots) + (P(),) * 11 + (rows,)
    out_specs = (rows, rows) + (P(),) * 11
    return jax.shard_map(
        functools.partial(on_device, count, groups),
        mesh=mesh,
        in_specs=in_specs,
        out_specs=out_specs,
        check_vma=False,
    )
```

```python
import functools

import jax
import jax.numpy as jnp
from jax import lax
from jax.experimental import pallas as pl
from jax.experimental.pallas import tpu as pltpu
from jax.sharding import PartitionSpec as P

D = 512
HEADS = 8
HEAD_DIM = 64
PAIRS = HEADS // 2
PAIR = 2 * HEAD_DIM
VIEWS = 5
PATCHES = 400
LANG = 77
ROWS = 512
USED = 480
TAIL = USED - PATCHES
SENT = 496
KEYS = VIEWS * PATCHES + TAIL
KEYS_PADDED = 2176
FF = 2048
FF_BLOCK = 512
NEGATIVE = -1e30
EPSILON = 1e-5
GRAD_ROWS = 2 * FF + 4 * D
SUMS = 16
SHARD = 16
STAGES = 8
SKEW = 2
IN_FLIGHT = 4
BESIDE = 1
PIECES = ((0, 128), (128, 128), (256, 128), (384, 112))

BF16 = jnp.bfloat16
F32 = jnp.float32
MESH = pl.DeviceIdType.MESH
NN = (((1,), (0,)), ((), ()))
NT = (((1,), (1,)), ((), ()))
TN = (((0,), (0,)), ((), ()))
TT = (((0,), (1,)), ((), ()))
MIB = 2**20

VMEM = pltpu.VMEM
IN_VMEM = pl.BlockSpec(memory_space=pltpu.VMEM)
IN_SMEM = pl.BlockSpec(memory_space=pltpu.SMEM)
ANYWHERE = pl.BlockSpec(memory_space=pl.ANY)


def dot(left, right, dims):
    return lax.dot_general(left, right, dims, preferred_element_type=F32)


def normalise(values):
    average = jnp.mean(values, -1, keepdims=True)
    centered = values - average
    variance = jnp.mean(centered * centered, -1, keepdims=True)
    scale = lax.rsqrt(variance + EPSILON)
    return centered * scale, scale


def norm_backward(grad, unit, scale, gain):
    grad = grad * gain
    first = jnp.mean(grad, -1, keepdims=True)
    second = jnp.mean(grad * unit, -1, keepdims=True)
    return scale * (grad - first - unit * second)


def greet(others):
    barrier = pltpu.get_barrier_semaphore()
    for other in others:
        pl.semaphore_signal(barrier, inc=1, device_id=other, device_id_type=MESH)
    pl.semaphore_wait(barrier, len(others))


def main_kernel(
    count,
    groups,
    chunks,
    part_rows,
    counts,
    slot_item,
    slot_view,
    keyframe,
    tokens,
    cotangent,
    w_query,
    w_keyval,
    w_output,
    bias_up,
    bias_down,
    gain_attn,
    shift_attn,
    gain_mlp,
    shift_mlp,
    w_up,
    w_down,
    block_output,
    grad_tokens,
    summed,
    sums_out,
    spilled,
    normed_all,
    query_norm,
    key_bias,
    keyval,
    query,
    weights,
    mixed,
    mixed_full,
    inverse,
    keyval_grad,
    mixed_grad,
    normed_mlp,
    branch_grad,
    residual,
    branch,
    mlp_back,
    sent,
    vectors,
    arena,
    grads,
    arrived_core,
    arrived_first,
    arrived_second,
    arrived_last,
    far_in,
    sums_at,
    there_sem,
    here_sem,
    weight_sem,
    spill_sem,
    send_sem,
    recv_sem,
    local_sem,
    sums_send,
    sums_recv,
    swap_sem,
    far_sem,
):
    me = lax.axis_index("view")
    group = lax.axis_index("dp")
    depth = count // 4
    core = lax.rem(me, 2)
    step = 1 - 2 * core
    place = {"x": lax.rem(me // 2, 2), "y": group, "z": me // 4}
    size = {"x": 2, "y": groups, "z": depth}
    orders = (("x", "y", "z"), ("y", "x", "z"))[-(2 if part_rows < D else 1) :]
    chunk_rows = len(orders) * part_rows
    fine = chunk_rows == D
    arrived = (arrived_first, arrived_second, arrived_last)

    def peer(dim, j):
        at = lax.rem(place[dim] + j, size[dim])
        if dim == "x":
            return {"view": me + 2 * (at - place["x"])}
        if dim == "y":
            return {"dp": at}
        return {"view": me + 4 * (at - place["z"])}

    def along(offset):
        return {"view": lax.rem(me + offset + count, count)}

    sibling = {"view": me + step}

    def window_at(offset, first, rows):
        n = VIEWS - 1 + offset
        columns = pl.ds(pl.multiple_of(lax.rem(n, 4) * D, D), D)
        return weights.at[n // 4, pl.ds(first, rows), columns]

    def weight_copies():
        blocks = FF // D
        return [
            pltpu.make_async_copy(
                w_up.at[:, pl.ds(c * D, D)], arena.at[c], weight_sem.at[c]
            )
            for c in range(blocks)
        ] + [
            pltpu.make_async_copy(
                w_down.at[pl.ds(c * D, D), :], arena.at[blocks + c], weight_sem.at[blocks + c]
            )
            for c in range(blocks)
        ]

    for copy in weight_copies():
        copy.start()
    my_view = slot_view[0]
    is_filled = jnp.logical_and(
        jnp.logical_and(counts[0] > 0, keyframe[0] == 1), slot_item[0] >= 0
    )
    my_filled = is_filled.astype(jnp.int32)
    label_here = jnp.where(is_filled, slot_item[0], -1).astype(F32)
    sent[: SENT - USED, :] = jnp.full((SENT - USED, D), label_here, F32).astype(BF16)
    sent[SENT - USED :, :] = tokens[:USED, :]
    peers = [peer(dim, j) for dim in "xyz" for j in range(1, size[dim])]
    greet([sibling] + peers)

    turn = 1 - 2 * place["x"]

    def hop(kind, source, offset, first, rows, device):
        return pltpu.make_async_remote_copy(
            source,
            window_at(offset, first, rows),
            there_sem.at[kind],
            here_sem.at[kind],
            device,
            MESH,
        )

    def piece_kind(line, q):
        return line * len(PIECES) + q

    def along_z(line, q):
        first, rows = PIECES[q]
        ahead = 4 - 8 * line
        source = sent.at[pl.ds(first, rows), :]
        return hop(piece_kind(line, q), source, -ahead, first, rows, along(ahead))

    def relay_x(q):
        first, rows = PIECES[q]
        source = window_at(4 * turn, first, rows)
        return hop(piece_kind(2, q), source, 2 * turn, first, rows, along(2 * turn))

    def across_relayed(q):
        first, rows = PIECES[q]
        source = window_at(-2 * turn, first, rows)
        return hop(piece_kind(3, q), source, -2 * turn - step, first, rows, sibling)

    last_kind = 4 * len(PIECES)
    direct_x = hop(last_kind, sent, -2 * turn, 0, SENT, along(2 * turn))
    across_own = hop(last_kind + 1, sent, -step, 0, SENT, sibling)
    across_x = hop(
        last_kind + 2, window_at(2 * turn, 0, SENT), 2 * turn - step, 0, SENT, sibling
    )
    across_z = hop(last_kind + 3, window_at(4 * step, 0, SENT), 3 * step, 0, SENT, sibling)
    for q in range(len(PIECES)):
        for line in range(2):
            along_z(line, q).start()
    direct_x.start()
    across_own.start()

    levels = []
    for order in orders:
        rows = part_rows
        offset = 0
        level = [(0, rows)]
        for dim in order:
            rows = rows // size[dim]
            offset = offset + place[dim] * rows
            level.append((offset, rows))
        levels.append(level)
    own_columns = pl.ds(pl.multiple_of(core * (D // 2), D // 2), D // 2)
    other_columns = pl.ds(pl.multiple_of((1 - core) * (D // 2), D // 2), D // 2)

    def slot_of(stage, p, j):
        slot = j - 1
        for order in orders[:p]:
            slot += size[order[stage - 1]] - 1
        return slot

    def rows_of(k, p, offset, rows):
        return pl.ds(pl.multiple_of(k * chunk_rows + p * part_rows + offset, SHARD), rows)

    def held(k):
        return lax.rem(k, IN_FLIGHT)

    first_sem = [0]
    for stage in range(STAGES):
        first_sem.append(first_sem[-1] + stage_copies(stage, size, orders))

    def copies(stage, k):
        out = []

        def add(source, target, device):
            n = first_sem[stage] + len(out)
            out.append(
                pltpu.make_async_remote_copy(
                    source, target, send_sem.at[held(k), n], recv_sem.at[held(k), n], device, MESH
                )
            )

        if stage == 0:
            add(grads.at[rows_of(k, 0, 0, chunk_rows), other_columns], arrived_core.at[held(k)], sibling)
        elif stage == 7:
            whole = summed.at[rows_of(k, 0, 0, chunk_rows), own_columns]
            add(whole, whole, sibling)
        for p, order in enumerate(orders):
            if 0 < stage < 4:
                dim = order[stage - 1]
                offset, _ = levels[p][stage - 1]
                _, rows = levels[p][stage]
                for j in range(1, size[dim]):
                    at = offset + lax.rem(place[dim] + j, size[dim]) * rows
                    add(
                        grads.at[rows_of(k, p, at, rows), own_columns],
                        arrived[stage - 1].at[held(k), slot_of(stage, p, j), pl.ds(0, rows), :],
                        peer(dim, j),
                    )
            elif 4 <= stage < 7:
                dim = order[6 - stage]
                offset, rows = levels[p][7 - stage]
                at = rows_of(k, p, offset, rows)
                source = grads if stage == 4 else summed
                for j in range(1, size[dim]):
                    add(source.at[at, own_columns], summed.at[at, own_columns], peer(dim, j))
        return out

    def own_shard(k, p):
        at = rows_of(k, p, *levels[p][3])
        return pltpu.make_async_copy(
            grads.at[at, own_columns], summed.at[at, own_columns], local_sem.at[held(k), p]
        )

    def start_stage(stage, k):
        for copy in copies(stage, k):
            copy.start()
        if stage == 4:
            for p in range(len(orders)):
                own_shard(k, p).start()

    def finish_stage(stage, k):
        for copy in copies(stage, k):
            copy.wait()
        if stage == 4:
            for p in range(len(orders)):
                own_shard(k, p).wait()
        if stage == 0:
            at = rows_of(k, 0, 0, chunk_rows)
            total = grads[at, own_columns].astype(F32) + arrived_core[held(k)].astype(F32)
            grads[at, own_columns] = total.astype(BF16)
        elif stage < 4:
            for p, order in enumerate(orders):
                offset, rows = levels[p][stage]
                at = rows_of(k, p, offset, rows)
                total = grads[at, own_columns].astype(F32)
                for j in range(1, size[order[stage - 1]]):
                    total += arrived[stage - 1][held(k), slot_of(stage, p, j), :rows, :].astype(F32)
                grads[at, own_columns] = total.astype(BF16)

    blocks = FF // D

    def tick(t):
        for stage in range(STAGES, -1, -1):
            at = t - SKEW * stage
            if fine:
                late = at - (2 * blocks + 2 * BESIDE - 1)
                early = jnp.logical_and(at >= 0, at < 2 * blocks)
                valid = jnp.logical_and(late >= 0, late < 2 * BESIDE * PAIRS)
                valid = jnp.logical_or(early, jnp.logical_and(valid, lax.rem(late, 2 * BESIDE) == 0))
                k = jnp.where(early, at, 2 * blocks + late // (2 * BESIDE))
            else:
                k = at
                valid = jnp.logical_and(at >= 0, at < chunks)

            def go(stage=stage, k=k):
                if stage > 0:
                    finish_stage(stage - 1, k)
                if stage < STAGES:
                    start_stage(stage, k)

            pl.when(valid)(go)

    def run_ticks(first, end):
        def body(t, _):
            tick(t)
            return 0

        lax.fori_loop(first, end, body, 0)

    sums_dims = ("core", "x", "y", "z")

    def sums_copies(level):
        dim = sums_dims[level]
        if dim == "core":
            targets, mine = [sibling], core
        else:
            targets, mine = [peer(dim, j) for j in range(1, size[dim])], place[dim]
        return [
            pltpu.make_async_remote_copy(
                sums_at.at[level, mine],
                sums_at.at[level, mine],
                sums_send.at[level, n],
                sums_recv.at[level, n],
                device,
                MESH,
            )
            for n, device in enumerate(targets)
        ]

    def sums_start(level, value):
        dim = sums_dims[level]
        sums_at[level, core if dim == "core" else place[dim]] = value
        for copy in sums_copies(level):
            copy.start()

    def sums_finish(level):
        for copy in sums_copies(level):
            copy.wait()
        dim = sums_dims[level]
        total = sums_at[level, 0]
        for i in range(1, 2 if dim == "core" else size[dim]):
            total += sums_at[level, i]
        return total

    for c in range(blocks):
        vectors[c : c + 1, :] = bias_up[c * D : (c + 1) * D].astype(F32).reshape(1, D)
    for n, vector in enumerate((bias_down, gain_attn, shift_attn, gain_mlp, shift_mlp)):
        vectors[4 + n : 5 + n, :] = vector[...].astype(F32).reshape(1, D)
    gain_a = vectors[5:6, :]
    shift_a = vectors[6:7, :]
    gain_m = vectors[7:8, :]
    shift_m = vectors[8:9, :]

    def project_keys(first, rows, values):
        unit, _ = normalise(values.astype(F32))
        normed = (unit * gain_a + shift_a).astype(BF16)
        normed_all[first : first + rows, :] = normed
        keyval[first : first + rows, :] = dot(normed, w_keyval[...], NN).astype(BF16)

    own_rows = tokens[:USED, :]
    own_unit, _ = normalise(own_rows.astype(F32))
    query_norm[...] = (own_unit * gain_a + shift_a).astype(BF16)
    query[...] = (dot(query_norm[...], w_query[...], NN).astype(BF16) * HEAD_DIM**-0.5).astype(BF16)
    project_keys(0, PATCHES, own_rows[:PATCHES, :])
    relayed = jnp.where(turn > 0, 1, 0)
    for q in range(len(PIECES)):
        along_z(relayed, q).wait_recv()
        relay_x(q).start()
    direct_x.wait_recv()
    across_x.start()
    for q in range(len(PIECES)):
        along_z(1 - relayed, q).wait_recv()
    across_z.start()
    for q in range(len(PIECES)):
        relay_x(q).wait_recv()
        across_relayed(q).start()
    for copy in (across_own, across_x, across_z):
        copy.wait()
    direct_x.wait_send()
    for q in range(len(PIECES)):
        for line in range(2):
            along_z(line, q).wait_send()
        relay_x(q).wait_send()
        across_relayed(q).wait()
    my_label = sent[: SENT - USED, :PAIR].astype(F32)

    def bias_of(label):
        match = jnp.logical_and(label == my_label, label >= 0)
        return jnp.where(match, 0.0, NEGATIVE)[:1, :]

    def block_at(n, first, rows, columns=D):
        return weights[n // 4, first : first + rows, n % 4 * D : n % 4 * D + columns]

    key_bias[:PATCHES, :] = jnp.broadcast_to(bias_of(my_label), (PATCHES, PAIR)).astype(BF16)
    language = own_rows[PATCHES:, :]
    language_bias = bias_of(my_label)
    top_rows = SENT - USED
    for j in range(1, VIEWS):
        ahead = my_view + j < VIEWS
        holds = lax.rem(my_view + j, VIEWS) == 0

        def either(first, rows, columns=D):
            return jnp.where(
                ahead, block_at(4 + j, first, rows, columns), block_at(j - 1, first, rows, columns)
            )

        project_keys(j * PATCHES, PATCHES, either(top_rows, PATCHES))
        bias = bias_of(either(0, top_rows, PAIR).astype(F32))
        rows = slice(j * PATCHES, (j + 1) * PATCHES)
        key_bias[rows, :] = jnp.broadcast_to(bias, (PATCHES, PAIR)).astype(BF16)
        language = jnp.where(holds, either(top_rows + PATCHES, TAIL), language)
        language_bias = jnp.where(holds, bias, language_bias)
    project_keys(VIEWS * PATCHES, TAIL, language)
    index = lax.broadcasted_iota(jnp.int32, (TAIL, PAIR), 0)
    key_bias[VIEWS * PATCHES : KEYS, :] = jnp.where(
        index < LANG, jnp.broadcast_to(language_bias, (TAIL, PAIR)), NEGATIVE
    ).astype(BF16)
    normed_all[KEYS:, :] = jnp.zeros((KEYS_PADDED - KEYS, D), BF16)
    keyval[KEYS:, :] = jnp.zeros((KEYS_PADDED - KEYS, 2 * D), BF16)
    key_bias[KEYS:, :] = jnp.full((KEYS_PADDED - KEYS, PAIR), NEGATIVE, BF16)

    lane = lax.broadcasted_iota(jnp.int32, (1, PAIR), 1)
    low_half = lane < HEAD_DIM

    def half_of(half, first, second):
        return jnp.where(low_half, first, second) if half == 0 else jnp.where(low_half, second, first)

    def head_keys(p, half):
        pair = keyval[:, pl.ds(pl.multiple_of(p * PAIR, PAIR), PAIR)]
        return half_of(half, pair, key_bias[...])

    def head_values(p, half):
        pair = keyval[:, pl.ds(pl.multiple_of(D + p * PAIR, PAIR), PAIR)]
        return half_of(half, pair, jnp.ones((), BF16))

    def spill(p, half):
        return pltpu.make_async_copy(
            weights.at[2 * lax.rem(p, 2) + half, pl.ds(0, USED), :], spilled.at[2 * p + half], spill_sem.at[lax.rem(p, 2), half]
        )

    def unspill(p, half):
        return pltpu.make_async_copy(
            spilled.at[2 * p + half], weights.at[2 * lax.rem(p, 2) + half, pl.ds(0, USED), :], spill_sem.at[lax.rem(p, 2), half]
        )

    def forward_pair(p, _):
        columns = pl.ds(pl.multiple_of(p * PAIR, PAIR), PAIR)
        pair = query[:, columns]
        outs = []
        totals = []

        def settle():
            for half in range(2):
                spill(p - 1, half).wait()

        pl.when(jnp.logical_and(p >= 1, p < 3))(settle)
        scores = []
        for half in range(2):
            one = (lane == HEAD_DIM * (1 - half)).astype(BF16)
            scores.append(dot(half_of(half, pair, one), head_keys(p, half), NT))
        for half in range(2):
            top = jnp.max(scores[half], -1, keepdims=True)
            weight = jnp.exp(scores[half] - top).astype(BF16)
            weights[2 * lax.rem(p, 2) + half, :USED, :] = weight
            out = dot(weight, head_values(p, half), NN)
            outs.append(out)
            totals.append(pltpu.roll(out, HEAD_DIM, 1))
        inv = 1.0 / jnp.where(low_half, totals[0], totals[1])
        full = jnp.where(low_half, outs[0], outs[1]) * inv
        inverse[:, columns] = inv
        mixed_full[:, columns] = full
        mixed[:, columns] = full.astype(BF16)

        def save():
            for half in range(2):
                spill(p, half).start()

        pl.when(p < 2)(save)
        return 0

    lax.fori_loop(0, PAIRS, forward_pair, 0)

    row = lax.broadcasted_iota(jnp.int32, (USED, PAIR), 0)
    has_language = (my_view == 0).astype(jnp.int32)
    live_rows = my_filled * (PATCHES + LANG * has_language)
    live = (row < live_rows).astype(F32)[:, :1]
    res = tokens[:USED, :].astype(F32) + live * dot(mixed[...], w_output[...], NN)
    residual[...] = res
    unit_m, scale_m = normalise(res)
    normed_mlp[...] = (unit_m * gain_m + shift_m).astype(BF16)
    upstream = cotangent[:USED, :].astype(F32)
    branch_grad[...] = (live * upstream).astype(BF16)
    branch[...] = jnp.zeros((USED, D), F32)
    mlp_back[...] = jnp.zeros((USED, D), F32)
    for copy in weight_copies():
        copy.wait()

    def feed_forward(c, _):
        up = arena[c]
        down = arena[blocks + c]
        before = dot(normed_mlp[...], up, NN) + vectors[pl.ds(c, 1), :]
        chance = 0.5 + 0.5 * lax.erf(before * 0.5**0.5)
        density = jnp.exp(-0.5 * before * before) * 0.3989422804014327
        activated = (before * chance).astype(BF16)
        slope = chance + before * density
        start = pl.multiple_of(2 * c * D, D)
        grads[pl.ds(start, D), :] = dot(activated, branch_grad[...], TN).astype(BF16)
        branch[...] += dot(activated, down, NN)
        if fine:
            tick(2 * c)
        before_full = dot(branch_grad[...], down, NT) * slope
        before_grad = before_full.astype(BF16)
        sums_out[pl.ds(c, 1), :] = jnp.sum(before_grad.astype(F32), 0, keepdims=True)
        grads[pl.ds(start + D, D), :] = dot(normed_mlp[...], before_grad, TN).astype(BF16)
        mlp_back[...] += dot(before_grad, up, NT)
        if fine:
            tick(2 * c + 1)
        return 0

    lax.fori_loop(0, blocks, feed_forward, 0)
    block_output[:USED, :] = (residual[...] + live * (branch[...] + vectors[4:5, :])).astype(BF16)
    block_output[USED:, :] = tokens[USED:, :]
    unit_m, scale_m = normalise(residual[...])
    back = mlp_back[...]
    sums_out[4:5, :] = jnp.sum(branch_grad[...].astype(F32), 0, keepdims=True)
    sums_out[5:6, :] = jnp.sum(back * unit_m, 0, keepdims=True)
    sums_out[6:7, :] = jnp.sum(back, 0, keepdims=True)
    res_grad = upstream + norm_backward(back, unit_m, scale_m, gain_m)
    grad_tokens[:USED, :] = res_grad
    grad_tokens[USED:, :] = cotangent[USED:, :].astype(F32)
    attended_grad = (live * res_grad).astype(BF16)
    base = 2 * FF
    out_grad = dot(mixed[...], attended_grad, TN).astype(BF16)
    for i in range(PAIRS):
        grads[base + i * D : base + i * D + PAIR, :] = out_grad[i * PAIR : (i + 1) * PAIR, :]
    mixed_grad[...] = dot(attended_grad, w_output[...], NT).astype(BF16)

    branch[...] = jnp.zeros((USED, D), F32)

    def backward_pair(i, _):
        p = PAIRS - 1 - i
        columns = pl.ds(pl.multiple_of(p * PAIR, PAIR), PAIR)
        grad = mixed_grad[:, columns].astype(F32)
        inv = inverse[:, columns]
        scaled = grad * inv
        product = scaled * mixed_full[:, columns]
        scaled_low = scaled.astype(BF16)
        scaled_t = scaled.T.astype(BF16)
        query_t = query[:, columns].astype(F32).T.astype(BF16)
        query_parts = []
        start = pl.multiple_of(p * PAIR, PAIR)

        def settle():
            for half in range(2):
                unspill(p, half).wait()

        pl.when(p < 2)(settle)
        for half in range(2):
            here = low_half if half == 0 else jnp.logical_not(low_half)
            dots = -jnp.sum(jnp.where(here, product, 0.0), -1, keepdims=True)
            dots_high = dots.astype(BF16)
            dots_low = (dots - dots_high.astype(F32)).astype(BF16)
            other = HEAD_DIM * (1 - half)
            rest = jnp.where(
                lane == other, dots_high, jnp.where(lane == other + 1, dots_low, jnp.zeros((), BF16))
            )
            weight = weights[2 * lax.rem(p, 2) + half, :USED, :]
            slope = dot(half_of(half, scaled_low, rest), head_values(p, half), NT)
            score_grad = weight * slope.astype(BF16)
            query_parts.append(dot(score_grad, head_keys(p, half), NN))
            rows = slice(half * HEAD_DIM, (half + 1) * HEAD_DIM)
            at = start + half * HEAD_DIM
            keyval_grad[pl.ds(at, HEAD_DIM), :] = dot(query_t[rows, :], score_grad, NN).astype(BF16)
            keyval_grad[pl.ds(D + at, HEAD_DIM), :] = dot(scaled_t[rows, :], weight, NN).astype(BF16)
            if fine and half == 0:
                run_ticks(2 * blocks + 2 * BESIDE * i, 2 * blocks + 2 * BESIDE * i + BESIDE)

        def load():
            for half in range(2):
                unspill(p - 2, half).start()

        pl.when(p >= 2)(load)
        part = jnp.where(low_half, query_parts[0], query_parts[1]) * HEAD_DIM**-0.5
        query_grad = part.astype(BF16)
        at = pl.multiple_of(base + i * D, D)
        grads[pl.ds(at + PAIR, PAIR), :] = dot(query_grad, query_norm[...], TN).astype(BF16)
        for c in range(2):
            of_pair = keyval_grad[pl.ds(c * D + start, PAIR), :]
            grads[pl.ds(at + (2 + c) * PAIR, PAIR), :] = dot(of_pair, normed_all[...], NN).astype(
                BF16
            )
        branch[...] += dot(query_grad, w_query[:, columns], NT)
        if fine:
            run_ticks(2 * blocks + 2 * BESIDE * i + BESIDE, 2 * blocks + 2 * BESIDE * (i + 1))
        return 0

    lax.fori_loop(0, PAIRS, backward_pair, 0)

    from_query = branch[...]
    normed = query_norm[...].astype(F32)
    shift_sum = jnp.sum(from_query, 0, keepdims=True)
    gain_sum = jnp.sum(from_query * normed, 0, keepdims=True)

    def parts_at(j):
        return weights.at[0, :USED, (j - 1) * D : j * D]

    for j in range(VIEWS + 1):
        rows = slice(j * PATCHES, min((j + 1) * PATCHES, KEYS))
        piece = dot(keyval_grad[:, rows], w_keyval[...], TT)
        normed = normed_all[rows, :].astype(F32)
        shift_sum += jnp.sum(piece, 0, keepdims=True)
        gain_sum += jnp.sum(piece * normed, 0, keepdims=True)
        if j == 0:
            branch[:PATCHES, :] += piece
        elif j < VIEWS:
            parts_at(j)[:PATCHES, :] = piece.astype(BF16)
        else:
            branch[PATCHES:, :] += jnp.where(my_view == 0, piece, 0.0)
            for i in range(1, VIEWS):
                holds = lax.rem(my_view + i, VIEWS) == 0
                parts_at(i)[PATCHES:, :] = jnp.where(holds, piece, 0.0).astype(BF16)
    sums_out[7:8, :] = (gain_sum - shift_a * shift_sum) / gain_a
    sums_out[8:9, :] = shift_sum
    sums_out[9:, :] = jnp.zeros((SUMS - 9, D), F32)

    def part_for(offset):
        slot = lax.rem(offset + VIEWS, VIEWS) - 1
        at = my_view + offset
        valid = jnp.logical_and(at >= 0, at < VIEWS)
        value = jnp.zeros((USED, D), BF16)
        for n in range(VIEWS - 1):
            value = jnp.where(jnp.logical_and(valid, slot == n), parts_at(n + 1)[...], value)
        return value

    def swap(n):
        return pltpu.make_async_remote_copy(
            arena.at[n, pl.ds(0, USED), :],
            arena.at[4 + n, pl.ds(0, USED), :],
            swap_sem.at[0, n],
            swap_sem.at[1, n],
            sibling,
            MESH,
        )

    back_pieces = ((0, 160), (160, 160), (320, 160))

    def back(kind, slot, target, offset, q):
        first, rows = back_pieces[q]
        n = kind * len(back_pieces) + q
        return pltpu.make_async_remote_copy(
            arena.at[slot, pl.ds(first, rows), :],
            far_in.at[target, pl.ds(first, rows), :],
            far_sem.at[0, n],
            far_sem.at[1, n],
            along(offset),
            MESH,
        )

    def back_relay(q):
        return back(0, 1, 0, 2 * turn, q)

    def back_x(q):
        return back(1, 2, 1, 2 * turn, q)

    def back_up(q):
        return back(2, 3, 2, 4 * turn, q)

    def back_down(q):
        return back(3, 0, 3, -4 * turn, q)

    ticks = 2 * blocks + 2 * BESIDE * PAIRS if fine else 0
    last = ticks + STAGES * SKEW if fine else chunks + STAGES * SKEW

    if not fine:
        run_ticks(0, SKEW + 1)
        ticks = SKEW + 1
    sums_start(0, sums_out[...])
    offsets = (step, step - 2 * turn, step + 2 * turn, -3 * step)
    for n, offset in ((1, offsets[1]), (3, offsets[3]), (2, offsets[2]), (0, offsets[0])):
        arena[n, :USED, :] = part_for(offset)
        swap(n).start()
    pieces = range(len(back_pieces))
    run_ticks(ticks + 0, ticks + 6)
    sums_start(1, sums_finish(0))
    swap(1).wait()
    both = part_for(-2 * turn).astype(F32) + arena[5, :USED, :].astype(F32)
    arena[1, :USED, :] = both.astype(BF16)
    for q in pieces:
        back_relay(q).start()
    run_ticks(ticks + 6, ticks + 8)
    sums_start(2, sums_finish(1))
    swap(0).wait()
    swap(3).wait()
    shared = arena[7, :USED, :].astype(F32)
    arena[0, :USED, :] = (
        part_for(-4 * turn).astype(F32) + jnp.where(step == turn, 0.0, shared)
    ).astype(BF16)
    for q in pieces:
        back_down(q).start()
    arena[3, :USED, :] = (
        part_for(4 * turn).astype(F32) + jnp.where(step == turn, shared, 0.0)
    ).astype(BF16)
    at = slice(0, 160)
    back_relay(0).wait_recv()
    both = arena[3, at, :].astype(F32) + far_in[0, at, :].astype(F32)
    arena[3, at, :] = both.astype(BF16)
    back_up(0).start()
    run_ticks(ticks + 8, ticks + 9)
    at = slice(160, 320)
    back_relay(1).wait_recv()
    both = arena[3, at, :].astype(F32) + far_in[0, at, :].astype(F32)
    arena[3, at, :] = both.astype(BF16)
    back_up(1).start()
    run_ticks(ticks + 9, ticks + 10)
    at = slice(320, 480)
    back_relay(2).wait_recv()
    both = arena[3, at, :].astype(F32) + far_in[0, at, :].astype(F32)
    arena[3, at, :] = both.astype(BF16)
    back_up(2).start()
    sums_start(3, sums_finish(2))
    run_ticks(ticks + 10, ticks + 12)
    swap(2).wait()
    both = part_for(2 * turn).astype(F32) + arena[6, :USED, :].astype(F32)
    arena[2, :USED, :] = both.astype(BF16)
    for q in pieces:
        back_x(q).start()
    run_ticks(ticks + 12, last)
    sums_out[...] = sums_finish(3)
    total = branch[...] + arena[4, :USED, :].astype(F32)
    for q in pieces:
        back_relay(q).wait_send()
        for copy in (back_x(q), back_up(q), back_down(q)):
            copy.wait()
    for n in range(1, 4):
        total += far_in[n].astype(F32)
    unit, scale = normalise(tokens[:USED, :].astype(F32))
    grad_tokens[:USED, :] += norm_backward(total, unit, scale, gain_a)


def stage_copies(stage, size, orders):
    if stage in (0, 7):
        return 1
    return sum(size[order[stage - 1 if stage < 4 else 6 - stage]] - 1 for order in orders)


def main(count, groups, *args):
    depth = count // 4
    part_rows = 2 * groups * depth * SHARD
    parts = 2 if part_rows < D else 1
    chunk_rows = parts * part_rows
    chunks = -(-GRAD_ROWS // chunk_rows)
    shape = jax.ShapeDtypeStruct
    dma = pltpu.SemaphoreType.DMA
    wide = max(groups, depth)
    half = D // 2
    orders = ((2, groups, depth), (groups, 2, depth))[-parts:]
    slots = [sum(order[stage] - 1 for order in orders) for stage in range(3)]
    sems = 2 + 2 * sum(slots)
    held = min(chunks, IN_FLIGHT)
    left = [part_rows // order[0] for order in orders]
    first = max(left)
    second = max(rows // order[1] for rows, order in zip(left, orders))
    scratch = [
        VMEM((KEYS_PADDED, D), BF16),
        VMEM((USED, D), BF16),
        VMEM((KEYS_PADDED, PAIR), BF16),
        VMEM((KEYS_PADDED, 2 * D), BF16),
        VMEM((USED, D), BF16),
        VMEM((4, SENT, KEYS_PADDED), BF16),
        VMEM((USED, D), BF16),
        VMEM((USED, D), F32),
        VMEM((USED, D), F32),
        VMEM((2 * D, KEYS_PADDED), BF16),
        VMEM((USED, D), BF16),
        VMEM((USED, D), BF16),
        VMEM((USED, D), BF16),
        VMEM((USED, D), F32),
        VMEM((USED, D), F32),
        VMEM((USED, D), F32),
        VMEM((SENT, D), BF16),
        VMEM((SUMS, D), F32),
        VMEM((2 * FF // D, D, D), BF16),
        VMEM((chunks * chunk_rows, D), BF16),
        VMEM((held, chunk_rows, half), BF16),
        VMEM((held, slots[0], first, half), BF16),
        VMEM((held, slots[1], second, half), BF16),
        VMEM((held, slots[2], SHARD, half), BF16),
        VMEM((4, USED, D), BF16),
        VMEM((4, wide, SUMS, D), F32),
        dma((4 * len(PIECES) + 4,)),
        dma((4 * len(PIECES) + 4,)),
        dma((2 * FF // D,)),
        dma((2, 2)),
        dma((held, sems)),
        dma((held, sems)),
        dma((held, 2)),
        dma((4, wide)),
        dma((4, wide)),
        dma((2, 4)),
        dma((2, 12)),
    ]
    return pl.pallas_call(
        functools.partial(main_kernel, count, groups, chunks, part_rows),
        out_shape=(
            shape((ROWS, D), BF16),
            shape((ROWS, D), F32),
            shape((chunks * chunk_rows, D), BF16),
            shape((SUMS, D), F32),
            shape((4, USED, KEYS_PADDED), BF16),
        ),
        in_specs=[IN_SMEM] * 4 + [IN_VMEM] * 11 + [ANYWHERE] * 2,
        out_specs=[IN_VMEM, IN_VMEM, ANYWHERE, IN_VMEM, ANYWHERE],
        scratch_shapes=scratch,
        compiler_params=pltpu.CompilerParams(
            collective_id=1, has_side_effects=True, vmem_limit_bytes=63 * MIB
        ),
        name="main",
    )(*args)


def widen_kernel(
    summed,
    rows_in,
    grad_in,
    sums,
    down,
    up,
    out,
    query,
    keyval,
    rows_out,
    grad_out,
    grad_bias_up,
    grad_bias_down,
    grad_gain_mlp,
    grad_shift_mlp,
    grad_gain_attn,
    grad_shift_attn,
    narrow,
    wide,
    rows_held,
    grad_held,
    in_sem,
    out_sem,
    pass_sem,
):
    blocks = FF // D
    passes_in = [
        pltpu.make_async_copy(rows_in, rows_held, pass_sem.at[0]),
        pltpu.make_async_copy(grad_in, grad_held, pass_sem.at[1]),
    ]
    passes_out = [
        pltpu.make_async_copy(rows_held, rows_out, pass_sem.at[2]),
        pltpu.make_async_copy(grad_held, grad_out, pass_sem.at[3]),
    ]
    count = 2 * blocks + PAIRS
    loads = [
        pltpu.make_async_copy(summed.at[pl.ds(b * D, D), :], narrow.at[b], in_sem.at[b])
        for b in range(count)
    ]
    for copy in passes_in + loads:
        copy.start()
    for c in range(blocks):
        grad_bias_up[c * D : (c + 1) * D] = sums[c : c + 1, :].reshape(D)
    rest = (grad_bias_down, grad_gain_mlp, grad_shift_mlp, grad_gain_attn, grad_shift_attn)
    for n, target in enumerate(rest):
        target[...] = sums[blocks + n : blocks + n + 1, :].reshape(D)
    for copy in passes_in:
        copy.wait()
    for copy in passes_out:
        copy.start()
    stores = []

    def store(b, source, target):
        stores.append(pltpu.make_async_copy(source, target, out_sem.at[len(stores)]))
        stores[-1].start()

    for b in range(count):
        loads[b].wait()
        c = b // 2
        if b < 2 * blocks:
            wide[b] = narrow[b].astype(F32)
            at = pl.ds(c * D, D)
            store(b, wide.at[b], down.at[at, :] if b % 2 == 0 else up.at[:, at])
        else:
            i = b - 2 * blocks
            p = PAIRS - 1 - i
            wide[b, :PAIR, :] = narrow[b, :PAIR, :].astype(F32)
            store(b, wide.at[b, pl.ds(0, PAIR), :], out.at[pl.ds(i * PAIR, PAIR), :])
            base = 2 * blocks + PAIRS
            for n, (target, column) in enumerate(((query, p), (keyval, p), (keyval, PAIRS + p))):
                piece = narrow[b, (n + 1) * PAIR : (n + 2) * PAIR, :].astype(F32).T
                columns = slice(p * PAIR, (p + 1) * PAIR)
                wide[base + n, :, columns] = piece
                store(
                    b,
                    wide.at[base + n, :, pl.ds(p * PAIR, PAIR)],
                    target.at[:, pl.ds(column * PAIR, PAIR)],
                )
    for copy in stores + passes_out:
        copy.wait()


def widen(summed, rows, grad, sums):
    blocks = 2 * FF // D + PAIRS
    shape = jax.ShapeDtypeStruct
    dma = pltpu.SemaphoreType.DMA
    return pl.pallas_call(
        widen_kernel,
        out_shape=(
            shape((FF, D), F32),
            shape((D, FF), F32),
            shape((D, D), F32),
            shape((D, D), F32),
            shape((D, 2 * D), F32),
            shape(rows.shape, rows.dtype),
            shape(grad.shape, grad.dtype),
            shape((FF,), F32),
        )
        + (shape((D,), F32),) * 5,
        in_specs=[ANYWHERE] * 3 + [IN_VMEM],
        out_specs=[ANYWHERE] * 7 + [IN_VMEM] * 6,
        scratch_shapes=[
            VMEM((blocks, D, D), BF16),
            VMEM((blocks + 3, D, D), F32),
            VMEM(rows.shape, rows.dtype),
            VMEM(grad.shape, grad.dtype),
            dma((blocks,)),
            dma((blocks + 3 * PAIRS,)),
            dma((4,)),
        ],
        compiler_params=pltpu.CompilerParams(vmem_limit_bytes=60 * MIB),
        name="widen",
    )(summed, rows, grad, sums)


def on_device(
    count,
    groups,
    tokens,
    counts,
    slot_item,
    slot_view,
    keyframe,
    w_query,
    w_keyval,
    w_output,
    w_up,
    bias_up,
    w_down,
    bias_down,
    gain_attn,
    shift_attn,
    gain_mlp,
    shift_mlp,
    cotangent,
):
    block_output, grad_tokens, summed, sums, _ = main(
        count,
        groups,
        counts.reshape(1),
        slot_item.reshape(1),
        slot_view.reshape(1),
        keyframe.reshape(1),
        tokens.reshape(ROWS, D),
        cotangent.reshape(ROWS, D),
        w_query,
        w_keyval,
        w_output,
        bias_up,
        bias_down,
        gain_attn,
        shift_attn,
        gain_mlp,
        shift_mlp,
        w_up,
        w_down,
    )
    down, up, out, query, keyval, block_output, grad_tokens, *small = widen(
        summed, block_output, grad_tokens, sums
    )
    grad_bias_up, grad_bias_down, gain_mlp, shift_mlp, gain_attn, shift_attn = small
    return (
        block_output.reshape(tokens.shape),
        grad_tokens.reshape(tokens.shape),
        query,
        keyval,
        out,
        up,
        grad_bias_up,
        down,
        grad_bias_down,
        gain_attn,
        shift_attn,
        gain_mlp,
        shift_mlp,
    )


def solution(mesh):
    count = mesh.shape["view"]
    groups = mesh.shape["dp"]
    slots = P("dp", "view", None)
    rows = P("dp", "view", None, None, None)
    in_specs = (rows, P("dp", "view"), slots, slots, slots) + (P(),) * 11 + (rows,)
    out_specs = (rows, rows) + (P(),) * 11
    return jax.shard_map(
        functools.partial(on_device, count, groups),
        mesh=mesh,
        in_specs=in_specs,
        out_specs=out_specs,
        check_vma=False,
    )
```

```python
import functools

import jax
import jax.numpy as jnp
from jax import lax
from jax.experimental import pallas as pl
from jax.experimental.pallas import tpu as pltpu
from jax.sharding import PartitionSpec as P

D = 512
HEADS = 8
HEAD_DIM = 64
PAIRS = HEADS // 2
PAIR = 2 * HEAD_DIM
VIEWS = 5
PATCHES = 400
LANG = 77
ROWS = 512
USED = 480
TAIL = USED - PATCHES
SENT = 496
KEYS = VIEWS * PATCHES + TAIL
KEYS_PADDED = 2176
FF = 2048
FF_BLOCK = 512
NEGATIVE = -1e30
EPSILON = 1e-5
GRAD_ROWS = 2 * FF + 4 * D
SUMS = 16
SHARD = 16
STAGES = 8
SKEW = 2
IN_FLIGHT = 4
LQ = 1
READY = (10, 12, 16)
PIECES = ((0, 128), (128, 144), (272, 144))
MAIN = SENT - TAIL

BF16 = jnp.bfloat16
F32 = jnp.float32
MESH = pl.DeviceIdType.MESH
NN = (((1,), (0,)), ((), ()))
NT = (((1,), (1,)), ((), ()))
TN = (((0,), (0,)), ((), ()))
TT = (((0,), (1,)), ((), ()))
MIB = 2**20

VMEM = pltpu.VMEM
IN_VMEM = pl.BlockSpec(memory_space=pltpu.VMEM)
IN_SMEM = pl.BlockSpec(memory_space=pltpu.SMEM)
ANYWHERE = pl.BlockSpec(memory_space=pl.ANY)


def dot(left, right, dims):
    return lax.dot_general(left, right, dims, preferred_element_type=F32)


def normalise(values):
    average = jnp.mean(values, -1, keepdims=True)
    centered = values - average
    variance = jnp.mean(centered * centered, -1, keepdims=True)
    scale = lax.rsqrt(variance + EPSILON)
    return centered * scale, scale


def norm_backward(grad, unit, scale, gain):
    grad = grad * gain
    first = jnp.mean(grad, -1, keepdims=True)
    second = jnp.mean(grad * unit, -1, keepdims=True)
    return scale * (grad - first - unit * second)


def greet(others):
    barrier = pltpu.get_barrier_semaphore()
    for other in others:
        pl.semaphore_signal(barrier, inc=1, device_id=other, device_id_type=MESH)
    pl.semaphore_wait(barrier, len(others))


def main_kernel(
    count,
    groups,
    chunks,
    part_rows,
    counts,
    slot_item,
    slot_view,
    keyframe,
    tokens,
    w_query,
    w_keyval,
    bias_up,
    bias_down,
    gain_attn,
    shift_attn,
    gain_mlp,
    shift_mlp,
    w_up,
    w_down,
    cotangent_in,
    w_output_in,
    block_output,
    grad_tokens,
    summed,
    sums_out,
    normed_all,
    query_norm,
    key_bias,
    keyval,
    query,
    weights,
    mixed,
    mixed_full,
    inverse,
    keyval_grad,
    branch_grad,
    branch,
    mlp_back,
    sent,
    vectors,
    arena,
    grads,
    arrived_core,
    arrived_first,
    arrived_second,
    arrived_last,
    far_in,
    sums_at,
    there_sem,
    here_sem,
    weight_sem,
    send_sem,
    recv_sem,
    local_sem,
    sums_send,
    sums_recv,
    swap_sem,
    far_sem,
):
    me = lax.axis_index("view")
    group = lax.axis_index("dp")
    depth = count // 4
    core = lax.rem(me, 2)
    step = 1 - 2 * core
    place = {"x": lax.rem(me // 2, 2), "y": group, "z": me // 4}
    size = {"x": 2, "y": groups, "z": depth}
    orders = (("x", "y", "z"), ("y", "x", "z"))[-(2 if part_rows < D else 1) :]
    chunk_rows = len(orders) * part_rows
    fine = chunk_rows == D
    arrived = (arrived_first, arrived_second, arrived_last)

    def peer(dim, j):
        at = lax.rem(place[dim] + j, size[dim])
        if dim == "x":
            return {"view": me + 2 * (at - place["x"])}
        if dim == "y":
            return {"dp": at}
        return {"view": me + 4 * (at - place["z"])}

    def along(offset):
        return {"view": lax.rem(me + offset + count, count)}

    sibling = {"view": me + step}

    def window_at(offset, first, rows):
        n = VIEWS - 1 + offset
        columns = pl.ds(pl.multiple_of(lax.rem(n, 4) * D, D), D)
        return weights.at[n // 4, pl.ds(first, rows), columns]

    def weight_copies():
        blocks = FF // D
        return [
            pltpu.make_async_copy(
                w_up.at[:, pl.ds(c * D, D)], arena.at[c], weight_sem.at[c]
            )
            for c in range(blocks)
        ] + [
            pltpu.make_async_copy(
                w_down.at[pl.ds(c * D, D), :], arena.at[blocks + c], weight_sem.at[blocks + c]
            )
            for c in range(blocks)
        ] + [
            pltpu.make_async_copy(cotangent_in, cotangent, weight_sem.at[2 * blocks]),
            pltpu.make_async_copy(w_output_in, w_output, weight_sem.at[2 * blocks + 1]),
        ]

    cotangent = keyval_grad.at[pl.ds(0, ROWS), pl.ds(0, D)]
    w_output = keyval_grad.at[pl.ds(0, D), pl.ds(D, D)]
    for copy in weight_copies():
        copy.start()
    my_view = slot_view[0]
    is_filled = jnp.logical_and(
        jnp.logical_and(counts[0] > 0, keyframe[0] == 1), slot_item[0] >= 0
    )
    my_filled = is_filled.astype(jnp.int32)
    label_here = jnp.where(is_filled, slot_item[0], -1).astype(F32)
    sent[: SENT - USED, :] = jnp.full((SENT - USED, D), label_here, F32).astype(BF16)
    sent[SENT - USED :, :] = tokens[:USED, :]
    peers = [peer(dim, j) for dim in "xyz" for j in range(1, size[dim])]
    greet([sibling] + peers)

    turn = 1 - 2 * place["x"]

    def hop(kind, source, offset, first, rows, device):
        return pltpu.make_async_remote_copy(
            source,
            window_at(offset, first, rows),
            there_sem.at[kind],
            here_sem.at[kind],
            device,
            MESH,
        )

    pieces_all = PIECES + ((MAIN, TAIL),)
    tail = len(PIECES)

    def piece_kind(line, q):
        return line * len(pieces_all) + q

    def along_z(line, q):
        first, rows = pieces_all[q]
        ahead = 4 - 8 * line
        source = sent.at[pl.ds(first, rows), :]
        return hop(piece_kind(line, q), source, -ahead, first, rows, along(ahead))

    def relay_x(q):
        first, rows = pieces_all[q]
        source = window_at(4 * turn, first, rows)
        return hop(piece_kind(2, q), source, 2 * turn, first, rows, along(2 * turn))

    def across_relayed(q):
        first, rows = pieces_all[q]
        source = window_at(-2 * turn, first, rows)
        return hop(piece_kind(3, q), source, -2 * turn - step, first, rows, sibling)

    def direct_x(lang):
        first, rows = (MAIN, TAIL) if lang else (0, MAIN)
        source = sent.at[pl.ds(first, rows), :]
        return hop(piece_kind(4, lang), source, -2 * turn, first, rows, along(2 * turn))

    def across_x(lang):
        first, rows = (MAIN, TAIL) if lang else (0, MAIN)
        source = window_at(2 * turn, first, rows)
        return hop(piece_kind(4, 2 + lang), source, 2 * turn - step, first, rows, sibling)

    def across_z(lang):
        first, rows = (MAIN, TAIL) if lang else (0, MAIN)
        source = window_at(4 * step, first, rows)
        return hop(piece_kind(5, lang), source, 3 * step, first, rows, sibling)

    across_own = hop(piece_kind(5, 2), sent, -step, 0, SENT, sibling)
    forth = turn > 0
    back_turn = turn < 0
    for q in range(tail):
        for line in range(2):
            along_z(line, q).start()
    along_z(0, tail).start()
    direct_x(0).start()
    pl.when(forth)(lambda: direct_x(1).start())
    across_own.start()

    levels = []
    for order in orders:
        rows = part_rows
        offset = 0
        level = [(0, rows)]
        for dim in order:
            rows = rows // size[dim]
            offset = offset + place[dim] * rows
            level.append((offset, rows))
        levels.append(level)
    own_columns = pl.ds(pl.multiple_of(core * (D // 2), D // 2), D // 2)
    other_columns = pl.ds(pl.multiple_of((1 - core) * (D // 2), D // 2), D // 2)

    def slot_of(stage, p, j):
        slot = j - 1
        for order in orders[:p]:
            slot += size[order[stage - 1]] - 1
        return slot

    def rows_of(k, p, offset, rows):
        return pl.ds(pl.multiple_of(k * chunk_rows + p * part_rows + offset, SHARD), rows)

    def held(k):
        return lax.rem(k, IN_FLIGHT)

    first_sem = [0]
    for stage in range(STAGES):
        first_sem.append(first_sem[-1] + stage_copies(stage, size, orders))

    def copies(stage, k):
        out = []

        def add(source, target, device):
            n = first_sem[stage] + len(out)
            out.append(
                pltpu.make_async_remote_copy(
                    source, target, send_sem.at[held(k), n], recv_sem.at[held(k), n], device, MESH
                )
            )

        if stage == 0:
            add(grads.at[rows_of(k, 0, 0, chunk_rows), other_columns], arrived_core.at[held(k)], sibling)
        elif stage == 7:
            whole = summed.at[rows_of(k, 0, 0, chunk_rows), own_columns]
            add(whole, whole, sibling)
        for p, order in enumerate(orders):
            if 0 < stage < 4:
                dim = order[stage - 1]
                offset, _ = levels[p][stage - 1]
                _, rows = levels[p][stage]
                for j in range(1, size[dim]):
                    at = offset + lax.rem(place[dim] + j, size[dim]) * rows
                    add(
                        grads.at[rows_of(k, p, at, rows), own_columns],
                        arrived[stage - 1].at[held(k), slot_of(stage, p, j), pl.ds(0, rows), :],
                        peer(dim, j),
                    )
            elif 4 <= stage < 7:
                dim = order[6 - stage]
                offset, rows = levels[p][7 - stage]
                at = rows_of(k, p, offset, rows)
                source = grads if stage == 4 else summed
                for j in range(1, size[dim]):
                    add(source.at[at, own_columns], summed.at[at, own_columns], peer(dim, j))
        return out

    def own_shard(k, p):
        at = rows_of(k, p, *levels[p][3])
        return pltpu.make_async_copy(
            grads.at[at, own_columns], summed.at[at, own_columns], local_sem.at[held(k), p]
        )

    def start_stage(stage, k):
        for copy in copies(stage, k):
            copy.start()
        if stage == 4:
            for p in range(len(orders)):
                own_shard(k, p).start()

    def finish_stage(stage, k):
        for copy in copies(stage, k):
            copy.wait()
        if stage == 4:
            for p in range(len(orders)):
                own_shard(k, p).wait()
        if stage == 0:
            at = rows_of(k, 0, 0, chunk_rows)
            total = grads[at, own_columns].astype(F32) + arrived_core[held(k)].astype(F32)
            grads[at, own_columns] = total.astype(BF16)
        elif stage < 4:
            for p, order in enumerate(orders):
                offset, rows = levels[p][stage]
                at = rows_of(k, p, offset, rows)
                total = grads[at, own_columns].astype(F32)
                for j in range(1, size[order[stage - 1]]):
                    total += arrived[stage - 1][held(k), slot_of(stage, p, j), :rows, :].astype(F32)
                grads[at, own_columns] = total.astype(BF16)

    blocks = FF // D

    def tick(t):
        for stage in range(STAGES, -1, -1):
            at = t - SKEW * stage
            if fine:
                early = jnp.logical_and(at >= 0, at <= 2 * blocks)
                valid = early
                k = at
                for n, ready in enumerate(READY):
                    now = at == ready
                    valid = jnp.logical_or(valid, now)
                    k = jnp.where(now, 2 * blocks + 1 + n, k)
            else:
                k = at
                valid = jnp.logical_and(at >= 0, at < chunks)

            def go(stage=stage, k=k):
                if stage > 0:
                    finish_stage(stage - 1, k)
                if stage < STAGES:
                    start_stage(stage, k)

            pl.when(valid)(go)

    def run_ticks(first, end):
        def body(t, _):
            tick(t)
            return 0

        lax.fori_loop(first, end, body, 0)

    sums_dims = ("core", "x", "y", "z")

    def sums_copies(level):
        dim = sums_dims[level]
        if dim == "core":
            targets, mine = [sibling], core
        else:
            targets, mine = [peer(dim, j) for j in range(1, size[dim])], place[dim]
        return [
            pltpu.make_async_remote_copy(
                sums_at.at[level, mine],
                sums_at.at[level, mine],
                sums_send.at[level, n],
                sums_recv.at[level, n],
                device,
                MESH,
            )
            for n, device in enumerate(targets)
        ]

    def sums_start(level, value):
        dim = sums_dims[level]
        sums_at[level, core if dim == "core" else place[dim]] = value
        for copy in sums_copies(level):
            copy.start()

    def sums_finish(level):
        for copy in sums_copies(level):
            copy.wait()
        dim = sums_dims[level]
        total = sums_at[level, 0]
        for i in range(1, 2 if dim == "core" else size[dim]):
            total += sums_at[level, i]
        return total

    for c in range(blocks):
        vectors[c : c + 1, :] = bias_up[c * D : (c + 1) * D].astype(F32).reshape(1, D)
    for n, vector in enumerate((bias_down, gain_attn, shift_attn, gain_mlp, shift_mlp)):
        vectors[4 + n : 5 + n, :] = vector[...].astype(F32).reshape(1, D)
    gain_a = vectors[5:6, :]
    shift_a = vectors[6:7, :]
    gain_m = vectors[7:8, :]
    shift_m = vectors[8:9, :]

    def project_keys(first, rows, values):
        unit, _ = normalise(values.astype(F32))
        normed = (unit * gain_a + shift_a).astype(BF16)
        normed_all[first : first + rows, :] = normed
        keyval[first : first + rows, :] = dot(normed, w_keyval[...], NN).astype(BF16)

    own_rows = tokens[:USED, :]
    own_unit, _ = normalise(own_rows.astype(F32))
    query_norm[...] = (own_unit * gain_a + shift_a).astype(BF16)
    query[...] = (dot(query_norm[...], w_query[...], NN).astype(BF16) * HEAD_DIM**-0.5).astype(BF16)
    project_keys(0, PATCHES, own_rows[:PATCHES, :])
    relayed = jnp.where(forth, 1, 0)
    for q in range(tail):
        along_z(relayed, q).wait_recv()
        relay_x(q).start()

    def relay_tail():
        along_z(0, tail).wait_recv()
        relay_x(tail).start()

    pl.when(back_turn)(relay_tail)
    direct_x(0).wait_recv()
    across_x(0).start()

    def pass_tail_x():
        direct_x(1).wait_recv()
        across_x(1).start()

    pl.when(back_turn)(pass_tail_x)
    for q in range(tail):
        along_z(1 - relayed, q).wait_recv()
    pl.when(forth)(lambda: along_z(0, tail).wait_recv())
    across_z(0).start()
    pl.when(step < 0)(lambda: across_z(1).start())
    for q in range(tail):
        relay_x(q).wait_recv()
        across_relayed(q).start()

    def pass_tail_relayed():
        relay_x(tail).wait_recv()
        across_relayed(tail).start()

    pl.when(forth)(pass_tail_relayed)
    for copy in (across_own, across_x(0), across_z(0)):
        copy.wait()
    direct_x(0).wait_send()
    for q in range(tail):
        for line in range(2):
            along_z(line, q).wait_send()
        relay_x(q).wait_send()
        across_relayed(q).wait()
    along_z(0, tail).wait_send()

    def settle_forth():
        direct_x(1).wait_send()
        across_relayed(tail).wait()

    def settle_back():
        relay_x(tail).wait_send()
        across_x(1).wait()

    pl.when(forth)(settle_forth)
    pl.when(back_turn)(settle_back)
    pl.when(step < 0)(lambda: across_z(1).wait_send())
    pl.when(step > 0)(lambda: across_z(1).wait_recv())
    my_label = sent[: SENT - USED, :PAIR].astype(F32)

    def bias_of(label):
        match = jnp.logical_and(label == my_label, label >= 0)
        return jnp.where(match, 0.0, NEGATIVE)[:1, :]

    def block_at(n, first, rows, columns=D):
        return weights[n // 4, first : first + rows, n % 4 * D : n % 4 * D + columns]

    key_bias[:PATCHES, :] = jnp.broadcast_to(bias_of(my_label), (PATCHES, PAIR)).astype(BF16)
    language = own_rows[PATCHES:, :]
    language_bias = bias_of(my_label)
    top_rows = SENT - USED
    for j in range(1, VIEWS):
        ahead = my_view + j < VIEWS
        holds = lax.rem(my_view + j, VIEWS) == 0

        def either(first, rows, columns=D):
            return jnp.where(
                ahead, block_at(4 + j, first, rows, columns), block_at(j - 1, first, rows, columns)
            )

        project_keys(j * PATCHES, PATCHES, either(top_rows, PATCHES))
        bias = bias_of(either(0, top_rows, PAIR).astype(F32))
        rows = slice(j * PATCHES, (j + 1) * PATCHES)
        key_bias[rows, :] = jnp.broadcast_to(bias, (PATCHES, PAIR)).astype(BF16)
        language = jnp.where(holds, block_at(j - 1, top_rows + PATCHES, TAIL), language)
        language_bias = jnp.where(holds, bias, language_bias)
    project_keys(VIEWS * PATCHES, TAIL, language)
    index = lax.broadcasted_iota(jnp.int32, (TAIL, PAIR), 0)
    key_bias[VIEWS * PATCHES : KEYS, :] = jnp.where(
        index < LANG, jnp.broadcast_to(language_bias, (TAIL, PAIR)), NEGATIVE
    ).astype(BF16)
    normed_all[KEYS:, :] = jnp.zeros((KEYS_PADDED - KEYS, D), BF16)
    keyval[KEYS:, :] = jnp.zeros((KEYS_PADDED - KEYS, 2 * D), BF16)
    key_bias[KEYS:, :] = jnp.full((KEYS_PADDED - KEYS, PAIR), NEGATIVE, BF16)

    lane = lax.broadcasted_iota(jnp.int32, (1, PAIR), 1)
    low_half = lane < HEAD_DIM

    def half_of(half, first, second):
        return jnp.where(low_half, first, second) if half == 0 else jnp.where(low_half, second, first)

    def head_keys(p, half):
        pair = keyval[:, pl.ds(pl.multiple_of(p * PAIR, PAIR), PAIR)]
        return half_of(half, pair, key_bias[...])

    def head_values(p, half):
        pair = keyval[:, pl.ds(pl.multiple_of(D + p * PAIR, PAIR), PAIR)]
        return half_of(half, pair, jnp.ones((), BF16))

    def forward_pair(p, _):
        columns = pl.ds(pl.multiple_of(p * PAIR, PAIR), PAIR)
        pair = query[:, columns]
        outs = []
        totals = []

        scores = []
        for half in range(2):
            one = (lane == HEAD_DIM * (1 - half)).astype(BF16)
            scores.append(dot(half_of(half, pair, one), head_keys(p, half), NT))
        for half in range(2):
            top = jnp.max(scores[half], -1, keepdims=True)
            weight = jnp.exp(scores[half] - top).astype(BF16)
            weights[2 * p + half, :USED, :] = weight
            out = dot(weight, head_values(p, half), NN)
            outs.append(out)
            totals.append(pltpu.roll(out, HEAD_DIM, 1))
        inv = 1.0 / jnp.where(low_half, totals[0], totals[1])
        full = jnp.where(low_half, outs[0], outs[1]) * inv
        inverse[:, columns] = inv
        mixed_full[:, columns] = full
        mixed[:, columns] = full.astype(BF16)

        return 0

    lax.fori_loop(0, PAIRS, forward_pair, 0)

    for copy in weight_copies():
        copy.wait()
    row = lax.broadcasted_iota(jnp.int32, (USED, PAIR), 0)
    has_language = (my_view == 0).astype(jnp.int32)
    live_rows = my_filled * (PATCHES + LANG * has_language)
    live = (row < live_rows).astype(F32)[:, :1]
    res = tokens[:USED, :].astype(F32) + live * dot(mixed[...], w_output[...], NN)
    grad_tokens[:USED, :] = res
    unit_m, scale_m = normalise(res)
    normed_mlp = sent.at[:USED, :]
    normed_mlp[...] = (unit_m * gain_m + shift_m).astype(BF16)
    upstream = cotangent[:USED, :].astype(F32)
    branch_grad[...] = (live * upstream).astype(BF16)
    branch[...] = jnp.zeros((USED, D), F32)
    mlp_back[...] = jnp.zeros((USED, D), F32)

    def feed_forward(c, _):
        up = arena[c]
        down = arena[blocks + c]
        before = dot(normed_mlp[...], up, NN) + vectors[pl.ds(c, 1), :]
        chance = 0.5 + 0.5 * lax.erf(before * 0.5**0.5)
        density = jnp.exp(-0.5 * before * before) * 0.3989422804014327
        activated = (before * chance).astype(BF16)
        slope = chance + before * density
        start = pl.multiple_of(2 * c * D, D)
        grads[pl.ds(start, D), :] = dot(activated, branch_grad[...], TN).astype(BF16)
        branch[...] += dot(activated, down, NN)
        if fine:
            tick(2 * c)
        before_full = dot(branch_grad[...], down, NT) * slope
        before_grad = before_full.astype(BF16)
        sums_out[pl.ds(c, 1), :] = jnp.sum(before_grad.astype(F32), 0, keepdims=True)
        grads[pl.ds(start + D, D), :] = dot(normed_mlp[...], before_grad, TN).astype(BF16)
        mlp_back[...] += dot(before_grad, up, NT)
        if fine:
            tick(2 * c + 1)
        return 0

    lax.fori_loop(0, blocks, feed_forward, 0)
    arena[0, :USED, :] = (grad_tokens[:USED, :] + live * (branch[...] + vectors[4:5, :])).astype(BF16)
    arena[0, USED:, :] = tokens[USED:, :]
    output_copy = pltpu.make_async_copy(arena.at[0], block_output, weight_sem.at[0])
    output_copy.start()
    unit_m, scale_m = normalise(grad_tokens[:USED, :])
    back = mlp_back[...]
    sums_out[4:5, :] = jnp.sum(branch_grad[...].astype(F32), 0, keepdims=True)
    sums_out[5:6, :] = jnp.sum(back * unit_m, 0, keepdims=True)
    sums_out[6:7, :] = jnp.sum(back, 0, keepdims=True)
    res_grad = upstream + norm_backward(back, unit_m, scale_m, gain_m)
    grad_tokens[:USED, :] = res_grad
    grad_tokens[USED:, :] = cotangent[USED:, :].astype(F32)
    attended_grad = (live * res_grad).astype(BF16)
    base = 2 * FF
    grads[base : base + D, :] = dot(mixed[...], attended_grad, TN).astype(BF16)
    mixed_grad = branch_grad
    mixed_grad[...] = dot(attended_grad, w_output[...], NT).astype(BF16)

    branch[...] = jnp.zeros((USED, D), F32)
    if fine:
        tick(2 * blocks)

    def backward_pair(p, _):
        columns = pl.ds(pl.multiple_of(p * PAIR, PAIR), PAIR)
        grad = mixed_grad[:, columns].astype(F32)
        scaled = grad * inverse[:, columns]
        product = scaled * mixed_full[:, columns]
        scaled_low = scaled.astype(BF16)
        scaled_t = scaled.T.astype(BF16)
        query_t = query[:, columns].astype(F32).T.astype(BF16)
        start = pl.multiple_of(p * PAIR, PAIR)
        for half in range(2):
            here = low_half if half == 0 else jnp.logical_not(low_half)
            dots = -jnp.sum(jnp.where(here, product, 0.0), -1, keepdims=True)
            dots_high = dots.astype(BF16)
            dots_low = (dots - dots_high.astype(F32)).astype(BF16)
            other = HEAD_DIM * (1 - half)
            rest = jnp.where(
                lane == other, dots_high, jnp.where(lane == other + 1, dots_low, jnp.zeros((), BF16))
            )
            weight = weights[2 * p + half, :USED, :]
            slope = dot(half_of(half, scaled_low, rest), head_values(p, half), NT)
            score_grad = weight * slope.astype(BF16)
            weights[2 * p + half, :USED, :] = score_grad
            rows = slice(half * HEAD_DIM, (half + 1) * HEAD_DIM)
            at = start + half * HEAD_DIM
            keyval_grad[pl.ds(at, HEAD_DIM), :] = dot(query_t[rows, :], score_grad, NN).astype(BF16)
            keyval_grad[pl.ds(D + at, HEAD_DIM), :] = dot(scaled_t[rows, :], weight, NN).astype(BF16)
        at = pl.multiple_of(base + D + 2 * PAIR * p, 2 * PAIR)
        for c in range(2):
            of_pair = keyval_grad[pl.ds(c * D + start, PAIR), :]
            grads[pl.ds(at + c * PAIR, PAIR), :] = dot(of_pair, normed_all[...], NN).astype(BF16)
        if fine:
            tick(2 * blocks + 1 + p)
        return 0

    lax.fori_loop(0, PAIRS, backward_pair, 0)

    def query_pair(p, _):
        columns = pl.ds(pl.multiple_of(p * PAIR, PAIR), PAIR)
        query_parts = [
            dot(weights[2 * p + half, :USED, :], head_keys(p, half), NN) for half in range(2)
        ]
        part = jnp.where(low_half, query_parts[0], query_parts[1]) * HEAD_DIM**-0.5
        query_grad = part.astype(BF16)
        at = pl.multiple_of(base + 3 * D + p * PAIR, PAIR)
        grads[pl.ds(at, PAIR), :] = dot(query_grad, query_norm[...], TN).astype(BF16)
        branch[...] += dot(query_grad, w_query[:, columns], NT)
        if fine:
            run_ticks(ticks + LQ * p, ticks + LQ * (p + 1))
        return 0

    shift_sum = jnp.zeros((1, D), F32)
    gain_sum = jnp.zeros((1, D), F32)

    def parts_at(j):
        return normed_all.at[(j - 1) * USED : j * USED, :]

    for j in range(VIEWS + 1):
        rows = slice(j * PATCHES, min((j + 1) * PATCHES, KEYS))
        piece = dot(keyval_grad[:, rows], w_keyval[...], TT)
        normed = normed_all[rows, :].astype(F32)
        shift_sum += jnp.sum(piece, 0, keepdims=True)
        gain_sum += jnp.sum(piece * normed, 0, keepdims=True)
        if j == 0:
            mlp_back[:PATCHES, :] = piece
        elif j < VIEWS:
            parts_at(j)[:PATCHES, :] = piece.astype(BF16)
        else:
            mlp_back[PATCHES:, :] = jnp.where(my_view == 0, piece, 0.0)
            for i in range(1, VIEWS):
                holds = lax.rem(my_view + i, VIEWS) == 0
                parts_at(i)[PATCHES:, :] = jnp.where(holds, piece, 0.0).astype(BF16)
    def part_for(offset):
        slot = lax.rem(offset + VIEWS, VIEWS) - 1
        at = my_view + offset
        valid = jnp.logical_and(at >= 0, at < VIEWS)
        value = jnp.zeros((USED, D), BF16)
        for n in range(VIEWS - 1):
            value = jnp.where(jnp.logical_and(valid, slot == n), parts_at(n + 1)[...], value)
        return value

    def swap(n):
        return pltpu.make_async_remote_copy(
            arena.at[n, pl.ds(0, USED), :],
            arena.at[4 + n, pl.ds(0, USED), :],
            swap_sem.at[0, n],
            swap_sem.at[1, n],
            sibling,
            MESH,
        )

    back_pieces = ((0, 144), (144, 128), (272, 128), (PATCHES, TAIL))

    def back(kind, slot, target, offset, q):
        first, rows = back_pieces[q]
        n = kind * len(back_pieces) + q
        return pltpu.make_async_remote_copy(
            arena.at[slot, pl.ds(first, rows), :],
            far_in.at[target, pl.ds(first, rows), :],
            far_sem.at[0, n],
            far_sem.at[1, n],
            along(offset),
            MESH,
        )

    def back_relay(q):
        return back(0, 1, 0, 2 * turn, q)

    def back_x(q):
        return back(1, 2, 1, 2 * turn, q)

    def back_up(q):
        return back(2, 3, 2, 4 * turn, q)

    def back_down(q):
        return back(3, 0, 3, -4 * turn, q)

    ticks = 2 * blocks + 1 + PAIRS if fine else 0
    last = READY[-1] + STAGES * SKEW + 1 if fine else chunks + STAGES * SKEW

    if not fine:
        lax.fori_loop(0, PAIRS, query_pair, 0)
        run_ticks(0, SKEW + 1)
        ticks = SKEW + 1
    output_copy.wait()
    offsets = (step, step - 2 * turn, step + 2 * turn, -3 * step)
    for n, offset in ((1, offsets[1]), (3, offsets[3]), (2, offsets[2]), (0, offsets[0])):
        arena[n, :USED, :] = part_for(offset)
        swap(n).start()
    pieces = range(len(back_pieces) - 1)
    lang = len(back_pieces) - 1
    pieces = range(len(back_pieces) - 1)
    lang = len(back_pieces) - 1
    if fine:
        lax.fori_loop(0, 4, query_pair, 0)
        ticks = ticks + LQ * PAIRS
    from_query = branch[...]
    shift_sum += jnp.sum(from_query, 0, keepdims=True)
    gain_sum += jnp.sum(from_query * query_norm[...].astype(F32), 0, keepdims=True)
    sums_out[7:8, :] = (gain_sum - shift_a * shift_sum) / gain_a
    sums_out[8:9, :] = shift_sum
    sums_out[9:, :] = jnp.zeros((SUMS - 9, D), F32)
    sums_start(0, sums_out[...])
    run_ticks(ticks + 0, ticks + 4)
    sums_start(1, sums_finish(0))
    run_ticks(ticks + 4, ticks + 8)
    swap(1).wait()
    both = part_for(-2 * turn).astype(F32) + arena[5, :USED, :].astype(F32)
    arena[1, :USED, :] = both.astype(BF16)
    for q in pieces:
        back_relay(q).start()
    pl.when(forth)(lambda: back_relay(lang).start())
    swap(0).wait()
    swap(3).wait()
    shared = arena[7, :USED, :].astype(F32)
    arena[0, :USED, :] = (
        part_for(-4 * turn).astype(F32) + jnp.where(step == turn, 0.0, shared)
    ).astype(BF16)
    for q in pieces:
        back_down(q).start()
    pl.when(forth)(lambda: back_down(lang).start())
    arena[3, :USED, :] = (
        part_for(4 * turn).astype(F32) + jnp.where(step == turn, shared, 0.0)
    ).astype(BF16)
    run_ticks(ticks + 8, ticks + 10)
    sums_start(2, sums_finish(1))
    at = slice(0, 144)
    back_relay(0).wait_recv()
    both = arena[3, at, :].astype(F32) + far_in[0, at, :].astype(F32)
    arena[3, at, :] = both.astype(BF16)
    back_up(0).start()
    run_ticks(ticks + 10, ticks + 11)
    at = slice(144, 272)
    back_relay(1).wait_recv()
    both = arena[3, at, :].astype(F32) + far_in[0, at, :].astype(F32)
    arena[3, at, :] = both.astype(BF16)
    back_up(1).start()
    run_ticks(ticks + 11, ticks + 12)
    at = slice(272, 400)
    back_relay(2).wait_recv()
    both = arena[3, at, :].astype(F32) + far_in[0, at, :].astype(F32)
    arena[3, at, :] = both.astype(BF16)
    back_up(2).start()

    def up_lang():
        at = slice(PATCHES, USED)
        back_relay(lang).wait_recv()
        both = arena[3, at, :].astype(F32) + far_in[0, at, :].astype(F32)
        arena[3, at, :] = both.astype(BF16)
        back_up(lang).start()

    pl.when(back_turn)(up_lang)
    sums_start(3, sums_finish(2))
    run_ticks(ticks + 12, ticks + 14)
    swap(2).wait()
    both = part_for(2 * turn).astype(F32) + arena[6, :USED, :].astype(F32)
    arena[2, :USED, :] = both.astype(BF16)
    for q in pieces:
        back_x(q).start()
    pl.when(back_turn)(lambda: back_x(lang).start())
    run_ticks(ticks + 14, last)
    sums_out[...] = sums_finish(3)
    for q in pieces:
        back_relay(q).wait_send()
        for copy in (back_x(q), back_up(q), back_down(q)):
            copy.wait()

    def settle_lang_forth():
        back_relay(lang).wait_send()
        back_down(lang).wait()
        back_x(lang).wait_recv()

    def settle_lang_back():
        back_x(lang).wait_send()
        back_up(lang).wait()

    pl.when(forth)(settle_lang_forth)
    pl.when(back_turn)(settle_lang_back)
    for at, whole in ((slice(0, PATCHES), True), (slice(PATCHES, USED), False)):
        total = branch[at, :] + mlp_back[at, :] + arena[4, at, :].astype(F32)
        for n, came in ((1, forth), (2, back_turn), (3, forth)):
            part = far_in[n, at, :].astype(F32)
            total += part if whole else jnp.where(came, part, 0.0)
        unit, scale = normalise(tokens[at, :].astype(F32))
        grad_tokens[at, :] += norm_backward(total, unit, scale, gain_a)


def stage_copies(stage, size, orders):
    if stage in (0, 7):
        return 1
    return sum(size[order[stage - 1 if stage < 4 else 6 - stage]] - 1 for order in orders)


def main(count, groups, *args):
    depth = count // 4
    part_rows = 2 * groups * depth * SHARD
    parts = 2 if part_rows < D else 1
    chunk_rows = parts * part_rows
    chunks = -(-GRAD_ROWS // chunk_rows)
    shape = jax.ShapeDtypeStruct
    dma = pltpu.SemaphoreType.DMA
    wide = max(groups, depth)
    half = D // 2
    orders = ((2, groups, depth), (groups, 2, depth))[-parts:]
    slots = [sum(order[stage] - 1 for order in orders) for stage in range(3)]
    sems = 2 + 2 * sum(slots)
    held = min(chunks, IN_FLIGHT)
    left = [part_rows // order[0] for order in orders]
    first = max(left)
    second = max(rows // order[1] for rows, order in zip(left, orders))
    scratch = [
        VMEM((KEYS_PADDED, D), BF16),
        VMEM((USED, D), BF16),
        VMEM((KEYS_PADDED, PAIR), BF16),
        VMEM((KEYS_PADDED, 2 * D), BF16),
        VMEM((USED, D), BF16),
        VMEM((HEADS, SENT, KEYS_PADDED), BF16),
        VMEM((USED, D), BF16),
        VMEM((USED, D), F32),
        VMEM((USED, D), F32),
        VMEM((2 * D, KEYS_PADDED), BF16),
        VMEM((USED, D), BF16),
        VMEM((USED, D), F32),
        VMEM((USED, D), F32),
        VMEM((SENT, D), BF16),
        VMEM((SUMS, D), F32),
        VMEM((2 * FF // D, D, D), BF16),
        VMEM((chunks * chunk_rows, D), BF16),
        VMEM((held, chunk_rows, half), BF16),
        VMEM((held, slots[0], first, half), BF16),
        VMEM((held, slots[1], second, half), BF16),
        VMEM((held, slots[2], SHARD, half), BF16),
        VMEM((4, USED, D), BF16),
        VMEM((4, wide, SUMS, D), F32),
        dma((6 * (len(PIECES) + 1),)),
        dma((6 * (len(PIECES) + 1),)),
        dma((2 * FF // D + 2,)),
        dma((held, sems)),
        dma((held, sems)),
        dma((held, 2)),
        dma((4, wide)),
        dma((4, wide)),
        dma((2, 4)),
        dma((2, 16)),
    ]
    return pl.pallas_call(
        functools.partial(main_kernel, count, groups, chunks, part_rows),
        out_shape=(
            shape((ROWS, D), BF16),
            shape((ROWS, D), F32),
            shape((chunks * chunk_rows, D), BF16),
            shape((SUMS, D), F32),
        ),
        in_specs=[IN_SMEM] * 4 + [IN_VMEM] * 9 + [ANYWHERE] * 4,
        out_specs=[ANYWHERE, IN_VMEM, ANYWHERE, IN_VMEM],
        scratch_shapes=scratch,
        compiler_params=pltpu.CompilerParams(
            collective_id=1, has_side_effects=True, vmem_limit_bytes=63 * MIB + (0 if parts == 2 else 800 * 1024)
        ),
        name="main",
    )(*args)


def widen_kernel(
    summed,
    rows_in,
    grad_in,
    sums,
    down,
    up,
    out,
    query,
    keyval,
    rows_out,
    grad_out,
    grad_bias_up,
    grad_bias_down,
    grad_gain_mlp,
    grad_shift_mlp,
    grad_gain_attn,
    grad_shift_attn,
    narrow,
    wide,
    rows_held,
    grad_held,
    in_sem,
    out_sem,
    pass_sem,
):
    blocks = FF // D
    passes_in = [
        pltpu.make_async_copy(rows_in, rows_held, pass_sem.at[0]),
        pltpu.make_async_copy(grad_in, grad_held, pass_sem.at[1]),
    ]
    passes_out = [
        pltpu.make_async_copy(rows_held, rows_out, pass_sem.at[2]),
        pltpu.make_async_copy(grad_held, grad_out, pass_sem.at[3]),
    ]
    count = 2 * blocks + 4
    loads = [
        pltpu.make_async_copy(summed.at[pl.ds(b * D, D), :], narrow.at[b], in_sem.at[b])
        for b in range(count)
    ]
    order = [count - 1, count - 2, count - 3] + list(range(count - 3))
    for b in order:
        loads[b].start()
    for copy in passes_in:
        copy.start()
    for c in range(blocks):
        grad_bias_up[c * D : (c + 1) * D] = sums[c : c + 1, :].reshape(D)
    rest = (grad_bias_down, grad_gain_mlp, grad_shift_mlp, grad_gain_attn, grad_shift_attn)
    for n, target in enumerate(rest):
        target[...] = sums[blocks + n : blocks + n + 1, :].reshape(D)
    stores = []

    def store(b, source, target):
        stores.append(pltpu.make_async_copy(source, target, out_sem.at[len(stores)]))
        stores[-1].start()

    for b in order:
        loads[b].wait()
        c = b // 2
        if b < 2 * blocks:
            wide[b] = narrow[b].astype(F32)
            at = pl.ds(c * D, D)
            store(b, wide.at[b], down.at[at, :] if b % 2 == 0 else up.at[:, at])
        elif b == 2 * blocks:
            wide[b] = narrow[b].astype(F32)
            store(b, wide.at[b], out)
        elif b == 2 * blocks + 3:
            wide[b] = narrow[b].astype(F32).T
            store(b, wide.at[b], query)
        else:
            pairs = 2 * (b - 2 * blocks - 1)
            for n in range(2):
                for c in range(2):
                    first = (2 * n + c) * PAIR
                    at = pl.ds(first, PAIR)
                    wide[b, :, first : first + PAIR] = (
                        narrow[b, first : first + PAIR, :].astype(F32).T
                    )
                    column = c * D + (pairs + n) * PAIR
                    store(b, wide.at[b, :, at], keyval.at[:, pl.ds(column, PAIR)])
    for copy in passes_in:
        copy.wait()
    for copy in passes_out:
        copy.start()
    for copy in stores + passes_out:
        copy.wait()


def widen(summed, rows, grad, sums):
    blocks = GRAD_ROWS // D
    shape = jax.ShapeDtypeStruct
    dma = pltpu.SemaphoreType.DMA
    return pl.pallas_call(
        widen_kernel,
        out_shape=(
            shape((FF, D), F32),
            shape((D, FF), F32),
            shape((D, D), F32),
            shape((D, D), F32),
            shape((D, 2 * D), F32),
            shape(rows.shape, rows.dtype),
            shape(grad.shape, grad.dtype),
            shape((FF,), F32),
        )
        + (shape((D,), F32),) * 5,
        in_specs=[ANYWHERE] * 3 + [IN_VMEM],
        out_specs=[ANYWHERE] * 7 + [IN_VMEM] * 6,
        scratch_shapes=[
            VMEM((blocks, D, D), BF16),
            VMEM((blocks, D, D), F32),
            VMEM(rows.shape, rows.dtype),
            VMEM(grad.shape, grad.dtype),
            dma((blocks,)),
            dma((blocks + 6,)),
            dma((4,)),
        ],
        compiler_params=pltpu.CompilerParams(vmem_limit_bytes=60 * MIB),
        name="widen",
    )(summed, rows, grad, sums)


def on_device(
    count,
    groups,
    tokens,
    counts,
    slot_item,
    slot_view,
    keyframe,
    w_query,
    w_keyval,
    w_output,
    w_up,
    bias_up,
    w_down,
    bias_down,
    gain_attn,
    shift_attn,
    gain_mlp,
    shift_mlp,
    cotangent,
):
    block_output, grad_tokens, summed, sums = main(
        count,
        groups,
        counts.reshape(1),
        slot_item.reshape(1),
        slot_view.reshape(1),
        keyframe.reshape(1),
        tokens.reshape(ROWS, D),
        w_query,
        w_keyval,
        bias_up,
        bias_down,
        gain_attn,
        shift_attn,
        gain_mlp,
        shift_mlp,
        w_up,
        w_down,
        cotangent.reshape(ROWS, D),
        w_output,
    )
    down, up, out, query, keyval, block_output, grad_tokens, *small = widen(
        summed, block_output, grad_tokens, sums
    )
    grad_bias_up, grad_bias_down, gain_mlp, shift_mlp, gain_attn, shift_attn = small
    return (
        block_output.reshape(tokens.shape),
        grad_tokens.reshape(tokens.shape),
        query,
        keyval,
        out,
        up,
        grad_bias_up,
        down,
        grad_bias_down,
        gain_attn,
        shift_attn,
        gain_mlp,
        shift_mlp,
    )


def solution(mesh):
    count = mesh.shape["view"]
    groups = mesh.shape["dp"]
    slots = P("dp", "view", None)
    rows = P("dp", "view", None, None, None)
    in_specs = (rows, P("dp", "view"), slots, slots, slots) + (P(),) * 11 + (rows,)
    out_specs = (rows, rows) + (P(),) * 11
    return jax.shard_map(
        functools.partial(on_device, count, groups),
        mesh=mesh,
        in_specs=in_specs,
        out_specs=out_specs,
        check_vma=False,
    )
```

```python
import functools

import jax
import jax.numpy as jnp
from jax import lax
from jax.experimental import pallas as pl
from jax.experimental.pallas import tpu as pltpu
from jax.sharding import PartitionSpec as P

D = 512
HEADS = 8
HEAD_DIM = 64
PAIRS = HEADS // 2
PAIR = 2 * HEAD_DIM
VIEWS = 5
PATCHES = 400
LANG = 77
ROWS = 512
USED = 480
TAIL = USED - PATCHES
SENT = 496
KEYS = VIEWS * PATCHES + TAIL
KEYS_PADDED = 2176
FF = 2048
FF_BLOCK = 512
NEGATIVE = -1e30
EPSILON = 1e-5
GRAD_ROWS = 2 * FF + 4 * D
SUMS = 16
SHARD = 16
STAGES = 8
SKEW = 2
IN_FLIGHT = 4
LQ = 1
READY = (10, 12, 16)
PIECES = ((0, 128), (128, 144), (272, 144))
MAIN = SENT - TAIL

BF16 = jnp.bfloat16
F32 = jnp.float32
MESH = pl.DeviceIdType.MESH
NN = (((1,), (0,)), ((), ()))
NT = (((1,), (1,)), ((), ()))
TN = (((0,), (0,)), ((), ()))
TT = (((0,), (1,)), ((), ()))
MIB = 2**20

VMEM = pltpu.VMEM
IN_VMEM = pl.BlockSpec(memory_space=pltpu.VMEM)
IN_SMEM = pl.BlockSpec(memory_space=pltpu.SMEM)
ANYWHERE = pl.BlockSpec(memory_space=pl.ANY)


def dot(left, right, dims):
    return lax.dot_general(left, right, dims, preferred_element_type=F32)


def normalise(values):
    average = jnp.mean(values, -1, keepdims=True)
    centered = values - average
    variance = jnp.mean(centered * centered, -1, keepdims=True)
    scale = lax.rsqrt(variance + EPSILON)
    return centered * scale, scale


def norm_backward(grad, unit, scale, gain):
    grad = grad * gain
    first = jnp.mean(grad, -1, keepdims=True)
    second = jnp.mean(grad * unit, -1, keepdims=True)
    return scale * (grad - first - unit * second)


def greet(others):
    barrier = pltpu.get_barrier_semaphore()
    for other in others:
        pl.semaphore_signal(barrier, inc=1, device_id=other, device_id_type=MESH)
    pl.semaphore_wait(barrier, len(others))


def main_kernel(
    count,
    groups,
    chunks,
    part_rows,
    counts,
    slot_item,
    slot_view,
    keyframe,
    tokens,
    w_query,
    w_keyval,
    bias_up,
    bias_down,
    gain_attn,
    shift_attn,
    gain_mlp,
    shift_mlp,
    w_up,
    w_down,
    cotangent_in,
    w_output_in,
    block_output,
    grad_tokens,
    summed,
    sums_out,
    normed_all,
    query_norm,
    key_bias,
    keyval,
    query,
    weights,
    mixed,
    mixed_full,
    inverse,
    keyval_grad,
    branch_grad,
    branch,
    mlp_back,
    sent,
    vectors,
    arena,
    grads,
    arrived_core,
    arrived_first,
    arrived_second,
    arrived_last,
    far_in,
    sums_at,
    there_sem,
    here_sem,
    weight_sem,
    send_sem,
    recv_sem,
    local_sem,
    sums_send,
    sums_recv,
    swap_sem,
    far_sem,
):
    me = lax.axis_index("view")
    group = lax.axis_index("dp")
    depth = count // 4
    core = lax.rem(me, 2)
    step = 1 - 2 * core
    place = {"x": lax.rem(me // 2, 2), "y": group, "z": me // 4}
    size = {"x": 2, "y": groups, "z": depth}
    orders = (("x", "y", "z"), ("y", "x", "z"))[-(2 if part_rows < D else 1) :]
    chunk_rows = len(orders) * part_rows
    fine = chunk_rows == D
    arrived = (arrived_first, arrived_second, arrived_last)

    def peer(dim, j):
        at = lax.rem(place[dim] + j, size[dim])
        if dim == "x":
            return {"view": me + 2 * (at - place["x"])}
        if dim == "y":
            return {"dp": at}
        return {"view": me + 4 * (at - place["z"])}

    def along(offset):
        return {"view": lax.rem(me + offset + count, count)}

    sibling = {"view": me + step}

    def window_at(offset, first, rows):
        n = VIEWS - 1 + offset
        columns = pl.ds(pl.multiple_of(lax.rem(n, 4) * D, D), D)
        return weights.at[n // 4, pl.ds(first, rows), columns]

    def weight_copies():
        blocks = FF // D
        return [
            pltpu.make_async_copy(
                w_up.at[:, pl.ds(c * D, D)], arena.at[c], weight_sem.at[c]
            )
            for c in range(blocks)
        ] + [
            pltpu.make_async_copy(
                w_down.at[pl.ds(c * D, D), :], arena.at[blocks + c], weight_sem.at[blocks + c]
            )
            for c in range(blocks)
        ] + [
            pltpu.make_async_copy(cotangent_in, cotangent, weight_sem.at[2 * blocks]),
            pltpu.make_async_copy(w_output_in, w_output, weight_sem.at[2 * blocks + 1]),
        ]

    cotangent = keyval_grad.at[pl.ds(0, ROWS), pl.ds(0, D)]
    w_output = keyval_grad.at[pl.ds(0, D), pl.ds(D, D)]
    for copy in weight_copies():
        copy.start()
    my_view = slot_view[0]
    is_filled = jnp.logical_and(
        jnp.logical_and(counts[0] > 0, keyframe[0] == 1), slot_item[0] >= 0
    )
    my_filled = is_filled.astype(jnp.int32)
    label_here = jnp.where(is_filled, slot_item[0], -1).astype(F32)
    sent[: SENT - USED, :] = jnp.full((SENT - USED, D), label_here, F32).astype(BF16)
    sent[SENT - USED :, :] = tokens[:USED, :]
    peers = [peer(dim, j) for dim in "xyz" for j in range(1, size[dim])]
    greet([sibling] + peers)

    turn = 1 - 2 * place["x"]

    def hop(kind, source, offset, first, rows, device):
        return pltpu.make_async_remote_copy(
            source,
            window_at(offset, first, rows),
            there_sem.at[kind],
            here_sem.at[kind],
            device,
            MESH,
        )

    pieces_all = PIECES + ((MAIN, TAIL),)
    tail = len(PIECES)

    def piece_kind(line, q):
        return line * len(pieces_all) + q

    def along_z(line, q):
        first, rows = pieces_all[q]
        ahead = 4 - 8 * line
        source = sent.at[pl.ds(first, rows), :]
        return hop(piece_kind(line, q), source, -ahead, first, rows, along(ahead))

    def relay_x(q):
        first, rows = pieces_all[q]
        source = window_at(4 * turn, first, rows)
        return hop(piece_kind(2, q), source, 2 * turn, first, rows, along(2 * turn))

    def across_relayed(q):
        first, rows = pieces_all[q]
        source = window_at(-2 * turn, first, rows)
        return hop(piece_kind(3, q), source, -2 * turn - step, first, rows, sibling)

    def direct_x(lang):
        first, rows = (MAIN, TAIL) if lang else (0, MAIN)
        source = sent.at[pl.ds(first, rows), :]
        return hop(piece_kind(4, lang), source, -2 * turn, first, rows, along(2 * turn))

    def across_x(lang):
        first, rows = (MAIN, TAIL) if lang else (0, MAIN)
        source = window_at(2 * turn, first, rows)
        return hop(piece_kind(4, 2 + lang), source, 2 * turn - step, first, rows, sibling)

    def across_z(lang):
        first, rows = (MAIN, TAIL) if lang else (0, MAIN)
        source = window_at(4 * step, first, rows)
        return hop(piece_kind(5, lang), source, 3 * step, first, rows, sibling)

    across_own = hop(piece_kind(5, 2), sent, -step, 0, SENT, sibling)
    forth = turn > 0
    back_turn = turn < 0
    for q in range(tail):
        for line in range(2):
            along_z(line, q).start()
    along_z(0, tail).start()
    direct_x(0).start()
    pl.when(forth)(lambda: direct_x(1).start())
    across_own.start()

    levels = []
    for order in orders:
        rows = part_rows
        offset = 0
        level = [(0, rows)]
        for dim in order:
            rows = rows // size[dim]
            offset = offset + place[dim] * rows
            level.append((offset, rows))
        levels.append(level)
    own_columns = pl.ds(pl.multiple_of(core * (D // 2), D // 2), D // 2)
    other_columns = pl.ds(pl.multiple_of((1 - core) * (D // 2), D // 2), D // 2)

    def slot_of(stage, p, j):
        slot = j - 1
        for order in orders[:p]:
            slot += size[order[stage - 1]] - 1
        return slot

    def rows_of(k, p, offset, rows):
        return pl.ds(pl.multiple_of(k * chunk_rows + p * part_rows + offset, SHARD), rows)

    def held(k):
        return lax.rem(k, IN_FLIGHT)

    first_sem = [0]
    for stage in range(STAGES):
        first_sem.append(first_sem[-1] + stage_copies(stage, size, orders))

    def copies(stage, k):
        out = []

        def add(source, target, device):
            n = first_sem[stage] + len(out)
            out.append(
                pltpu.make_async_remote_copy(
                    source, target, send_sem.at[held(k), n], recv_sem.at[held(k), n], device, MESH
                )
            )

        if stage == 0:
            add(grads.at[rows_of(k, 0, 0, chunk_rows), other_columns], arrived_core.at[held(k)], sibling)
        elif stage == 7:
            whole = summed.at[rows_of(k, 0, 0, chunk_rows), own_columns]
            add(whole, whole, sibling)
        for p, order in enumerate(orders):
            if 0 < stage < 4:
                dim = order[stage - 1]
                offset, _ = levels[p][stage - 1]
                _, rows = levels[p][stage]
                for j in range(1, size[dim]):
                    at = offset + lax.rem(place[dim] + j, size[dim]) * rows
                    add(
                        grads.at[rows_of(k, p, at, rows), own_columns],
                        arrived[stage - 1].at[held(k), slot_of(stage, p, j), pl.ds(0, rows), :],
                        peer(dim, j),
                    )
            elif 4 <= stage < 7:
                dim = order[6 - stage]
                offset, rows = levels[p][7 - stage]
                at = rows_of(k, p, offset, rows)
                source = grads if stage == 4 else summed
                for j in range(1, size[dim]):
                    add(source.at[at, own_columns], summed.at[at, own_columns], peer(dim, j))
        return out

    def own_shard(k, p):
        at = rows_of(k, p, *levels[p][3])
        return pltpu.make_async_copy(
            grads.at[at, own_columns], summed.at[at, own_columns], local_sem.at[held(k), p]
        )

    def start_stage(stage, k):
        for copy in copies(stage, k):
            copy.start()
        if stage == 4:
            for p in range(len(orders)):
                own_shard(k, p).start()

    def finish_stage(stage, k):
        for copy in copies(stage, k):
            copy.wait()
        if stage == 4:
            for p in range(len(orders)):
                own_shard(k, p).wait()
        if stage == 0:
            at = rows_of(k, 0, 0, chunk_rows)
            total = grads[at, own_columns].astype(F32) + arrived_core[held(k)].astype(F32)
            grads[at, own_columns] = total.astype(BF16)
        elif stage < 4:
            for p, order in enumerate(orders):
                offset, rows = levels[p][stage]
                at = rows_of(k, p, offset, rows)
                total = grads[at, own_columns].astype(F32)
                for j in range(1, size[order[stage - 1]]):
                    total += arrived[stage - 1][held(k), slot_of(stage, p, j), :rows, :].astype(F32)
                grads[at, own_columns] = total.astype(BF16)

    blocks = FF // D

    def tick(t):
        for stage in range(STAGES, -1, -1):
            at = t - SKEW * stage
            if fine:
                early = jnp.logical_and(at >= 0, at <= 2 * blocks)
                valid = early
                k = at
                for n, ready in enumerate(READY):
                    now = at == ready
                    valid = jnp.logical_or(valid, now)
                    k = jnp.where(now, 2 * blocks + 1 + n, k)
            else:
                k = at
                valid = jnp.logical_and(at >= 0, at < chunks)

            def go(stage=stage, k=k):
                if stage > 0:
                    finish_stage(stage - 1, k)
                if stage < STAGES:
                    start_stage(stage, k)

            pl.when(valid)(go)

    def run_ticks(first, end):
        def body(t, _):
            tick(t)
            return 0

        lax.fori_loop(first, end, body, 0)

    sums_dims = ("core", "x", "y", "z")

    def sums_copies(level):
        dim = sums_dims[level]
        if dim == "core":
            targets, mine = [sibling], core
        else:
            targets, mine = [peer(dim, j) for j in range(1, size[dim])], place[dim]
        return [
            pltpu.make_async_remote_copy(
                sums_at.at[level, mine],
                sums_at.at[level, mine],
                sums_send.at[level, n],
                sums_recv.at[level, n],
                device,
                MESH,
            )
            for n, device in enumerate(targets)
        ]

    def sums_start(level, value):
        dim = sums_dims[level]
        sums_at[level, core if dim == "core" else place[dim]] = value
        for copy in sums_copies(level):
            copy.start()

    def sums_finish(level):
        for copy in sums_copies(level):
            copy.wait()
        dim = sums_dims[level]
        total = sums_at[level, 0]
        for i in range(1, 2 if dim == "core" else size[dim]):
            total += sums_at[level, i]
        return total

    for c in range(blocks):
        vectors[c : c + 1, :] = bias_up[c * D : (c + 1) * D].astype(F32).reshape(1, D)
    for n, vector in enumerate((bias_down, gain_attn, shift_attn, gain_mlp, shift_mlp)):
        vectors[4 + n : 5 + n, :] = vector[...].astype(F32).reshape(1, D)
    gain_a = vectors[5:6, :]
    shift_a = vectors[6:7, :]
    gain_m = vectors[7:8, :]
    shift_m = vectors[8:9, :]

    def project_keys(first, rows, values):
        unit, _ = normalise(values.astype(F32))
        normed = (unit * gain_a + shift_a).astype(BF16)
        normed_all[first : first + rows, :] = normed
        keyval[first : first + rows, :] = dot(normed, w_keyval[...], NN).astype(BF16)

    own_rows = tokens[:USED, :]
    own_unit, _ = normalise(own_rows.astype(F32))
    query_norm[...] = (own_unit * gain_a + shift_a).astype(BF16)
    query[...] = (dot(query_norm[...], w_query[...], NN).astype(BF16) * HEAD_DIM**-0.5).astype(BF16)
    project_keys(0, PATCHES, own_rows[:PATCHES, :])
    relayed = jnp.where(forth, 1, 0)
    for q in range(tail):
        along_z(relayed, q).wait_recv()
        relay_x(q).start()

    def relay_tail():
        along_z(0, tail).wait_recv()
        relay_x(tail).start()

    pl.when(back_turn)(relay_tail)
    direct_x(0).wait_recv()
    across_x(0).start()

    def pass_tail_x():
        direct_x(1).wait_recv()
        across_x(1).start()

    pl.when(back_turn)(pass_tail_x)
    for q in range(tail):
        along_z(1 - relayed, q).wait_recv()
    pl.when(forth)(lambda: along_z(0, tail).wait_recv())
    across_z(0).start()
    pl.when(step < 0)(lambda: across_z(1).start())
    for q in range(tail):
        relay_x(q).wait_recv()
        across_relayed(q).start()

    def pass_tail_relayed():
        relay_x(tail).wait_recv()
        across_relayed(tail).start()

    pl.when(forth)(pass_tail_relayed)
    for copy in (across_own, across_x(0), across_z(0)):
        copy.wait()
    direct_x(0).wait_send()
    for q in range(tail):
        for line in range(2):
            along_z(line, q).wait_send()
        relay_x(q).wait_send()
        across_relayed(q).wait()
    along_z(0, tail).wait_send()

    def settle_forth():
        direct_x(1).wait_send()
        across_relayed(tail).wait()

    def settle_back():
        relay_x(tail).wait_send()
        across_x(1).wait()

    pl.when(forth)(settle_forth)
    pl.when(back_turn)(settle_back)
    pl.when(step < 0)(lambda: across_z(1).wait_send())
    pl.when(step > 0)(lambda: across_z(1).wait_recv())
    my_label = sent[: SENT - USED, :PAIR].astype(F32)

    def bias_of(label):
        match = jnp.logical_and(label == my_label, label >= 0)
        return jnp.where(match, 0.0, NEGATIVE)[:1, :]

    def block_at(n, first, rows, columns=D):
        return weights[n // 4, first : first + rows, n % 4 * D : n % 4 * D + columns]

    key_bias[:PATCHES, :] = jnp.broadcast_to(bias_of(my_label), (PATCHES, PAIR)).astype(BF16)
    language = own_rows[PATCHES:, :]
    language_bias = bias_of(my_label)
    top_rows = SENT - USED
    for j in range(1, VIEWS):
        ahead = my_view + j < VIEWS
        holds = lax.rem(my_view + j, VIEWS) == 0

        def either(first, rows, columns=D):
            return jnp.where(
                ahead, block_at(4 + j, first, rows, columns), block_at(j - 1, first, rows, columns)
            )

        project_keys(j * PATCHES, PATCHES, either(top_rows, PATCHES))
        bias = bias_of(either(0, top_rows, PAIR).astype(F32))
        rows = slice(j * PATCHES, (j + 1) * PATCHES)
        key_bias[rows, :] = jnp.broadcast_to(bias, (PATCHES, PAIR)).astype(BF16)
        language = jnp.where(holds, block_at(j - 1, top_rows + PATCHES, TAIL), language)
        language_bias = jnp.where(holds, bias, language_bias)
    project_keys(VIEWS * PATCHES, TAIL, language)
    index = lax.broadcasted_iota(jnp.int32, (TAIL, PAIR), 0)
    key_bias[VIEWS * PATCHES : KEYS, :] = jnp.where(
        index < LANG, jnp.broadcast_to(language_bias, (TAIL, PAIR)), NEGATIVE
    ).astype(BF16)
    normed_all[KEYS:, :] = jnp.zeros((KEYS_PADDED - KEYS, D), BF16)
    keyval[KEYS:, :] = jnp.zeros((KEYS_PADDED - KEYS, 2 * D), BF16)
    key_bias[KEYS:, :] = jnp.full((KEYS_PADDED - KEYS, PAIR), NEGATIVE, BF16)

    lane = lax.broadcasted_iota(jnp.int32, (1, PAIR), 1)
    low_half = lane < HEAD_DIM

    def half_of(half, first, second):
        return jnp.where(low_half, first, second) if half == 0 else jnp.where(low_half, second, first)

    def head_keys(p, half):
        pair = keyval[:, pl.ds(pl.multiple_of(p * PAIR, PAIR), PAIR)]
        return half_of(half, pair, key_bias[...])

    def head_values(p, half):
        pair = keyval[:, pl.ds(pl.multiple_of(D + p * PAIR, PAIR), PAIR)]
        return half_of(half, pair, jnp.ones((), BF16))

    def forward_pair(p, _):
        columns = pl.ds(pl.multiple_of(p * PAIR, PAIR), PAIR)
        pair = query[:, columns]
        outs = []
        totals = []

        scores = []
        for half in range(2):
            one = (lane == HEAD_DIM * (1 - half)).astype(BF16)
            scores.append(dot(half_of(half, pair, one), head_keys(p, half), NT))
        for half in range(2):
            top = jnp.max(scores[half], -1, keepdims=True)
            weight = jnp.exp(scores[half] - top).astype(BF16)
            weights[2 * p + half, :USED, :] = weight
            out = dot(weight, head_values(p, half), NN)
            outs.append(out)
            totals.append(pltpu.roll(out, HEAD_DIM, 1))
        inv = 1.0 / jnp.where(low_half, totals[0], totals[1])
        full = jnp.where(low_half, outs[0], outs[1]) * inv
        inverse[:, columns] = inv
        mixed_full[:, columns] = full
        mixed[:, columns] = full.astype(BF16)

        return 0

    lax.fori_loop(0, PAIRS, forward_pair, 0)

    for copy in weight_copies():
        copy.wait()
    row = lax.broadcasted_iota(jnp.int32, (USED, PAIR), 0)
    has_language = (my_view == 0).astype(jnp.int32)
    live_rows = my_filled * (PATCHES + LANG * has_language)
    live = (row < live_rows).astype(F32)[:, :1]
    res = tokens[:USED, :].astype(F32) + live * dot(mixed[...], w_output[...], NN)
    grad_tokens[:USED, :] = res
    unit_m, scale_m = normalise(res)
    normed_mlp = sent.at[:USED, :]
    normed_mlp[...] = (unit_m * gain_m + shift_m).astype(BF16)
    upstream = cotangent[:USED, :].astype(F32)
    branch_grad[...] = (live * upstream).astype(BF16)
    branch[...] = jnp.zeros((USED, D), F32)
    mlp_back[...] = jnp.zeros((USED, D), F32)

    def feed_forward(c, _):
        up = arena[c]
        down = arena[blocks + c]
        before = dot(normed_mlp[...], up, NN) + vectors[pl.ds(c, 1), :]
        chance = 0.5 + 0.5 * lax.erf(before * 0.5**0.5)
        density = jnp.exp(-0.5 * before * before) * 0.3989422804014327
        activated = (before * chance).astype(BF16)
        slope = chance + before * density
        start = pl.multiple_of(2 * c * D, D)
        grads[pl.ds(start, D), :] = dot(activated, branch_grad[...], TN).astype(BF16)
        branch[...] += dot(activated, down, NN)
        if fine:
            tick(2 * c)
        before_full = dot(branch_grad[...], down, NT) * slope
        before_grad = before_full.astype(BF16)
        sums_out[pl.ds(c, 1), :] = jnp.sum(before_grad.astype(F32), 0, keepdims=True)
        grads[pl.ds(start + D, D), :] = dot(normed_mlp[...], before_grad, TN).astype(BF16)
        mlp_back[...] += dot(before_grad, up, NT)
        if fine:
            tick(2 * c + 1)
        return 0

    lax.fori_loop(0, blocks, feed_forward, 0)
    arena[0, :USED, :] = (grad_tokens[:USED, :] + live * (branch[...] + vectors[4:5, :])).astype(BF16)
    arena[0, USED:, :] = tokens[USED:, :]
    output_copy = pltpu.make_async_copy(arena.at[0], block_output, weight_sem.at[0])
    output_copy.start()
    unit_m, scale_m = normalise(grad_tokens[:USED, :])
    back = mlp_back[...]
    sums_out[4:5, :] = jnp.sum(branch_grad[...].astype(F32), 0, keepdims=True)
    sums_out[5:6, :] = jnp.sum(back * unit_m, 0, keepdims=True)
    sums_out[6:7, :] = jnp.sum(back, 0, keepdims=True)
    res_grad = upstream + norm_backward(back, unit_m, scale_m, gain_m)
    grad_tokens[:USED, :] = res_grad
    grad_tokens[USED:, :] = cotangent[USED:, :].astype(F32)
    attended_grad = (live * res_grad).astype(BF16)
    base = 2 * FF
    grads[base : base + D, :] = dot(mixed[...], attended_grad, TN).astype(BF16)
    mixed_grad = branch_grad
    mixed_grad[...] = dot(attended_grad, w_output[...], NT).astype(BF16)

    branch[...] = jnp.zeros((USED, D), F32)
    if fine:
        tick(2 * blocks)

    def backward_pair(p, _):
        columns = pl.ds(pl.multiple_of(p * PAIR, PAIR), PAIR)
        grad = mixed_grad[:, columns].astype(F32)
        scaled = grad * inverse[:, columns]
        product = scaled * mixed_full[:, columns]
        scaled_low = scaled.astype(BF16)
        scaled_t = scaled.T.astype(BF16)
        query_t = query[:, columns].astype(F32).T.astype(BF16)
        start = pl.multiple_of(p * PAIR, PAIR)
        for half in range(2):
            here = low_half if half == 0 else jnp.logical_not(low_half)
            dots = -jnp.sum(jnp.where(here, product, 0.0), -1, keepdims=True)
            dots_high = dots.astype(BF16)
            dots_low = (dots - dots_high.astype(F32)).astype(BF16)
            other = HEAD_DIM * (1 - half)
            rest = jnp.where(
                lane == other, dots_high, jnp.where(lane == other + 1, dots_low, jnp.zeros((), BF16))
            )
            weight = weights[2 * p + half, :USED, :]
            slope = dot(half_of(half, scaled_low, rest), head_values(p, half), NT)
            score_grad = weight * slope.astype(BF16)
            weights[2 * p + half, :USED, :] = score_grad
            rows = slice(half * HEAD_DIM, (half + 1) * HEAD_DIM)
            at = start + half * HEAD_DIM
            keyval_grad[pl.ds(at, HEAD_DIM), :] = dot(query_t[rows, :], score_grad, NN).astype(BF16)
            keyval_grad[pl.ds(D + at, HEAD_DIM), :] = dot(scaled_t[rows, :], weight, NN).astype(BF16)
        at = pl.multiple_of(base + D + 2 * PAIR * p, 2 * PAIR)
        for c in range(2):
            of_pair = keyval_grad[pl.ds(c * D + start, PAIR), :]
            grads[pl.ds(at + c * PAIR, PAIR), :] = dot(of_pair, normed_all[...], NN).astype(BF16)
        if fine:
            tick(2 * blocks + 1 + p)
        return 0

    lax.fori_loop(0, PAIRS, backward_pair, 0)

    def query_pair(p, _):
        columns = pl.ds(pl.multiple_of(p * PAIR, PAIR), PAIR)
        query_parts = [
            dot(weights[2 * p + half, :USED, :], head_keys(p, half), NN) for half in range(2)
        ]
        part = jnp.where(low_half, query_parts[0], query_parts[1]) * HEAD_DIM**-0.5
        query_grad = part.astype(BF16)
        at = pl.multiple_of(base + 3 * D + p * PAIR, PAIR)
        grads[pl.ds(at, PAIR), :] = dot(query_grad, query_norm[...], TN).astype(BF16)
        branch[...] += dot(query_grad, w_query[:, columns], NT)
        if fine:
            run_ticks(ticks + LQ * p, ticks + LQ * (p + 1))
        return 0

    shift_sum = jnp.zeros((1, D), F32)
    gain_sum = jnp.zeros((1, D), F32)

    def parts_at(j):
        return normed_all.at[(j - 1) * USED : j * USED, :]

    for j in range(VIEWS + 1):
        rows = slice(j * PATCHES, min((j + 1) * PATCHES, KEYS))
        piece = dot(keyval_grad[:, rows], w_keyval[...], TT)
        normed = normed_all[rows, :].astype(F32)
        shift_sum += jnp.sum(piece, 0, keepdims=True)
        gain_sum += jnp.sum(piece * normed, 0, keepdims=True)
        if j == 0:
            mlp_back[:PATCHES, :] = piece
        elif j < VIEWS:
            parts_at(j)[:PATCHES, :] = piece.astype(BF16)
        else:
            mlp_back[PATCHES:, :] = jnp.where(my_view == 0, piece, 0.0)
            for i in range(1, VIEWS):
                holds = lax.rem(my_view + i, VIEWS) == 0
                parts_at(i)[PATCHES:, :] = jnp.where(holds, piece, 0.0).astype(BF16)
    def part_for(offset):
        slot = lax.rem(offset + VIEWS, VIEWS) - 1
        at = my_view + offset
        valid = jnp.logical_and(at >= 0, at < VIEWS)
        value = jnp.zeros((USED, D), BF16)
        for n in range(VIEWS - 1):
            value = jnp.where(jnp.logical_and(valid, slot == n), parts_at(n + 1)[...], value)
        return value

    def swap(n):
        return pltpu.make_async_remote_copy(
            arena.at[n, pl.ds(0, USED), :],
            arena.at[4 + n, pl.ds(0, USED), :],
            swap_sem.at[0, n],
            swap_sem.at[1, n],
            sibling,
            MESH,
        )

    back_pieces = ((0, 144), (144, 128), (272, 128), (PATCHES, TAIL))

    def back(kind, slot, target, offset, q):
        first, rows = back_pieces[q]
        n = kind * len(back_pieces) + q
        return pltpu.make_async_remote_copy(
            arena.at[slot, pl.ds(first, rows), :],
            far_in.at[target, pl.ds(first, rows), :],
            far_sem.at[0, n],
            far_sem.at[1, n],
            along(offset),
            MESH,
        )

    def back_relay(q):
        return back(0, 1, 0, 2 * turn, q)

    def back_x(q):
        return back(1, 2, 1, 2 * turn, q)

    def back_up(q):
        return back(2, 3, 2, 4 * turn, q)

    def back_down(q):
        return back(3, 0, 3, -4 * turn, q)

    ticks = 2 * blocks + 1 + PAIRS if fine else 0
    last = READY[-1] + STAGES * SKEW + 1 if fine else chunks + STAGES * SKEW

    if not fine:
        lax.fori_loop(0, PAIRS, query_pair, 0)
        run_ticks(0, SKEW + 1)
        ticks = SKEW + 1
    output_copy.wait()
    offsets = (step, step - 2 * turn, step + 2 * turn, -3 * step)
    for n, offset in ((1, offsets[1]), (3, offsets[3]), (2, offsets[2]), (0, offsets[0])):
        arena[n, :USED, :] = part_for(offset)
        swap(n).start()
    pieces = range(len(back_pieces) - 1)
    lang = len(back_pieces) - 1
    pieces = range(len(back_pieces) - 1)
    lang = len(back_pieces) - 1
    if fine:
        lax.fori_loop(0, 4, query_pair, 0)
        ticks = ticks + LQ * PAIRS
    from_query = branch[...]
    shift_sum += jnp.sum(from_query, 0, keepdims=True)
    gain_sum += jnp.sum(from_query * query_norm[...].astype(F32), 0, keepdims=True)
    sums_out[7:8, :] = (gain_sum - shift_a * shift_sum) / gain_a
    sums_out[8:9, :] = shift_sum
    sums_out[9:, :] = jnp.zeros((SUMS - 9, D), F32)
    sums_start(0, sums_out[...])
    run_ticks(ticks + 0, ticks + 4)
    sums_start(1, sums_finish(0))
    run_ticks(ticks + 4, ticks + 8)
    swap(1).wait()
    both = part_for(-2 * turn).astype(F32) + arena[5, :USED, :].astype(F32)
    arena[1, :USED, :] = both.astype(BF16)
    for q in pieces:
        back_relay(q).start()
    pl.when(forth)(lambda: back_relay(lang).start())
    swap(0).wait()
    swap(3).wait()
    shared = arena[7, :USED, :].astype(F32)
    arena[0, :USED, :] = (
        part_for(-4 * turn).astype(F32) + jnp.where(step == turn, 0.0, shared)
    ).astype(BF16)
    for q in pieces:
        back_down(q).start()
    pl.when(forth)(lambda: back_down(lang).start())
    arena[3, :USED, :] = (
        part_for(4 * turn).astype(F32) + jnp.where(step == turn, shared, 0.0)
    ).astype(BF16)
    run_ticks(ticks + 8, ticks + 10)
    sums_start(2, sums_finish(1))
    at = slice(0, 144)
    back_relay(0).wait_recv()
    both = arena[3, at, :].astype(F32) + far_in[0, at, :].astype(F32)
    arena[3, at, :] = both.astype(BF16)
    back_up(0).start()
    run_ticks(ticks + 10, ticks + 11)
    at = slice(144, 272)
    back_relay(1).wait_recv()
    both = arena[3, at, :].astype(F32) + far_in[0, at, :].astype(F32)
    arena[3, at, :] = both.astype(BF16)
    back_up(1).start()
    run_ticks(ticks + 11, ticks + 12)
    at = slice(272, 400)
    back_relay(2).wait_recv()
    both = arena[3, at, :].astype(F32) + far_in[0, at, :].astype(F32)
    arena[3, at, :] = both.astype(BF16)
    back_up(2).start()

    def up_lang():
        at = slice(PATCHES, USED)
        back_relay(lang).wait_recv()
        both = arena[3, at, :].astype(F32) + far_in[0, at, :].astype(F32)
        arena[3, at, :] = both.astype(BF16)
        back_up(lang).start()

    pl.when(back_turn)(up_lang)
    sums_start(3, sums_finish(2))
    swap(2).wait()
    both = part_for(2 * turn).astype(F32) + arena[6, :USED, :].astype(F32)
    arena[2, :USED, :] = both.astype(BF16)
    for q in pieces:
        back_x(q).start()
    pl.when(back_turn)(lambda: back_x(lang).start())
    run_ticks(ticks + 12, last)
    sums_out[...] = sums_finish(3)
    for q in pieces:
        back_relay(q).wait_send()
        for copy in (back_x(q), back_up(q), back_down(q)):
            copy.wait()

    def settle_lang_forth():
        back_relay(lang).wait_send()
        back_down(lang).wait()
        back_x(lang).wait_recv()

    def settle_lang_back():
        back_x(lang).wait_send()
        back_up(lang).wait()

    pl.when(forth)(settle_lang_forth)
    pl.when(back_turn)(settle_lang_back)
    for at, whole in ((slice(0, PATCHES), True), (slice(PATCHES, USED), False)):
        total = branch[at, :] + mlp_back[at, :] + arena[4, at, :].astype(F32)
        for n, came in ((1, forth), (2, back_turn), (3, forth)):
            part = far_in[n, at, :].astype(F32)
            total += part if whole else jnp.where(came, part, 0.0)
        unit, scale = normalise(tokens[at, :].astype(F32))
        grad_tokens[at, :] += norm_backward(total, unit, scale, gain_a)


def stage_copies(stage, size, orders):
    if stage in (0, 7):
        return 1
    return sum(size[order[stage - 1 if stage < 4 else 6 - stage]] - 1 for order in orders)


def main(count, groups, *args):
    depth = count // 4
    part_rows = 2 * groups * depth * SHARD
    parts = 2 if part_rows < D else 1
    chunk_rows = parts * part_rows
    chunks = -(-GRAD_ROWS // chunk_rows)
    shape = jax.ShapeDtypeStruct
    dma = pltpu.SemaphoreType.DMA
    wide = max(groups, depth)
    half = D // 2
    orders = ((2, groups, depth), (groups, 2, depth))[-parts:]
    slots = [sum(order[stage] - 1 for order in orders) for stage in range(3)]
    sems = 2 + 2 * sum(slots)
    held = min(chunks, IN_FLIGHT)
    left = [part_rows // order[0] for order in orders]
    first = max(left)
    second = max(rows // order[1] for rows, order in zip(left, orders))
    scratch = [
        VMEM((KEYS_PADDED, D), BF16),
        VMEM((USED, D), BF16),
        VMEM((KEYS_PADDED, PAIR), BF16),
        VMEM((KEYS_PADDED, 2 * D), BF16),
        VMEM((USED, D), BF16),
        VMEM((HEADS, SENT, KEYS_PADDED), BF16),
        VMEM((USED, D), BF16),
        VMEM((USED, D), F32),
        VMEM((USED, D), F32),
        VMEM((2 * D, KEYS_PADDED), BF16),
        VMEM((USED, D), BF16),
        VMEM((USED, D), F32),
        VMEM((USED, D), F32),
        VMEM((SENT, D), BF16),
        VMEM((SUMS, D), F32),
        VMEM((2 * FF // D, D, D), BF16),
        VMEM((chunks * chunk_rows, D), BF16),
        VMEM((held, chunk_rows, half), BF16),
        VMEM((held, slots[0], first, half), BF16),
        VMEM((held, slots[1], second, half), BF16),
        VMEM((held, slots[2], SHARD, half), BF16),
        VMEM((4, USED, D), BF16),
        VMEM((4, wide, SUMS, D), F32),
        dma((6 * (len(PIECES) + 1),)),
        dma((6 * (len(PIECES) + 1),)),
        dma((2 * FF // D + 2,)),
        dma((held, sems)),
        dma((held, sems)),
        dma((held, 2)),
        dma((4, wide)),
        dma((4, wide)),
        dma((2, 4)),
        dma((2, 16)),
    ]
    return pl.pallas_call(
        functools.partial(main_kernel, count, groups, chunks, part_rows),
        out_shape=(
            shape((ROWS, D), BF16),
            shape((ROWS, D), F32),
            shape((chunks * chunk_rows, D), BF16),
            shape((SUMS, D), F32),
        ),
        in_specs=[IN_SMEM] * 4 + [IN_VMEM] * 9 + [ANYWHERE] * 4,
        out_specs=[ANYWHERE, IN_VMEM, ANYWHERE, IN_VMEM],
        scratch_shapes=scratch,
        compiler_params=pltpu.CompilerParams(
            collective_id=1, has_side_effects=True, vmem_limit_bytes=63 * MIB + (0 if parts == 2 else 800 * 1024)
        ),
        name="main",
    )(*args)


def widen_kernel(
    summed,
    rows_in,
    grad_in,
    sums,
    down,
    up,
    out,
    query,
    keyval,
    rows_out,
    grad_out,
    grad_bias_up,
    grad_bias_down,
    grad_gain_mlp,
    grad_shift_mlp,
    grad_gain_attn,
    grad_shift_attn,
    narrow,
    wide,
    rows_held,
    grad_held,
    in_sem,
    out_sem,
    pass_sem,
):
    blocks = FF // D
    passes_in = [
        pltpu.make_async_copy(rows_in, rows_held, pass_sem.at[0]),
        pltpu.make_async_copy(grad_in, grad_held, pass_sem.at[1]),
    ]
    passes_out = [
        pltpu.make_async_copy(rows_held, rows_out, pass_sem.at[2]),
        pltpu.make_async_copy(grad_held, grad_out, pass_sem.at[3]),
    ]
    count = 2 * blocks + 4
    loads = [
        pltpu.make_async_copy(summed.at[pl.ds(b * D, D), :], narrow.at[b], in_sem.at[b])
        for b in range(count)
    ]
    order = [count - 1, count - 2, count - 3] + list(range(count - 3))
    for b in order:
        loads[b].start()
    for copy in passes_in:
        copy.start()
    for c in range(blocks):
        grad_bias_up[c * D : (c + 1) * D] = sums[c : c + 1, :].reshape(D)
    rest = (grad_bias_down, grad_gain_mlp, grad_shift_mlp, grad_gain_attn, grad_shift_attn)
    for n, target in enumerate(rest):
        target[...] = sums[blocks + n : blocks + n + 1, :].reshape(D)
    stores = []

    def store(b, source, target):
        stores.append(pltpu.make_async_copy(source, target, out_sem.at[len(stores)]))
        stores[-1].start()

    for b in order:
        loads[b].wait()
        c = b // 2
        if b < 2 * blocks:
            wide[b] = narrow[b].astype(F32)
            at = pl.ds(c * D, D)
            store(b, wide.at[b], down.at[at, :] if b % 2 == 0 else up.at[:, at])
        elif b == 2 * blocks:
            wide[b] = narrow[b].astype(F32)
            store(b, wide.at[b], out)
        elif b == 2 * blocks + 3:
            wide[b] = narrow[b].astype(F32).T
            store(b, wide.at[b], query)
        else:
            pairs = 2 * (b - 2 * blocks - 1)
            for n in range(2):
                for c in range(2):
                    first = (2 * n + c) * PAIR
                    at = pl.ds(first, PAIR)
                    wide[b, :, first : first + PAIR] = (
                        narrow[b, first : first + PAIR, :].astype(F32).T
                    )
                    column = c * D + (pairs + n) * PAIR
                    store(b, wide.at[b, :, at], keyval.at[:, pl.ds(column, PAIR)])
    for copy in passes_in:
        copy.wait()
    for copy in passes_out:
        copy.start()
    for copy in stores + passes_out:
        copy.wait()


def widen(summed, rows, grad, sums):
    blocks = GRAD_ROWS // D
    shape = jax.ShapeDtypeStruct
    dma = pltpu.SemaphoreType.DMA
    return pl.pallas_call(
        widen_kernel,
        out_shape=(
            shape((FF, D), F32),
            shape((D, FF), F32),
            shape((D, D), F32),
            shape((D, D), F32),
            shape((D, 2 * D), F32),
            shape(rows.shape, rows.dtype),
            shape(grad.shape, grad.dtype),
            shape((FF,), F32),
        )
        + (shape((D,), F32),) * 5,
        in_specs=[ANYWHERE] * 3 + [IN_VMEM],
        out_specs=[ANYWHERE] * 7 + [IN_VMEM] * 6,
        scratch_shapes=[
            VMEM((blocks, D, D), BF16),
            VMEM((blocks, D, D), F32),
            VMEM(rows.shape, rows.dtype),
            VMEM(grad.shape, grad.dtype),
            dma((blocks,)),
            dma((blocks + 6,)),
            dma((4,)),
        ],
        compiler_params=pltpu.CompilerParams(vmem_limit_bytes=60 * MIB),
        name="widen",
    )(summed, rows, grad, sums)


def on_device(
    count,
    groups,
    tokens,
    counts,
    slot_item,
    slot_view,
    keyframe,
    w_query,
    w_keyval,
    w_output,
    w_up,
    bias_up,
    w_down,
    bias_down,
    gain_attn,
    shift_attn,
    gain_mlp,
    shift_mlp,
    cotangent,
):
    block_output, grad_tokens, summed, sums = main(
        count,
        groups,
        counts.reshape(1),
        slot_item.reshape(1),
        slot_view.reshape(1),
        keyframe.reshape(1),
        tokens.reshape(ROWS, D),
        w_query,
        w_keyval,
        bias_up,
        bias_down,
        gain_attn,
        shift_attn,
        gain_mlp,
        shift_mlp,
        w_up,
        w_down,
        cotangent.reshape(ROWS, D),
        w_output,
    )
    down, up, out, query, keyval, block_output, grad_tokens, *small = widen(
        summed, block_output, grad_tokens, sums
    )
    grad_bias_up, grad_bias_down, gain_mlp, shift_mlp, gain_attn, shift_attn = small
    return (
        block_output.reshape(tokens.shape),
        grad_tokens.reshape(tokens.shape),
        query,
        keyval,
        out,
        up,
        grad_bias_up,
        down,
        grad_bias_down,
        gain_attn,
        shift_attn,
        gain_mlp,
        shift_mlp,
    )


def solution(mesh):
    count = mesh.shape["view"]
    groups = mesh.shape["dp"]
    slots = P("dp", "view", None)
    rows = P("dp", "view", None, None, None)
    in_specs = (rows, P("dp", "view"), slots, slots, slots) + (P(),) * 11 + (rows,)
    out_specs = (rows, rows) + (P(),) * 11
    return jax.shard_map(
        functools.partial(on_device, count, groups),
        mesh=mesh,
        in_specs=in_specs,
        out_specs=out_specs,
        check_vma=False,
    )
```
